32 devices in a mesh: elem: 16 (over z, y, x), face: 2 (over core).
Axes of the slice: x: 2, y: 2, z: 4, core: 2. Of those that a mesh axis runs over, the one named last changes fastest.
Arguments:
- forcing: float32 [8192, 512], P(('elem', 'face')), may hold values from -15 to 15, as said below
- kappa: float32 [8192], P(('elem', 'face')), may hold values from 0.3 to 3
- elem_order: int32 [32, 256], P(('elem', 'face')), may hold values from 0 to 255, each once within a row
Outputs:
- solution: float32 [8192, 512], P(('elem', 'face'))
- residual: float32 [8192, 512], P(('elem', 'face'))
The draws below stay inside these ranges and needn't reach their ends.
Inputs may be any that keep to these rules, and one draw needn't show every extreme that they name: `forcing`: element loads of order one, with a scale that varies by element and along z. `elem_order`: each row is a permutation of the 256 grid positions of the device's block.
All inputs are finite; a program needn't handle non-finite values.
Results may differ from the reference program's by a relative error of at most 0.0004.
Values sent between devices are 32-bit elements; how exact they have to be, the bound alone decides.
No kernel may reach another device: no remote copies, remote signals or barrier semaphores. Data moves between devices by JAX's collectives and lax.ppermute only.
A program may use at most 192 MiB of HBM per device.

```python
import math
import jax
import jax.numpy as jnp
import numpy as np
from jax import lax

EX = 8
EY = 32
SWEEPS = 4
ITERS = 2
E_DEV = 256
GZ = 32
ELEMENTS = 8192
N_ELEM = 16
N_FACE = 2


def draw_forcing(key, part):
    key = jax.random.fold_in(key, 11)
    base_key, scale_key = jax.random.split(key)
    shape = (ELEMENTS, 512)
    rows = jnp.arange(ELEMENTS, dtype=jnp.int32) // E_DEV
    devices = ELEMENTS // E_DEV
    ramp = 0.6 + 1.2 * rows.astype(jnp.float32) / max(devices - 1, 1)
    rough = jnp.exp(jax.random.uniform(scale_key, (ELEMENTS, 1), jnp.float32, -0.7, 0.7))
    base = jnp.clip(jax.random.normal(base_key, shape, jnp.float32), -4.0, 4.0)
    return (base * ramp[:, None] * rough).astype(jnp.float32)


def levels(key, dims, shards, low, high):
    gain = 1.0
    for dim, shards_of in shards:
        heights = jax.random.uniform(jax.random.fold_in(jax.random.fold_in(key, 6), dim), (shards_of,), jnp.float32, low / len(shards), high / len(shards))
        gain = gain * jnp.repeat(jnp.exp(heights), dims[dim] // shards_of).reshape((-1,) + (1,) * (len(dims) - 1 - dim))
    return gain


def setup_inputs(seed: int = 0) -> dict:
    seeds = jax.random.split(jax.random.key(seed), 4)
    return {
        "forcing": draw_forcing(jax.random.fold_in(seeds[3], 71), 0),
        "kappa": jnp.clip(jnp.exp(math.log(3.0) - 2.3025851 * jax.random.uniform(seeds[1], (ELEMENTS,), jnp.float32) ** levels(seeds[1], (ELEMENTS,), ((0, 32),), -0.2, 0.2)), 0.3, 3.0),
        "elem_order": jax.vmap(lambda own: jax.random.permutation(own, E_DEV))(jax.random.split(seeds[2], (N_ELEM * N_FACE))).reshape((N_ELEM * N_FACE, E_DEV)).astype(jnp.int32),
    }


REACT = 0.02
OMEGA = 0.6


def legendre_seven(points):
    before = np.ones(8)
    current = np.array(points)
    for degree in range(1, 7):
        following = ((2 * degree + 1) * points * current - degree * before) / (degree + 1)
        before = current
        current = following
    return current


def element_tables():
    points = np.array([-1.0, -0.8717401485096066, -0.5917001814331423, -0.2092992179024789, 0.2092992179024789, 0.5917001814331423, 0.8717401485096066, 1.0])
    weights = np.array([1.0 / 28.0, 0.2107042271435061, 0.3411226924835044, 0.4124587946587038, 0.4124587946587038, 0.3411226924835044, 0.2107042271435061, 1.0 / 28.0])
    legendre = legendre_seven(points)
    derivative = np.zeros((8, 8))
    for left_node in range(8):
        for right_node in range(8):
            if left_node != right_node:
                derivative[left_node, right_node] = legendre[left_node] / (legendre[right_node] * (points[left_node] - points[right_node]))
    derivative[0, 0] = -14.0
    derivative[7, 7] = 14.0
    stiffness = derivative.T @ (weights[:, None] * derivative)
    mass = np.eye(8) * weights[None, :]
    full_stiff = np.kron(np.kron(mass, mass), stiffness) + np.kron(np.kron(mass, stiffness), mass) + np.kron(np.kron(stiffness, mass), mass)
    mass_nodes = np.kron(np.kron(weights, weights), weights)
    interp = np.stack([(1.0 - points) / 2.0, (1.0 + points) / 2.0], 1)
    prolong = np.kron(np.kron(interp, interp), interp)
    coarse_stiff = prolong.T @ full_stiff @ prolong
    coarse_mass = prolong.T @ (mass_nodes[:, None] * prolong)
    ends = np.ones(8)
    ends[0] = 2.0
    ends[7] = 2.0
    inverse_mult = 1.0 / np.kron(np.kron(ends, ends), ends)
    return stiffness, weights, full_stiff, mass_nodes, prolong, coarse_stiff, coarse_mass, inverse_mult


def pair_sum(grid, elem_axis, node_axis):
    upper = lax.index_in_dim(grid, 7, node_axis, keepdims=True)
    lower = lax.index_in_dim(grid, 0, node_axis, keepdims=True)
    shared = upper + jnp.roll(lower, -1, elem_axis)
    middle = lax.slice_in_dim(grid, 1, 7, axis=node_axis)
    return jnp.concatenate([jnp.roll(shared, 1, elem_axis), middle, shared], node_axis)


def direct_sum(field):
    grid = field.reshape(GZ, EY, EX, 8, 8, 8)
    grid = pair_sum(grid, 2, 5)
    grid = pair_sum(grid, 1, 4)
    grid = pair_sum(grid, 0, 3)
    return grid.reshape(-1, 512)


def full_corners(vert):
    parts = []
    for corner in range(8):
        along_z, along_y, along_x = corner // 4, corner // 2 % 2, corner % 2
        parts.append(jnp.roll(vert, (-along_z, -along_y, -along_x), (0, 1, 2)))
    return jnp.stack(parts, -1)


def full_assemble(contrib):
    total = jnp.zeros(contrib.shape[:3], jnp.float32)
    for corner in range(8):
        along_z, along_y, along_x = corner // 4, corner // 2 % 2, corner % 2
        total = total + jnp.roll(contrib[..., corner], (along_z, along_y, along_x), (0, 1, 2))
    return total


def reference(forcing, kappa, elem_order):
    tabs = [jnp.asarray(table, jnp.float32) for table in element_tables()]
    stiffness, weights, full_stiff, mass_nodes = tabs[0], tabs[1], tabs[2], tabs[3]
    prolong, coarse_stiff, coarse_mass, inverse_mult = tabs[4], tabs[5], tabs[6], tabs[7]
    highest = lax.Precision.HIGHEST
    devices = elem_order.shape[0]
    per_dev = elem_order.shape[1]
    where = (jnp.arange(devices, dtype=jnp.int32)[:, None] * per_dev + elem_order).reshape(-1).astype(jnp.int32)
    load = jnp.zeros_like(forcing).at[where].set(forcing)
    coeff = jnp.zeros_like(kappa).at[where].set(kappa)

    def apply_op(field):
        cube = field.reshape(-1, 8, 8, 8)
        term_x = jnp.einsum('xa,ecba->ecbx', stiffness, cube, precision=highest) * (weights[:, None, None] * weights[None, :, None])
        term_y = jnp.einsum('yb,ecba->ecya', stiffness, cube, precision=highest) * (weights[:, None, None] * weights[None, None, :])
        term_z = jnp.einsum('zc,ecba->ezba', stiffness, cube, precision=highest) * (weights[None, :, None] * weights[None, None, :])
        local = coeff[:, None] * (term_x + term_y + term_z).reshape(-1, 512) + REACT * mass_nodes[None, :] * field
        return direct_sum(local)

    diag_fine = direct_sum(coeff[:, None] * jnp.diag(full_stiff)[None, :] + REACT * mass_nodes[None, :])
    coeff_grid = coeff.reshape(GZ, EY, EX)
    coarse_diag = full_assemble(coeff_grid[..., None] * jnp.diag(coarse_stiff) + REACT * jnp.diag(coarse_mass))

    def coarse_apply(vert):
        values = full_corners(vert).reshape(-1, 8)
        contrib = coeff[:, None] * jnp.dot(values, coarse_stiff, precision=highest) + REACT * jnp.dot(values, coarse_mass, precision=highest)
        return full_assemble(contrib.reshape(GZ, EY, EX, 8))

    def precondition(resid):
        restricted = jnp.dot(resid * inverse_mult[None, :], prolong, precision=highest).reshape(GZ, EY, EX, 8)
        target = full_assemble(restricted)
        vert = jnp.zeros_like(target)
        for sweep in range(SWEEPS):
            vert = vert + OMEGA * (target - coarse_apply(vert)) / coarse_diag
        values = full_corners(vert).reshape(-1, 8)
        return resid / diag_fine + jnp.dot(values, prolong.T, precision=highest)

    def inner(left, right):
        return jnp.sum(left * right * inverse_mult[None, :])

    resid = direct_sum(load)
    solution = jnp.zeros_like(resid)
    precond = precondition(resid)
    direction = precond
    gamma = inner(resid, precond)
    for step in range(ITERS):
        image = apply_op(direction)
        alpha = gamma / inner(direction, image)
        solution = solution + alpha * direction
        resid = resid - alpha * image
        if step + 1 < ITERS:
            precond = precondition(resid)
            gamma_new = inner(resid, precond)
            direction = precond + (gamma_new / gamma) * direction
            gamma = gamma_new
    return solution[where], resid[where]
```

```python
import functools
import math

import jax
import jax.numpy as jnp
import numpy as np
from jax import lax
from jax.experimental import pallas as pl
from jax.experimental.pallas import tpu as pltpu
from jax.sharding import PartitionSpec as P

EX = 8
EY = 32
PLANE = EX * EY
SWEEPS = 4
REACT = 0.02
OMEGA = 0.6
AXES = ("elem", "face")
F32 = jnp.float32


def legendre_seven(points):
    before = np.ones(8)
    current = np.array(points)
    for degree in range(1, 7):
        following = ((2 * degree + 1) * points * current - degree * before) / (degree + 1)
        before = current
        current = following
    return current


def line_tables():
    points = np.array(
        [
            -1.0,
            -0.8717401485096066,
            -0.5917001814331423,
            -0.2092992179024789,
            0.2092992179024789,
            0.5917001814331423,
            0.8717401485096066,
            1.0,
        ]
    )
    weights = np.array(
        [
            1.0 / 28.0,
            0.2107042271435061,
            0.3411226924835044,
            0.4124587946587038,
            0.4124587946587038,
            0.3411226924835044,
            0.2107042271435061,
            1.0 / 28.0,
        ]
    )
    legendre = legendre_seven(points)
    derivative = np.zeros((8, 8))
    for left_node in range(8):
        for right_node in range(8):
            if left_node != right_node:
                derivative[left_node, right_node] = legendre[left_node] / (
                    legendre[right_node] * (points[left_node] - points[right_node])
                )
    derivative[0, 0] = -14.0
    derivative[7, 7] = 14.0
    stiffness = derivative.T @ (weights[:, None] * derivative)
    return points, weights, stiffness


POINTS, WEIGHTS, STIFF = line_tables()
DIAG = np.diag(STIFF)
ENDS = np.array([2.0] + [1.0] * 6 + [2.0])
MASS = np.diag(WEIGHTS)
STIFF_XY = np.tile(np.kron(MASS, STIFF) + np.kron(STIFF, MASS), (1, 2))
INTERP = np.stack([(1.0 - POINTS) / 2.0, (1.0 + POINTS) / 2.0], 1)
LINE_MASS = INTERP.T @ (WEIGHTS[:, None] * INTERP)
LINE_STIFF = INTERP.T @ STIFF @ INTERP
MASS_SUM = (LINE_MASS[0, 0] + LINE_MASS[0, 1]) / 2.0
MASS_DIF = (LINE_MASS[0, 0] - LINE_MASS[0, 1]) / 2.0
STIFF_DIF = LINE_STIFF[0, 0]
MODE_STIFF = [
    0.0,
    STIFF_DIF * MASS_SUM**2,
    2.0 * STIFF_DIF * MASS_DIF * MASS_SUM,
    3.0 * STIFF_DIF * MASS_DIF**2,
]
MODE_MASS = [MASS_SUM ** (3 - j) * MASS_DIF**j for j in range(4)]
CORNER_STIFF = 3.0 * LINE_STIFF[0, 0] * LINE_MASS[0, 0] ** 2
CORNER_MASS = LINE_MASS[0, 0] ** 3


def lane(shape):
    return lax.broadcasted_iota(jnp.int32, shape, len(shape) - 1)


def next_x(v):
    return jnp.where(lane(v.shape) % EX == EX - 1, pltpu.roll(v, EX - 1, 1), pltpu.roll(v, PLANE - 1, 1))


def prev_x(v):
    return jnp.where(lane(v.shape) % EX == 0, pltpu.roll(v, PLANE - EX + 1, 1), pltpu.roll(v, 1, 1))


def next_y(v):
    return pltpu.roll(v, PLANE - EX, 1)


def prev_y(v):
    return pltpu.roll(v, EX, 1)


def next_z(v):
    half = v.shape[0] // 2
    return jnp.concatenate([v[half:], pltpu.roll(v[:half], half - 1, 0)], axis=0)


def prev_z(v):
    half = v.shape[0] // 2
    return jnp.concatenate([pltpu.roll(v[half:], 1, 0), v[:half]], axis=0)


def plane_row(layer, planes):
    layer = lax.rem(layer + planes, planes)
    return pl.ds(lax.div(layer, 2) + lax.rem(layer, 2) * (planes // 2), 1)


def column(values):
    row = lax.broadcasted_iota(jnp.int32, (8, PLANE), 0)
    out = jnp.full((8, PLANE), float(values[0]), F32)
    for k in range(1, 8):
        out = jnp.where(row == k, float(values[k]), out)
    return out


def rows_of(nz, ny):
    start = (nz * 8 + ny) * 8
    return slice(start, start + 8)


def get(ref, rows):
    return jnp.concatenate([ref[0, rows, :], ref[1, rows, :]], axis=1)


def put(ref, rows, value):
    ref[0, rows, :] = value[:, :128]
    ref[1, rows, :] = value[:, 128:]


def sum_xy(ref):
    planes = ref.shape[1] // 64
    first, last = pl.ds(0, planes * 8, stride=8), pl.ds(7, planes * 8, stride=8)
    shared = get(ref, last) + next_x(get(ref, first))
    put(ref, last, shared)
    put(ref, first, prev_x(shared))
    for nz in range(planes):
        shared = get(ref, rows_of(nz, 7)) + next_y(get(ref, rows_of(nz, 0)))
        put(ref, rows_of(nz, 7), shared)
        put(ref, rows_of(nz, 0), prev_y(shared))


def restrict(ref, points, inv_ends):
    sums_z, difs_z = [], []
    for ny in range(8):
        tiles = [get(ref, rows_of(nz, ny)) for nz in range(8)]
        sums_z.append(functools.reduce(lambda a, b: a + b, tiles))
        difs_z.append(sum(float(POINTS[7 - k]) * (tiles[7 - k] - tiles[k]) for k in range(4)))
    return restrict_xy(sums_z, difs_z, points, inv_ends)


def restrict_xy(sums_z, difs_z, points, inv_ends):
    planes = []
    for parts in (sums_z, difs_z):
        parts = [part * float(1.0 / ENDS[ny]) for ny, part in enumerate(parts)]
        total = functools.reduce(lambda a, b: a + b, parts)
        slope = sum(float(POINTS[7 - k]) * (parts[7 - k] - parts[k]) for k in range(4))
        in_y = []
        for part in (total * inv_ends, slope * inv_ends):
            flat = jnp.sum(part, axis=0, keepdims=True)
            steep = jnp.sum(part * points, axis=0, keepdims=True)
            in_y.append((flat - steep) + prev_x(flat + steep))
        planes.append((in_y[0] - in_y[1]) + prev_y(in_y[0] + in_y[1]))
    return (planes[0] - planes[1]) * 0.125, (planes[0] + planes[1]) * 0.125


def both(v, following):
    after = following(v)
    return after + v, after - v


def both_back(total, dif, preceding):
    return (total - dif) + preceding(total + dif)


def coarse_modes(coeff):
    return [float(REACT * MODE_MASS[0])] + [
        float(MODE_STIFF[j]) * coeff + float(REACT * MODE_MASS[j]) for j in range(1, 4)
    ]


def coarse_tables(coeff):
    near = coeff + prev_x(coeff)
    near = near + prev_y(near)
    near = near + prev_z(near)
    scale = float(OMEGA) / (float(CORNER_STIFF) * near + float(8.0 * REACT * CORNER_MASS))
    return coarse_modes(coeff), scale


def coarse_apply(vert, modes):
    in_x = both(vert, next_x)
    back_x = []
    for jx in range(2):
        in_y = both(in_x[jx], next_y)
        back_y = []
        for jy in range(2):
            in_z = both(in_y[jy], next_z)
            scaled = [modes[jx + jy + jz] * in_z[jz] for jz in range(2)]
            back_y.append(both_back(scaled[0], scaled[1], prev_z))
        back_x.append(both_back(back_y[0], back_y[1], prev_y))
    return both_back(back_x[0], back_x[1], prev_x)


def coarse_solve(target, modes, scale):
    vert = scale * target
    for _ in range(SWEEPS - 1):
        vert = vert + scale * (target - coarse_apply(vert, modes))
    return vert


def gathered(ref, k, size):
    chips = ref.shape[0] // (4 * size)
    parts = []
    for core in range(2):
        rows = [ref[pl.ds((core * size + k) * 2 + h, chips, stride=4 * size), :] for h in range(2)]
        parts.append(jnp.concatenate(rows, axis=1))
    return jnp.concatenate(parts, axis=0)


def halves(row):
    return [row[:, :128], row[:, 128:]]


def send(ref, planes):
    block = jnp.concatenate([half for plane in planes for half in halves(plane)], axis=0)
    rows = block.shape[0]
    times = 8 // math.gcd(rows, 8)
    block = jnp.concatenate([block] * times, axis=0)
    for k in range(0, ref.shape[0], rows * times):
        ref[k : k + rows * times, :] = block


def layer_modes(vert_ref, shift):
    me, devices = my_layer(), vert_ref.shape[0]
    lower, upper = (vert_ref[plane_row(me + shift + k, devices), :] for k in range(2))
    modes = []
    for along_z in (upper + lower, upper - lower):
        for along_y in both(along_z, next_y):
            modes += both(along_y, next_x)
    return 0.125 * jnp.concatenate(modes, axis=0)


class Smooth:
    def __init__(self, modes, coeff, points, weight_x):
        row = lax.broadcasted_iota(jnp.int32, (8, PLANE), 0)
        ends = jnp.where(row == 0, -1.0, jnp.where(row == 7, 1.0, 0.0))
        m = [[[modes[4 * z + 2 * y + x : 4 * z + 2 * y + x + 1] for x in range(2)] for y in range(2)] for z in range(2)]
        self.xy = [[m[z][y][0] + m[z][y][1] * points for y in range(2)] for z in range(2)]
        self.dx = [[m[z][y][1] for y in range(2)] for z in range(2)]
        self.ends_coeff = ends * coeff
        self.weight_coeff = weight_x * coeff
        self.mass = float(REACT) * weight_x

    def value(self, nz, ny):
        by_y = [self.xy[z][0] + float(POINTS[ny]) * self.xy[z][1] for z in range(2)]
        return by_y[0] + float(POINTS[nz]) * by_y[1]

    def operated(self, nz, ny, value):
        wy, wz, py, pz = (float(t) for t in (WEIGHTS[ny], WEIGHTS[nz], POINTS[ny], POINTS[nz]))
        slope = (self.dx[0][0] + py * self.dx[0][1]) + pz * (self.dx[1][0] + py * self.dx[1][1])
        out = self.ends_coeff * (slope * (wy * wz)) + (self.mass * (wy * wz)) * value
        flux = None
        if ny in (0, 7):
            flux = (self.xy[0][1] + pz * self.xy[1][1]) * (wz * py)
        if nz in (0, 7):
            along = (self.xy[1][0] + py * self.xy[1][1]) * (wy * pz)
            flux = along if flux is None else flux + along
        return out if flux is None else out + self.weight_coeff * flux


def kappa_sums(own, below, above):
    row = lax.broadcasted_iota(jnp.int32, (8, PLANE), 0)
    table = []
    for along_z in (own + below, own, own + above):
        in_z = []
        for along_y in (along_z + prev_y(along_z), along_z, along_z + next_y(along_z)):
            first = along_y + prev_x(along_y)
            last = along_y + next_x(along_y)
            in_z.append(jnp.where(row == 0, first, jnp.where(row == 7, last, along_y)))
        table.append(in_z)
    return table


def kind(node):
    return 0 if node == 0 else (2 if node == 7 else 1)


def operate(z_ref, xy_ref, out_ref, table_ref, coeff, weight_x):
    table = jnp.tile(table_ref[...], (4, 2))
    row, col = (lax.broadcasted_iota(jnp.int32, table.shape, axis) for axis in range(2))
    table = jnp.where(row // 64 == col // 64, table, 0.0)
    for half in range(2):
        rows = slice(half * 256, half * 256 + 256)
        xy_ref[rows, :] = jnp.dot(
            table, get(z_ref, rows), precision=lax.Precision.HIGHEST, preferred_element_type=F32
        )
    for ny in range(8):
        tiles = [get(z_ref, rows_of(nz, ny)) for nz in range(8)]
        even = [tiles[k] + tiles[7 - k] for k in range(4)]
        odd = [tiles[k] - tiles[7 - k] for k in range(4)]
        for nz in range(4):
            even_part = sum(float((STIFF[nz, k] + STIFF[nz, 7 - k]) / 2) * even[k] for k in range(4))
            odd_part = sum(float((STIFF[nz, k] - STIFF[nz, 7 - k]) / 2) * odd[k] for k in range(4))
            for node, term in ((nz, even_part + odd_part), (7 - nz, even_part - odd_part)):
                area = weight_x * float(WEIGHTS[ny])
                local = coeff * (
                    float(WEIGHTS[node]) * xy_ref[rows_of(node, ny), :] + area * term
                ) + (float(REACT * WEIGHTS[node]) * area) * tiles[node]
                put(out_ref, rows_of(node, ny), local)


def fine_diag(sums, nz, ny, weight_x, diag_x, ends_x):
    wy, wz, ky, kz = (float(t) for t in (WEIGHTS[ny], WEIGHTS[nz], DIAG[ny], DIAG[nz]))
    stiff = diag_x * (wy * wz) + weight_x * (ky * wz + wy * kz)
    mass = (weight_x * ends_x) * float(REACT * wy * wz * ENDS[ny] * ENDS[nz])
    return sums[kind(nz)][kind(ny)] * stiff + mass


def my_layer():
    return lax.axis_index("elem") * lax.axis_size("face") + lax.axis_index("face")


def face_rows(ref):
    even = lax.rem(my_layer(), 2) == 0
    last = ref.shape[1] - 64
    near = pl.multiple_of(jnp.where(even, last, 0), 64)
    far = pl.multiple_of(jnp.where(even, 0, last), 64)
    return pl.ds(near, 64), pl.ds(far, 64)


def faces_out(ref, near_ref, far_ref):
    near, far = face_rows(ref)
    near_ref[:, 0:64, :] = ref[:, near, :]
    far_ref[:, 0:64, :] = ref[:, far, :]


def faces_in(ref, near_ref, far_ref):
    near, far = face_rows(ref)
    ref[:, near, :] += near_ref[:, 0:64, :]
    ref[:, far, :] += far_ref[:, 0:64, :]


def columns_of_nodes():
    return column(POINTS), column(WEIGHTS), column(DIAG), column(ENDS)


def pieces(v):
    high = v.astype(jnp.bfloat16)
    rest = v - high.astype(F32)
    middle = rest.astype(jnp.bfloat16)
    low = (rest - middle.astype(F32)).astype(jnp.bfloat16)
    return low, middle, high


def selection(order):
    place = lax.broadcasted_iota(jnp.int32, (PLANE, PLANE), 0).astype(order.dtype)
    return jnp.where(place == order, 1.0, 0.0).astype(jnp.bfloat16)


def opening(
    forcing_ref, kappa_ref, order_ref, load_ref, far_ref, near_ref, own_ref, held, held_kappa, held_order, sems
):
    small = [
        pltpu.make_async_copy(order_ref, held_order, sems.at[0]),
        pltpu.make_async_copy(kappa_ref, held_kappa, sems.at[1]),
    ]
    parts = [
        pltpu.make_async_copy(forcing_ref.at[:, pl.ds(256 * k, 256)], held.at[k], sems.at[2 + k]) for k in range(2)
    ]
    for copy in small + parts:
        copy.start()
    for copy in small:
        copy.wait()
    order = held_order[...]
    choose = selection(order)
    coeff = jnp.zeros((8, PLANE), F32)
    for piece in pieces(jnp.broadcast_to(held_kappa[...], (8, PLANE))):
        coeff = coeff + lax.dot_general(piece, choose, (((1,), (1,)), ((), ())), preferred_element_type=F32)
    own = jnp.concatenate([coeff[0:3], order.astype(F32), coeff[4:8]], axis=0)
    own_ref[...] = own
    for k, copy in enumerate(parts):
        copy.wait()
        load = jnp.zeros((PLANE, 256), F32)
        for piece in pieces(held[k]):
            load = load + jnp.dot(choose, piece, preferred_element_type=F32)
        put(load_ref, slice(256 * k, 256 * k + 256), load.T)
    sum_xy(load_ref)
    faces_out(load_ref, near_ref, far_ref)
    put(near_ref, slice(64, 72), own)
    put(far_ref, slice(64, 72), own)


def opening_payload(load_ref, own_ref, payload_ref):
    lower, upper = restrict(load_ref, column(POINTS), column(1.0 / ENDS))
    send(payload_ref, [lower, upper, own_ref[0:1, :]])


def below_above(near, far):
    even = lax.rem(my_layer(), 2) == 0
    return jnp.where(even, far, near), jnp.where(even, near, far)


def row_after_face(ref):
    return get(ref, slice(64, 72))[0:1]


def first_faces(
    load_ref, far_in_ref, near_in_ref, own_ref, table_ref,
    resid_ref, scaled_ref, image_ref, layers_ref, lower_ref, far_ref, near_ref, xy_ref,
):
    points, weight_x, _, _ = columns_of_nodes()
    own = own_ref[0:1, :]
    below, above = below_above(row_after_face(near_in_ref), row_after_face(far_in_ref))
    layers_ref[...] = jnp.concatenate([own, below, above, own_ref[3:8, :]], axis=0)
    resid_ref[...] = load_ref[...]
    faces_in(resid_ref, near_in_ref, far_in_ref)
    over_diag(functools.partial(get, resid_ref), scaled_ref, layers_ref)
    operate(scaled_ref, xy_ref, image_ref, table_ref, own, weight_x)
    sum_xy(image_ref)
    faces_out(image_ref, near_ref, far_ref)
    lower, upper = restrict(image_ref, points, column(1.0 / ENDS))
    lower_ref[...] = jnp.broadcast_to(lower, lower_ref.shape)
    put(near_ref, slice(64, 72), jnp.broadcast_to(upper, (8, PLANE)))
    put(far_ref, slice(64, 72), jnp.broadcast_to(upper, (8, PLANE)))


def over_diag(resid, scaled_ref, layers_ref):
    _, weight_x, diag_x, ends_x = columns_of_nodes()
    sums = kappa_sums(*(layers_ref[k : k + 1, :] for k in range(3)))
    for nz in range(8):
        for ny in range(8):
            rows = rows_of(nz, ny)
            put(scaled_ref, rows, resid(rows) / fine_diag(sums, nz, ny, weight_x, diag_x, ends_x))


def three_modes(vert_ref):
    return jnp.concatenate([layer_modes(vert_ref, shift) for shift in (0, -1, 1)], axis=0)


def smooths_of(modes, layers_ref):
    points, weight_x, _, _ = columns_of_nodes()
    return [Smooth(modes[8 * k : 8 * k + 8], layers_ref[k : k + 1, :], points, weight_x) for k in range(3)]


def smooth_image(smooths, out_ref, edge_ref):
    own, below, above = smooths
    for nz in range(8):
        for ny in range(8):
            put(out_ref, rows_of(nz, ny), own.operated(nz, ny, own.value(nz, ny)))
    sum_xy(out_ref)
    for plane, (smooth, nz) in enumerate(((below, 7), (above, 0))):
        for ny in range(8):
            put(edge_ref, rows_of(plane, ny), smooth.operated(nz, ny, smooth.value(nz, ny)))
    sum_xy(edge_ref)
    out_ref[:, 0:64, :] += edge_ref[:, 0:64, :]
    out_ref[:, 448:512, :] += edge_ref[:, 64:128, :]


def first_coarse(
    coarse_ref, layers_ref, vert_ref, applied_ref, target_ref, scale_ref, coeff_ref, choose_ref, smooth_ref, edge_ref
):
    coeff = gathered(coarse_ref, 2, 3)
    coeff_ref[...] = coeff
    choose_ref[...] = selection(layers_ref[3:4, :]).astype(F32).T.astype(jnp.bfloat16)
    modes, scale = coarse_tables(coeff)
    target = gathered(coarse_ref, 0, 3) + prev_z(gathered(coarse_ref, 1, 3))
    vert = coarse_solve(target, modes, scale)
    vert_ref[...] = vert
    applied_ref[...] = coarse_apply(vert, modes)
    target_ref[...] = target
    scale_ref[...] = scale
    smooth_image(smooths_of(three_modes(vert_ref), layers_ref), smooth_ref, edge_ref)


def pack(sums):
    rows = [jnp.sum(t, axis=0, keepdims=True) for t in sums]
    rows = jnp.concatenate(rows + [jnp.zeros((1, PLANE), F32)] * (8 - len(rows)), axis=0)
    for by in (128, 64, 32):
        rows = rows + pltpu.roll(rows, by, 1)
    place = lax.broadcasted_iota(jnp.int32, rows.shape, 0)
    return jnp.sum(jnp.where(lane(rows.shape) // 32 == place, rows, 0.0), axis=0, keepdims=True)


def second_rough(
    first_ref, smooth_ref, near_in_ref, layers_ref, table_ref, resid_ref, scaled_ref,
    image_ref, whole_ref, scaled_change_ref, change_ref, sums_ref, planes_ref, xy_ref,
):
    points, weight_x, _, _ = columns_of_nodes()
    inv_ends = column(1.0 / ENDS)
    image_ref[...] = first_ref[...]
    near, _ = face_rows(image_ref)
    image_ref[:, near, :] += near_in_ref[:, 0:64, :]
    whole_ref[...] = image_ref[...] + smooth_ref[...]
    over_diag(functools.partial(get, whole_ref), scaled_change_ref, layers_ref)
    operate(scaled_change_ref, xy_ref, change_ref, table_ref, layers_ref[0:1, :], weight_x)
    sum_xy(change_ref)
    sums = [jnp.zeros((8, PLANE), F32)] * 5
    for nz in range(8):
        for ny in range(8):
            rows = rows_of(nz, ny)
            share = float(1.0 / (ENDS[nz] * ENDS[ny]))
            scaled, scaled_change = get(scaled_ref, rows) * share, get(scaled_change_ref, rows) * share
            whole, image = get(whole_ref, rows), get(image_ref, rows)
            terms = [
                scaled * get(resid_ref, rows), scaled * whole, scaled_change * whole, scaled * image, scaled_change * image
            ]
            sums = [total + term for total, term in zip(sums, terms)]
    sums_ref[...] = jnp.concatenate(sums, axis=0)
    planes_ref[...] = jnp.concatenate(list(restrict(change_ref, points, inv_ends)) * 4, axis=0)


def second_faces(
    first_ref, first_scaled_ref, first_change_ref, whole_ref, far_in_ref, near_in_ref, layers_ref, table_ref,
    scaled_ref, lower_ref, sums_ref, planes_ref,
    image_ref, scaled_change_ref, change_ref, far_ref, near_ref, payload_ref, edge_ref, xy_ref,
):
    points, weight_x, diag_x, ends_x = columns_of_nodes()
    inv_ends = column(1.0 / ENDS)
    for out_ref, ref in (
        (image_ref, first_ref), (scaled_change_ref, first_scaled_ref), (change_ref, first_change_ref)
    ):
        out_ref[...] = ref[...]
    even = lax.rem(my_layer(), 2) == 0
    own = layers_ref[0:1, :]
    beyond = jnp.where(even, layers_ref[1:2, :], layers_ref[2:3, :])
    kappas = kappa_sums(own, beyond, beyond)
    _, far = face_rows(image_ref)
    sums = [sums_ref[8 * k : 8 * k + 8, :] for k in range(5)]
    s_plane, q_plane, i_plane, w_plane = (
        get(ref, far) for ref in (scaled_ref, scaled_change_ref, image_ref, whole_ref)
    )
    added = []
    for ny in range(8):
        tile = slice(8 * ny, 8 * ny + 8)
        face = get(far_in_ref, tile)
        dq = face / fine_diag(kappas, 0, ny, weight_x, diag_x, ends_x)
        added.append(dq)
        share = float(1.0 / (ENDS[0] * ENDS[ny]))
        s, q, image, whole = s_plane[tile] * share, q_plane[tile] * share, i_plane[tile], w_plane[tile]
        dq = dq * share
        sums[1] = sums[1] + s * face
        sums[2] = sums[2] + (q * face + dq * (whole + face))
        sums[3] = sums[3] + s * face
        sums[4] = sums[4] + (q * face + dq * (image + face))
    plane = jnp.concatenate(added, axis=0)
    put(image_ref, far, i_plane + get(far_in_ref, slice(0, 64)))
    put(scaled_change_ref, far, q_plane + plane)
    xy_ref[...] = jnp.dot(
        table_ref[:, 0:64], plane, precision=lax.Precision.HIGHEST, preferred_element_type=F32
    )
    for ny in range(8):
        area = weight_x * float(WEIGHTS[ny])
        put(edge_ref, rows_of(0, ny), own * area * added[ny])
        flux = own * xy_ref[8 * ny : 8 * ny + 8, :] + (float(REACT) * area) * added[ny]
        put(edge_ref, rows_of(1, ny), float(WEIGHTS[0]) * flux)
    sum_xy(edge_ref)
    put(change_ref, far, get(change_ref, far) + get(edge_ref, slice(64, 128)))
    energy = jnp.zeros((8, PLANE), F32)
    for nz in range(8):
        factor = jnp.where(even, float(STIFF[nz, 0]), float(STIFF[nz, 7]))
        for ny in range(8):
            rows = rows_of(nz, ny)
            change = get(change_ref, rows) + factor * get(edge_ref, rows_of(0, ny))
            put(change_ref, rows, change)
            energy = energy + (get(scaled_change_ref, rows) * change) * float(1.0 / ENDS[ny])
    faces_out(change_ref, near_ref, far_ref)
    sign = jnp.where(even, -1.0, 1.0)
    along = [get(edge_ref, rows_of(0, ny)) for ny in range(8)]
    at_face = [get(edge_ref, rows_of(1, ny)) for ny in range(8)]
    lower, upper = restrict_xy(at_face, [sign * (a + b) for a, b in zip(along, at_face)], points, inv_ends)
    lower, upper = lower + planes_ref[0:1, :], upper + planes_ref[1:2, :]
    below, _ = below_above(row_after_face(near_in_ref), row_after_face(far_in_ref))
    sums = pack([total * inv_ends for total in sums + [energy]])
    send(payload_ref, [lower_ref[0:1, :] + below, lower, upper, sums])


def folded(value):
    return functools.reduce(lambda a, b: a + b, [value[k : k + 8] for k in range(0, value.shape[0], 8)])


def second_coarse(
    coeff_ref, step_ref, first_ref, applied_ref, target_ref, scale_ref, modes_ref, scalars_ref, vert_ref
):
    modes = coarse_modes(coeff_ref[...])
    target, first, applied = target_ref[...], first_ref[...], applied_ref[...]
    rough, rough_change = gathered(step_ref, 0, 4), gathered(step_ref, 1, 4) + prev_z(gathered(step_ref, 2, 4))
    parts = folded(gathered(step_ref, 3, 4))
    sums = [parts] + [pltpu.roll(parts, PLANE - 32 * k, 1) for k in range(1, 6)]
    used = lane(parts.shape) < 32

    def total(fine, coarse):
        return jnp.sum(jnp.where(used, fine, 0.0) + folded(coarse), keepdims=True)

    gamma = total(sums[0], target * first)
    energy = total(sums[3], first * (2.0 * rough + applied))
    alpha = gamma / energy
    change = rough + applied
    target = target - alpha * change
    vert = coarse_solve(target, modes, scale_ref[...])
    progress = total(sums[0] - alpha * (2.0 * sums[1] - alpha * sums[2]), target * vert)
    second = total(
        sums[3] - alpha * (2.0 * sums[4] - alpha * sums[5]),
        vert * (2.0 * (rough - alpha * rough_change) + coarse_apply(vert, modes)),
    )
    cross = total(sums[1] - alpha * sums[2], vert * change)
    beta = progress / gamma
    alpha_next = progress / (second + beta * (2.0 * cross + beta * energy))
    share = alpha + alpha_next * beta
    vert_ref[...] = share * first + alpha_next * vert
    modes_ref[...] = three_modes(vert_ref)
    scalars = [share + alpha_next, alpha_next * alpha]
    scalars_ref[...] = jnp.concatenate([jnp.broadcast_to(t, (1, 128)) for t in scalars * 4], axis=0)


def to_stored(choose, value):
    total = jnp.zeros((PLANE, value.shape[0]), F32)
    for piece in pieces(value)[1:]:
        total = total + lax.dot_general(choose, piece, (((1,), (1,)), ((), ())), preferred_element_type=F32)
    return total


def closing(
    resid_ref, scaled_ref, image_ref, scaled_change_ref, change_ref, far_ref, near_ref, modes_ref, layers_ref, scalars_ref,
    choose_ref, solution_ref, residual_ref, grid_ref, sum_ref, edge_ref, held, sems,
):
    smooths = smooths_of(modes_ref[...], layers_ref)
    first, second = scalars_ref[0:1, 0:1], scalars_ref[1:2, 0:1]
    choose = choose_ref[...]
    for nz in range(8):
        for ny in range(8):
            rows = rows_of(nz, ny)
            rough = first * get(scaled_ref, rows) - second * get(scaled_change_ref, rows)
            grid_ref[rows, :] = rough + smooths[0].value(nz, ny)
    held[0] = to_stored(choose, grid_ref[...])
    copies = [pltpu.make_async_copy(held.at[0], solution_ref, sems.at[0])]
    copies[0].start()
    smooth_image(smooths, sum_ref, edge_ref)
    first, second = first[None], second[None]
    sum_ref[...] = resid_ref[...] - first * image_ref[...] + second * change_ref[...] - sum_ref[...]
    near, far = face_rows(sum_ref)
    sum_ref[:, near, :] += second * near_ref[...]
    sum_ref[:, far, :] += second * far_ref[...]
    held[1] = to_stored(choose, get(sum_ref, slice(0, 512)))
    copies.append(pltpu.make_async_copy(held.at[1], residual_ref, sems.at[1]))
    copies[1].start()
    for copy in copies:
        copy.wait()


def call(kernel, outs, scratch=(), sems=0, hbm_out=False, cost=None, in_place=None, hbm_in=0):
    spec = pl.BlockSpec(memory_space=pltpu.HBM if hbm_out else pltpu.VMEM)
    more = {"in_specs": [pl.BlockSpec(memory_space=pltpu.HBM)] * hbm_in} if hbm_in else {}
    return pl.pallas_call(
        kernel,
        out_shape=[jax.ShapeDtypeStruct(*(s if isinstance(s[0], tuple) else (s, F32))) for s in outs],
        out_specs=[spec for _ in outs],
        scratch_shapes=[pltpu.VMEM(*(s if isinstance(s[0], tuple) else (s, F32))) for s in scratch]
        + ([pltpu.SemaphoreType.DMA((sems,))] if sems else []),
        compiler_params=pltpu.CompilerParams(vmem_limit_bytes=12 * 1024 * 1024),
        cost_estimate=cost,
        input_output_aliases=in_place or {},
        **more,
    )


def swapped(x, far):
    size = lax.axis_size(AXES)
    return lax.ppermute(x, AXES, [(i, (i + (1 if (i % 2 == 0) != far else -1)) % size) for i in range(size)])


def everyone(payload, size):
    devices = lax.axis_size(AXES)
    return lax.all_to_all(payload.reshape(devices, size, 2, 128), AXES, 0, 0, tiled=True).reshape(-1, 128)


def per_device(forcing, kappa, elem_order):
    devices = lax.axis_size(AXES)
    nodes, face, face_row = (2, 512, 128), (2, 64, 128), (2, 72, 128)
    plane, grid, flat = (8, PLANE), (devices, PLANE), (512, PLANE)
    edge, stored, choice = (2, 128, 128), (PLANE, 512), ((PLANE, PLANE), jnp.bfloat16)
    table = jnp.asarray(STIFF_XY, F32)
    long = pl.CostEstimate(flops=10**11, bytes_accessed=2**28, transcendentals=0)
    load, far, near, own = call(
        opening,
        [nodes, face_row, face_row, plane],
        [(2, PLANE, 256), (1, PLANE), ((1, PLANE), jnp.int32)],
        4,
        hbm_in=3,
    )(*(pltpu.with_memory_space_constraint(x, pltpu.HBM) for x in (forcing, kappa.reshape(1, PLANE), elem_order)))
    far, near = swapped(far, True), swapped(near, False)
    (payload,) = call(opening_payload, [(devices * 6, 128)])(load, own)
    gather = everyone(payload, 3)
    resid, scaled, image, layers, lower, far, near = call(
        first_faces, [nodes, nodes, nodes, plane, plane, face_row, face_row], [flat], cost=long, in_place={0: 0}
    )(load, far, near, own, table)
    far, near = swapped(far, True), swapped(near, False)
    vert, applied, target, scale, coeff, choose, smooth = call(first_coarse, [grid] * 5 + [choice, nodes], [edge])(
        gather, layers
    )
    image, whole, scaled_change, change, sums, planes = call(
        second_rough, [nodes] * 4 + [(40, PLANE), plane], [flat], in_place={0: 0, 1: 1}
    )(image, smooth, near, layers, table, resid, scaled)
    image, scaled_change, change, far, near, payload = call(
        second_faces, [nodes] * 3 + [face, face, (devices * 8, 128)], [edge, (64, PLANE)], in_place={0: 0, 1: 1, 2: 2}
    )(image, scaled_change, change, whole, far, near, layers, table, scaled, lower, sums, planes)
    step = everyone(payload, 4)
    far, near = swapped(far, True), swapped(near, False)
    modes, scalars = call(second_coarse, [(24, PLANE), (8, 128)], [grid])(coeff, step, vert, applied, target, scale)
    found, left = call(closing, [stored, stored], [flat, nodes, edge, (2,) + stored], 2, hbm_out=True)(
        resid, scaled, image, scaled_change, change, far, near, modes, layers, scalars, choose
    )
    return found, left


def solution(mesh):
    in_specs = (P(AXES, None), P(AXES), P(AXES, None))
    out_specs = (P(AXES, None), P(AXES, None))
    return jax.shard_map(
        per_device, mesh=mesh, in_specs=in_specs, out_specs=out_specs, check_vma=False
    )
```

```python
import functools
import math

import jax
import jax.numpy as jnp
import ml_dtypes
import numpy as np
from jax import lax
from jax.experimental import pallas as pl
from jax.experimental.pallas import tpu as pltpu
from jax.sharding import PartitionSpec as P

EX = 8
EY = 32
PLANE = EX * EY
SWEEPS = 4
REACT = 0.02
OMEGA = 0.6
AXES = ("elem", "face")
F32 = jnp.float32


def legendre_seven(points):
    before = np.ones(8)
    current = np.array(points)
    for degree in range(1, 7):
        following = ((2 * degree + 1) * points * current - degree * before) / (degree + 1)
        before = current
        current = following
    return current


def line_tables():
    points = np.array(
        [
            -1.0,
            -0.8717401485096066,
            -0.5917001814331423,
            -0.2092992179024789,
            0.2092992179024789,
            0.5917001814331423,
            0.8717401485096066,
            1.0,
        ]
    )
    weights = np.array(
        [
            1.0 / 28.0,
            0.2107042271435061,
            0.3411226924835044,
            0.4124587946587038,
            0.4124587946587038,
            0.3411226924835044,
            0.2107042271435061,
            1.0 / 28.0,
        ]
    )
    legendre = legendre_seven(points)
    derivative = np.zeros((8, 8))
    for left_node in range(8):
        for right_node in range(8):
            if left_node != right_node:
                derivative[left_node, right_node] = legendre[left_node] / (
                    legendre[right_node] * (points[left_node] - points[right_node])
                )
    derivative[0, 0] = -14.0
    derivative[7, 7] = 14.0
    stiffness = derivative.T @ (weights[:, None] * derivative)
    return points, weights, stiffness


POINTS, WEIGHTS, STIFF = line_tables()
DIAG = np.diag(STIFF)
ENDS = np.array([2.0] + [1.0] * 6 + [2.0])
MASS = np.diag(WEIGHTS)
STIFF_XY = np.tile(np.kron(MASS, STIFF) + np.kron(STIFF, MASS), (1, 2))
STIFF_PARTS = []
for part in range(3):
    STIFF_PARTS.append((STIFF_XY - sum(STIFF_PARTS)).astype(ml_dtypes.bfloat16).astype(np.float64))
INTERP = np.stack([(1.0 - POINTS) / 2.0, (1.0 + POINTS) / 2.0], 1)
LINE_MASS = INTERP.T @ (WEIGHTS[:, None] * INTERP)
LINE_STIFF = INTERP.T @ STIFF @ INTERP
MASS_SUM = (LINE_MASS[0, 0] + LINE_MASS[0, 1]) / 2.0
MASS_DIF = (LINE_MASS[0, 0] - LINE_MASS[0, 1]) / 2.0
STIFF_DIF = LINE_STIFF[0, 0]
MODE_STIFF = [
    0.0,
    STIFF_DIF * MASS_SUM**2,
    2.0 * STIFF_DIF * MASS_DIF * MASS_SUM,
    3.0 * STIFF_DIF * MASS_DIF**2,
]
MODE_MASS = [MASS_SUM ** (3 - j) * MASS_DIF**j for j in range(4)]
CORNER_STIFF = 3.0 * LINE_STIFF[0, 0] * LINE_MASS[0, 0] ** 2
CORNER_MASS = LINE_MASS[0, 0] ** 3


def lane(shape):
    return lax.broadcasted_iota(jnp.int32, shape, len(shape) - 1)


def next_x(v):
    return jnp.where(lane(v.shape) % EX == EX - 1, pltpu.roll(v, EX - 1, 1), pltpu.roll(v, PLANE - 1, 1))


def prev_x(v):
    return jnp.where(lane(v.shape) % EX == 0, pltpu.roll(v, PLANE - EX + 1, 1), pltpu.roll(v, 1, 1))


def next_y(v):
    return pltpu.roll(v, PLANE - EX, 1)


def prev_y(v):
    return pltpu.roll(v, EX, 1)


def next_xy(v):
    return jnp.where(lane(v.shape) % EX == EX - 1, pltpu.roll(v, PLANE - 1, 1), pltpu.roll(v, PLANE - EX - 1, 1))


def prev_xy(v):
    return jnp.where(lane(v.shape) % EX == 0, pltpu.roll(v, 1, 1), pltpu.roll(v, EX + 1, 1))


def next_z(v):
    half = v.shape[0] // 2
    return jnp.concatenate([v[half:], pltpu.roll(v[:half], half - 1, 0)], axis=0)


def prev_z(v):
    half = v.shape[0] // 2
    return jnp.concatenate([pltpu.roll(v[half:], 1, 0), v[:half]], axis=0)


def plane_row(layer, planes):
    layer = lax.rem(layer + planes, planes)
    return pl.ds(lax.div(layer, 2) + lax.rem(layer, 2) * (planes // 2), 1)


def column(values):
    row = lax.broadcasted_iota(jnp.int32, (8, PLANE), 0)
    out = jnp.full((8, PLANE), float(values[0]), F32)
    for k in range(1, 8):
        out = jnp.where(row == k, float(values[k]), out)
    return out


def rows_of(nz, ny):
    start = (nz * 8 + ny) * 8
    return slice(start, start + 8)


def get(ref, rows):
    return jnp.concatenate([ref[0, rows, :], ref[1, rows, :]], axis=1)


def put(ref, rows, value):
    ref[0, rows, :] = value[:, :128]
    ref[1, rows, :] = value[:, 128:]


def sum_xy(ref):
    planes = ref.shape[1] // 64
    first, last = pl.ds(0, planes * 8, stride=8), pl.ds(7, planes * 8, stride=8)
    shared = get(ref, last) + next_x(get(ref, first))
    put(ref, last, shared)
    put(ref, first, prev_x(shared))
    for nz in range(planes):
        shared = get(ref, rows_of(nz, 7)) + next_y(get(ref, rows_of(nz, 0)))
        put(ref, rows_of(nz, 7), shared)
        put(ref, rows_of(nz, 0), prev_y(shared))


def restrict(ref, points):
    sums_z, difs_z = [], []
    for ny in range(8):
        tiles = [get(ref, rows_of(nz, ny)) for nz in range(8)]
        sums_z.append(functools.reduce(lambda a, b: a + b, tiles))
        difs_z.append(sum(float(POINTS[7 - k]) * (tiles[7 - k] - tiles[k]) for k in range(4)))
    return restrict_xy(sums_z, difs_z, points)


def restrict_summed(ref, points):
    inv_ends = column(1.0 / ENDS)
    sums_z, difs_z = [], []
    for ny in range(8):
        tiles = [get(ref, rows_of(nz, ny)) for nz in range(8)]
        share = inv_ends * float(1.0 / ENDS[ny])
        sums_z.append(functools.reduce(lambda a, b: a + b, tiles) * share)
        difs_z.append(sum(float(POINTS[7 - k]) * (tiles[7 - k] - tiles[k]) for k in range(4)) * share)
    return restrict_xy(sums_z, difs_z, points)


def restrict_xy(sums_z, difs_z, points):
    planes = []
    for parts in (sums_z, difs_z):
        total = functools.reduce(lambda a, b: a + b, parts)
        slope = sum(float(POINTS[7 - k]) * (parts[7 - k] - parts[k]) for k in range(4))
        in_y = []
        for part in (total, slope):
            flat = jnp.sum(part, axis=0, keepdims=True)
            steep = jnp.sum(part * points, axis=0, keepdims=True)
            in_y.append((flat - steep) + prev_x(flat + steep))
        planes.append((in_y[0] - in_y[1]) + prev_y(in_y[0] + in_y[1]))
    return (planes[0] - planes[1]) * 0.125, (planes[0] + planes[1]) * 0.125


def both(v, following):
    after = following(v)
    return after + v, after - v


def both_back(total, dif, preceding):
    return (total - dif) + preceding(total + dif)


def coarse_modes(coeff):
    return [float(REACT * MODE_MASS[0])] + [
        float(MODE_STIFF[j]) * coeff + float(REACT * MODE_MASS[j]) for j in range(1, 4)
    ]


def coarse_tables(coeff):
    near = coeff + prev_x(coeff)
    near = near + prev_y(near)
    near = near + prev_z(near)
    scale = float(OMEGA) / (float(CORNER_STIFF) * near + float(8.0 * REACT * CORNER_MASS))
    return coarse_modes(coeff), scale


def coarse_apply(vert, modes):
    after_x, after_y, after_xy = next_x(vert), next_y(vert), next_xy(vert)
    in_x = [(after_x + vert, after_xy + after_y), (after_x - vert, after_xy - after_y)]
    back = []
    for jx in range(2):
        first, second = in_x[jx]
        for jy, in_y in enumerate((second + first, second - first)):
            in_z = both(in_y, next_z)
            scaled = [modes[jx + jy + jz] * in_z[jz] for jz in range(2)]
            back.append(both_back(scaled[0], scaled[1], prev_z))
    ss, sd, ds, dd = back
    low, high = (ss - sd, ss + sd), (ds - dd, ds + dd)
    return ((low[0] - high[0]) + prev_x(low[0] + high[0])) + (prev_y(low[1] - high[1]) + prev_xy(low[1] + high[1]))


def coarse_solve(target, modes, scale):
    vert = scale * target
    for _ in range(SWEEPS - 1):
        vert = vert + scale * (target - coarse_apply(vert, modes))
    return vert


def gathered_rows(ref, row, size):
    chips = ref.shape[0] // (2 * size)
    return jnp.concatenate([ref[pl.ds(core * size + row, chips, stride=2 * size), :] for core in range(2)], axis=0)


def gathered(ref, k, size):
    return jnp.concatenate([gathered_rows(ref, 2 * k + h, size) for h in range(2)], axis=1)


def halves(row):
    return [row[:, :128], row[:, 128:]]


def send(ref, rows):
    count = len(rows)
    times = 8 // math.gcd(count, 8)
    block = jnp.concatenate(rows * times, axis=0)
    for k in range(0, ref.shape[0], count * times):
        ref[k : k + count * times, :] = block


def layer_modes(vert_ref, shift):
    me, devices = my_layer(), vert_ref.shape[0]
    lower, upper = (vert_ref[plane_row(me + shift + k, devices), :] for k in range(2))
    modes = []
    for along_z in (upper + lower, upper - lower):
        for along_y in both(along_z, next_y):
            modes += both(along_y, next_x)
    return 0.125 * jnp.concatenate(modes, axis=0)


class Smooth:
    def __init__(self, modes, coeff, points, weight_x):
        row = lax.broadcasted_iota(jnp.int32, (8, PLANE), 0)
        ends = jnp.where(row == 0, -1.0, jnp.where(row == 7, 1.0, 0.0))
        m = [[[modes[4 * z + 2 * y + x : 4 * z + 2 * y + x + 1] for x in range(2)] for y in range(2)] for z in range(2)]
        self.xy = [[m[z][y][0] + m[z][y][1] * points for y in range(2)] for z in range(2)]
        self.dx = [[m[z][y][1] for y in range(2)] for z in range(2)]
        self.ends_coeff = ends * coeff
        self.weight_coeff = weight_x * coeff
        self.mass = float(REACT) * weight_x

    def value(self, nz, ny):
        by_y = [self.xy[z][0] + float(POINTS[ny]) * self.xy[z][1] for z in range(2)]
        return by_y[0] + float(POINTS[nz]) * by_y[1]

    def operated(self, nz, ny, value):
        wy, wz, py, pz = (float(t) for t in (WEIGHTS[ny], WEIGHTS[nz], POINTS[ny], POINTS[nz]))
        slope = (self.dx[0][0] + py * self.dx[0][1]) + pz * (self.dx[1][0] + py * self.dx[1][1])
        out = self.ends_coeff * (slope * (wy * wz)) + (self.mass * (wy * wz)) * value
        flux = None
        if ny in (0, 7):
            flux = (self.xy[0][1] + pz * self.xy[1][1]) * (wz * py)
        if nz in (0, 7):
            along = (self.xy[1][0] + py * self.xy[1][1]) * (wy * pz)
            flux = along if flux is None else flux + along
        return out if flux is None else out + self.weight_coeff * flux


def kappa_sums(own, below, above):
    row = lax.broadcasted_iota(jnp.int32, (8, PLANE), 0)
    table = []
    for along_z in (own + below, own, own + above):
        in_z = []
        for along_y in (along_z + prev_y(along_z), along_z, along_z + next_y(along_z)):
            first = along_y + prev_x(along_y)
            last = along_y + next_x(along_y)
            in_z.append(jnp.where(row == 0, first, jnp.where(row == 7, last, along_y)))
        table.append(in_z)
    return table


def kind(node):
    return 0 if node == 0 else (2 if node == 7 else 1)


def product(tables, values):
    low, middle, high = pieces(values)

    def dot(k, right):
        return jnp.dot(tables[k], right, preferred_element_type=F32)

    return dot(0, high) + ((dot(0, middle) + dot(1, high)) + (dot(1, middle) + (dot(0, low) + dot(2, high))))


def operate(z_ref, xy_ref, out_ref, table_ref, coeff, weight_x):
    row, col = (lax.broadcasted_iota(jnp.int32, (256, 256), axis) for axis in range(2))
    tables = [
        jnp.where(row // 64 == col // 64, jnp.tile(table_ref[k].astype(F32), (4, 2)), 0.0).astype(jnp.bfloat16) for k in range(3)
    ]
    for half in range(2):
        rows = slice(half * 256, half * 256 + 256)
        xy_ref[rows, :] = product(tables, get(z_ref, rows))
    for ny in range(8):
        tiles = [get(z_ref, rows_of(nz, ny)) for nz in range(8)]
        even = [tiles[k] + tiles[7 - k] for k in range(4)]
        odd = [tiles[k] - tiles[7 - k] for k in range(4)]
        for nz in range(4):
            even_part = sum(float((STIFF[nz, k] + STIFF[nz, 7 - k]) / 2) * even[k] for k in range(4))
            odd_part = sum(float((STIFF[nz, k] - STIFF[nz, 7 - k]) / 2) * odd[k] for k in range(4))
            for node, term in ((nz, even_part + odd_part), (7 - nz, even_part - odd_part)):
                area = weight_x * float(WEIGHTS[ny])
                local = coeff * (
                    float(WEIGHTS[node]) * xy_ref[rows_of(node, ny), :] + area * term
                ) + (float(REACT * WEIGHTS[node]) * area) * tiles[node]
                put(out_ref, rows_of(node, ny), local)


def fine_diag(sums, nz, ny, weight_x, diag_x, ends_x):
    wy, wz, ky, kz = (float(t) for t in (WEIGHTS[ny], WEIGHTS[nz], DIAG[ny], DIAG[nz]))
    stiff = diag_x * (wy * wz) + weight_x * (ky * wz + wy * kz)
    mass = (weight_x * ends_x) * float(REACT * wy * wz * ENDS[ny] * ENDS[nz])
    return sums[kind(nz)][kind(ny)] * stiff + mass


def my_layer():
    return lax.axis_index("elem") * lax.axis_size("face") + lax.axis_index("face")


def face_rows(ref):
    even = lax.rem(my_layer(), 2) == 0
    last = ref.shape[1] - 64
    near = pl.multiple_of(jnp.where(even, last, 0), 64)
    far = pl.multiple_of(jnp.where(even, 0, last), 64)
    return pl.ds(near, 64), pl.ds(far, 64)


def faces_out(ref, near_ref, far_ref):
    for rows, out_ref in zip(face_rows(ref), (near_ref, far_ref)):
        out_ref[:, 0:56, :] = ref[:, pl.ds(rows.start, 56), :]


def face_in(ref):
    return jnp.concatenate([get(ref, slice(0, 56)), next_y(get(ref, slice(0, 8)))], axis=0)


def faces_in(ref, near_ref, far_ref):
    for rows, in_ref in zip(face_rows(ref), (near_ref, far_ref)):
        put(ref, rows, get(ref, rows) + face_in(in_ref))


def columns_of_nodes():
    return column(POINTS), column(WEIGHTS), column(DIAG), column(ENDS)


def pieces(v):
    high = v.astype(jnp.bfloat16)
    rest = v - high.astype(F32)
    middle = rest.astype(jnp.bfloat16)
    low = (rest - middle.astype(F32)).astype(jnp.bfloat16)
    return low, middle, high


def selection(order):
    place = lax.broadcasted_iota(jnp.int32, (PLANE, PLANE), 0).astype(order.dtype)
    return jnp.where(place == order, 1.0, 0.0).astype(jnp.bfloat16)


def opening(
    forcing_ref, kappa_ref, order_ref, load_ref, far_ref, near_ref, own_ref, payload_ref,
    held, held_kappa, held_order, held_payload, sems,
):
    small = [
        pltpu.make_async_copy(order_ref, held_order, sems.at[0]),
        pltpu.make_async_copy(kappa_ref, held_kappa, sems.at[1]),
    ]
    parts = [
        pltpu.make_async_copy(forcing_ref.at[:, pl.ds(256 * k, 256)], held.at[k], sems.at[2 + k]) for k in range(2)
    ]
    for copy in small + parts:
        copy.start()
    for copy in small:
        copy.wait()
    order = held_order[...]
    choose = selection(order)
    coeff = jnp.zeros((8, PLANE), F32)
    for piece in pieces(jnp.broadcast_to(held_kappa[...], (8, PLANE))):
        coeff = coeff + lax.dot_general(piece, choose, (((1,), (1,)), ((), ())), preferred_element_type=F32)
    own = jnp.concatenate([coeff[0:3], order.astype(F32), coeff[4:8]], axis=0)
    own_ref[...] = own
    for k, copy in enumerate(parts):
        copy.wait()
        load = jnp.zeros((PLANE, 256), F32)
        for piece in pieces(held[k]):
            load = load + jnp.dot(choose, piece, preferred_element_type=F32)
        put(load_ref, slice(256 * k, 256 * k + 256), load.T)
    sum_xy(load_ref)
    faces_out(load_ref, near_ref, far_ref)
    put(near_ref, slice(56, 64), own)
    put(far_ref, slice(56, 64), own)


    @pl.when(starts_early())
    def _():
        write_payload(load_ref, own_ref, payload_ref, held_payload, sems.at[4])


def starts_early():
    return my_layer() < lax.axis_size("elem") * lax.axis_size("face") // 2


def write_payload(load_ref, own_ref, payload_ref, held, sem):
    lower, upper = restrict_summed(load_ref, column(POINTS))
    send(held, halves(lower) + halves(upper) + halves(own_ref[0:1, :]))
    copy = pltpu.make_async_copy(held, payload_ref, sem)
    copy.start()
    copy.wait()


def late_payload(load_ref, own_ref, _, payload_ref, held, sems):
    @pl.when(jnp.logical_not(starts_early()))
    def _():
        write_payload(load_ref, own_ref, payload_ref, held, sems.at[0])


def below_above(near, far):
    even = lax.rem(my_layer(), 2) == 0
    return jnp.where(even, far, near), jnp.where(even, near, far)


def row_after_face(ref):
    return get(ref, slice(56, 64))[0:1]


def first_faces(
    load_ref, far_in_ref, near_in_ref, own_ref, table_ref,
    resid_ref, scaled_ref, image_ref, layers_ref, lower_ref, far_ref, near_ref, xy_ref,
):
    points, weight_x, _, _ = columns_of_nodes()
    own = own_ref[0:1, :]
    below, above = below_above(row_after_face(near_in_ref), row_after_face(far_in_ref))
    layers_ref[...] = jnp.concatenate([own, below, above, own_ref[3:8, :]], axis=0)
    resid_ref[...] = load_ref[...]
    faces_in(resid_ref, near_in_ref, far_in_ref)
    over_diag(functools.partial(get, resid_ref), scaled_ref, layers_ref)
    operate(scaled_ref, xy_ref, image_ref, table_ref, own, weight_x)
    lower, upper = restrict(image_ref, points)
    sum_xy(image_ref)
    faces_out(image_ref, near_ref, far_ref)
    lower_ref[...] = jnp.broadcast_to(lower, lower_ref.shape)
    put(near_ref, slice(56, 64), jnp.broadcast_to(upper, (8, PLANE)))
    put(far_ref, slice(56, 64), jnp.broadcast_to(upper, (8, PLANE)))


def over_diag(resid, scaled_ref, layers_ref):
    _, weight_x, diag_x, ends_x = columns_of_nodes()
    sums = kappa_sums(*(layers_ref[k : k + 1, :] for k in range(3)))
    for nz in range(8):
        for ny in range(8):
            rows = rows_of(nz, ny)
            put(scaled_ref, rows, resid(rows) / fine_diag(sums, nz, ny, weight_x, diag_x, ends_x))


def three_modes(vert_ref):
    return jnp.concatenate([layer_modes(vert_ref, shift) for shift in (0, -1, 1)], axis=0)


def smooths_of(modes, layers_ref):
    points, weight_x, _, _ = columns_of_nodes()
    return [Smooth(modes[8 * k : 8 * k + 8], layers_ref[k : k + 1, :], points, weight_x) for k in range(3)]


def smooth_image(smooths, out_ref, edge_ref):
    own, below, above = smooths
    for nz in range(8):
        for ny in range(8):
            put(out_ref, rows_of(nz, ny), own.operated(nz, ny, own.value(nz, ny)))
    sum_xy(out_ref)
    for plane, (smooth, nz) in enumerate(((below, 7), (above, 0))):
        for ny in range(8):
            put(edge_ref, rows_of(plane, ny), smooth.operated(nz, ny, smooth.value(nz, ny)))
    sum_xy(edge_ref)
    out_ref[:, 0:64, :] += edge_ref[:, 0:64, :]
    out_ref[:, 448:512, :] += edge_ref[:, 64:128, :]


def first_coarse(coarse_ref, layers_ref, vert_ref, target_ref, scale_ref, coeff_ref, smooth_ref, edge_ref):
    coeff = gathered(coarse_ref, 2, 6)
    coeff_ref[...] = coeff
    modes, scale = coarse_tables(coeff)
    target = gathered(coarse_ref, 0, 6) + prev_z(gathered(coarse_ref, 1, 6))
    vert = coarse_solve(target, modes, scale)
    vert_ref[...] = vert
    target_ref[...] = target
    scale_ref[...] = scale
    smooth_image(smooths_of(three_modes(vert_ref), layers_ref), smooth_ref, edge_ref)


def pack(sums):
    place = lane((8, 128)) // 16
    packed = jnp.zeros((8, 128), F32)
    for k, total in enumerate(sums):
        total = total[:, :128] + total[:, 128:]
        for by in (64, 32, 16):
            total = total + pltpu.roll(total, by, 1)
        packed = jnp.where(place == k, total, packed)
    return jnp.sum(packed, axis=0, keepdims=True)


def second_rough(
    image_ref, smooth_ref, layers_ref, table_ref, resid_ref, scaled_ref,
    scaled_change_ref, change_ref, sums_ref, planes_ref, column_ref, outer_ref, xy_ref, whole_ref,
):
    points, weight_x, _, _ = columns_of_nodes()
    inv_ends = column(1.0 / ENDS)
    whole_ref[...] = image_ref[...] + smooth_ref[...]
    over_diag(functools.partial(get, whole_ref), scaled_change_ref, layers_ref)
    operate(scaled_change_ref, xy_ref, change_ref, table_ref, layers_ref[0:1, :], weight_x)
    planes_ref[...] = jnp.concatenate(list(restrict(change_ref, points)) * 4, axis=0)
    sum_xy(change_ref)
    sums = [jnp.zeros((8, PLANE), F32)] * 6
    for ny in range(8):
        along = [jnp.zeros((8, PLANE), F32)] * 2
        for nz in range(8):
            rows = rows_of(nz, ny)
            share = float(1.0 / (ENDS[nz] * ENDS[ny]))
            scaled, change = get(scaled_ref, rows) * share, get(scaled_change_ref, rows)
            along = [total + float(STIFF[nz, node]) * change for total, node in zip(along, (0, 7))]
            change = change * share
            whole, image = get(whole_ref, rows), get(image_ref, rows)
            terms = [
                scaled * get(resid_ref, rows), scaled * whole, change * whole, scaled * image, change * image,
                change * (get(change_ref, rows) * float(ENDS[nz])),
            ]
            sums = [total + term for total, term in zip(sums, terms)]
        for k in range(2):
            column_ref[64 * k + 8 * ny : 64 * k + 8 * ny + 8, :] = along[k]
    sums_ref[...] = jnp.concatenate([total * inv_ends for total in sums], axis=0)
    for k, rows in enumerate((slice(0, 64), slice(448, 512))):
        outer_ref[64 * k : 64 * k + 64, :] = get(whole_ref, rows)


def second_faces(
    image_ref, scaled_change_ref, change_ref, outer_ref, far_in_ref, near_in_ref, layers_ref, table_ref,
    scaled_ref, lower_ref, sums_ref, planes_ref, column_ref,
    added_ref, far_ref, near_ref, payload_ref, edge_ref, xy_ref,
):
    points, weight_x, _, _ = columns_of_nodes()
    inv_ends = column(1.0 / ENDS)
    even = lax.rem(my_layer(), 2) == 0
    own = layers_ref[0:1, :]
    kappas = kappa_sums(*(layers_ref[k : k + 1, :] for k in range(3)))
    faces = below_above(face_in(near_in_ref), face_in(far_in_ref))
    tiles = [slice(8 * ny, 8 * ny + 8) for ny in range(8)]
    added = added_by(faces, kappas, columns_of_nodes())
    small_tables = [table_ref[k, :, 0:64] for k in range(3)]
    xy_ref[...] = product(small_tables, jnp.concatenate(added, axis=1))
    along, at_face = [], []
    for k in range(2):
        along.append(local_along(own, weight_x, added[k]))
        flux = own * xy_ref[:, PLANE * k : PLANE * k + PLANE]
        at_face.append(float(WEIGHTS[0]) * jnp.concatenate(
            [flux[t] + (float(REACT * WEIGHTS[ny]) * weight_x) * added[k][t] for ny, t in enumerate(tiles)], axis=0
        ))
    local = [
        (float(STIFF[nz, 0]) * along[0] + float(STIFF[nz, 7]) * along[1]) + at_face[k] for k, nz in enumerate((0, 7))
    ]
    flat = at_face[0] + at_face[1]
    slope = (along[1] + at_face[1]) - (along[0] + at_face[0])
    lower, upper = restrict_xy([flat[t] for t in tiles], [slope[t] for t in tiles], points)
    lower, upper = lower + planes_ref[0:1, :], upper + planes_ref[1:2, :]
    sums = [jnp.zeros((8, PLANE), F32)] * 5
    energy = jnp.zeros((8, PLANE), F32)
    planes = [slice(0, 64), slice(448, 512)]
    for k in range(2):
        s_plane, q_plane, i_plane, c_plane = (
            get(ref, planes[k]) for ref in (scaled_ref, scaled_change_ref, image_ref, change_ref)
        )
        w_plane = outer_ref[64 * k : 64 * k + 64, :]
        for ny in range(8):
            tile = tiles[ny]
            share = float(1.0 / ENDS[ny])
            half = share * float(1.0 / ENDS[0])
            face = faces[k][tile]
            s, q, dq = s_plane[tile] * half, q_plane[tile] * half, added[k][tile] * half
            sums[0] = sums[0] + s * face
            sums[1] = sums[1] + (q * face + dq * (w_plane[tile] + face))
            sums[2] = sums[2] + s * face
            sums[3] = sums[3] + (q * face + dq * (i_plane[tile] + face))
            sums[4] = sums[4] + (added[k][tile] * c_plane[tile]) * share
            energy = energy + (
                column_ref[64 * k + 8 * ny : 64 * k + 8 * ny + 8, :] * along[k][tile]
                + q_plane[tile] * at_face[k][tile]
                + added[k][tile] * local[k][tile]
            )
    sums = [sums_ref[8 * k + 8 : 8 * k + 16, :] + sums[k] * inv_ends for k in range(5)]
    sums = pack([sums_ref[0:8, :]] + sums[:4] + [sums[4] + energy])
    below, _ = below_above(row_after_face(near_in_ref), row_after_face(far_in_ref))
    send(payload_ref, halves(lower_ref[0:1, :] + below) + halves(lower) + halves(upper) + [sums])
    for k in range(2):
        put(edge_ref, slice(64 * k, 64 * k + 64), local[k])
        added_ref[64 * k : 64 * k + 64, :] = at_face[k]
    sum_xy(edge_ref)
    change = [(get(change_ref, planes[k]) + get(edge_ref, slice(64 * k, 64 * k + 64)))[0:56] for k in range(2)]
    put(far_ref, slice(0, 56), jnp.where(even, change[0], change[1]))
    put(near_ref, slice(0, 56), jnp.where(even, change[1], change[0]))


def local_along(own, weight_x, added):
    return own * jnp.concatenate(
        [(weight_x * float(WEIGHTS[ny])) * added[8 * ny : 8 * ny + 8] for ny in range(8)], axis=0
    )


def added_by(faces, kappas, columns):
    _, weight_x, diag_x, ends_x = columns
    return [
        jnp.concatenate(
            [
                face[8 * ny : 8 * ny + 8] / fine_diag(kappas, nz, ny, weight_x, diag_x, ends_x)
                for ny in range(8)
            ],
            axis=0,
        )
        for nz, face in zip((0, 7), faces)
    ]


def complete(
    first_ref, first_scaled_ref, first_change_ref, far_in_ref, near_in_ref, at_face_ref, layers_ref, coeff_ref, vert_ref,
    image_ref, scaled_change_ref, change_ref, choose_ref, applied_ref, modes_ref, edge_ref,
):
    columns = columns_of_nodes()
    applied_ref[...] = coarse_apply(vert_ref[...], coarse_modes(coeff_ref[...]))
    modes_ref[...] = three_modes(vert_ref)
    choose_ref[...] = selection(layers_ref[3:4, :]).astype(F32).T.astype(jnp.bfloat16)
    image_ref[...] = first_ref[...]
    scaled_change_ref[...] = first_scaled_ref[...]
    faces_in(image_ref, near_in_ref, far_in_ref)
    kappas = kappa_sums(*(layers_ref[k : k + 1, :] for k in range(3)))
    added = added_by(below_above(face_in(near_in_ref), face_in(far_in_ref)), kappas, columns)
    for k, rows in enumerate((slice(0, 64), slice(448, 512))):
        put(scaled_change_ref, rows, get(scaled_change_ref, rows) + added[k])
        put(edge_ref, slice(64 * k, 64 * k + 64), local_along(layers_ref[0:1, :], columns[1], added[k]))
        put(edge_ref, slice(128 + 64 * k, 192 + 64 * k), at_face_ref[64 * k : 64 * k + 64, :])
    sum_xy(edge_ref)
    along = [get(edge_ref, slice(64 * k, 64 * k + 64)) for k in range(2)]
    for nz in range(8):
        rows = slice(64 * nz, 64 * nz + 64)
        new = get(first_change_ref, rows) + (float(STIFF[nz, 0]) * along[0] + float(STIFF[nz, 7]) * along[1])
        if nz in (0, 7):
            new = new + get(edge_ref, slice(128 + 64 * (nz // 7), 192 + 64 * (nz // 7)))
        put(change_ref, rows, new)


def folded(value):
    return functools.reduce(lambda a, b: a + b, [value[k : k + 8] for k in range(0, value.shape[0], 8)])


def second_coarse(
    coeff_ref, step_ref, first_ref, applied_ref, target_ref, scale_ref, first_modes_ref, modes_ref, scalars_ref, vert_ref
):
    modes = coarse_modes(coeff_ref[...])
    target, first, applied = target_ref[...], first_ref[...], applied_ref[...]
    rough, rough_change = gathered(step_ref, 0, 7), gathered(step_ref, 1, 7) + prev_z(gathered(step_ref, 2, 7))
    parts = folded(gathered_rows(step_ref, 6, 7))
    sums = [parts] + [pltpu.roll(parts, 128 - 16 * k, 1) for k in range(1, 6)]
    used = lane(parts.shape) < 16

    def total(fine, coarse):
        coarse = folded(coarse)
        return jnp.sum(jnp.where(used, fine, 0.0) + (coarse[:, :128] + coarse[:, 128:]), keepdims=True)

    image = rough + applied
    change = coarse_solve(image, modes, scale_ref[...])
    vert_ref[...] = change
    change_modes = three_modes(vert_ref)
    change_applied = coarse_apply(change, modes)
    gamma = total(sums[0], target * first)
    energy = total(sums[3], first * (2.0 * rough + applied))
    alpha = gamma / energy
    vert = first - alpha * change
    progress = total(sums[0] - alpha * (2.0 * sums[1] - alpha * sums[2]), (target - alpha * image) * vert)
    second = total(
        sums[3] - alpha * (2.0 * sums[4] - alpha * sums[5]),
        vert * (2.0 * (rough - alpha * rough_change) + (applied - alpha * change_applied)),
    )
    cross = total(sums[1] - alpha * sums[2], vert * image)
    beta = progress / gamma
    alpha_next = progress / (second + beta * (2.0 * cross + beta * energy))
    scalars = [alpha + alpha_next * beta + alpha_next, alpha_next * alpha]
    modes_ref[...] = scalars[0] * first_modes_ref[...] - scalars[1] * change_modes
    scalars_ref[...] = jnp.concatenate([jnp.broadcast_to(t, (1, 128)) for t in scalars * 4], axis=0)


def to_stored(choose, value):
    total = jnp.zeros((choose.shape[0], value.shape[0]), F32)
    for piece in pieces(value)[1:]:
        total = total + lax.dot_general(choose, piece, (((1,), (1,)), ((), ())), preferred_element_type=F32)
    return total


def closing(
    resid_ref, scaled_ref, image_ref, scaled_change_ref, change_ref, far_ref, near_ref, modes_ref, layers_ref, scalars_ref,
    choose_ref, solution_ref, residual_ref, grid_ref, sum_ref, edge_ref, held, sems,
):
    smooths = smooths_of(modes_ref[...], layers_ref)
    first, second = scalars_ref[0:1, 0:1], scalars_ref[1:2, 0:1]
    choose = choose_ref[...]
    for nz in range(8):
        for ny in range(8):
            rows = rows_of(nz, ny)
            rough = first * get(scaled_ref, rows) - second * get(scaled_change_ref, rows)
            grid_ref[rows, :] = rough + smooths[0].value(nz, ny)
    held[0] = to_stored(choose, grid_ref[...])
    smooth_image(smooths, sum_ref, edge_ref)
    first, second = first[None], second[None]
    sum_ref[...] = resid_ref[...] - first * image_ref[...] + second * change_ref[...] - sum_ref[...]
    for rows, ref in zip(face_rows(sum_ref), (near_ref, far_ref)):
        put(sum_ref, rows, get(sum_ref, rows) + second[0] * face_in(ref))
    copies = [pltpu.make_async_copy(held.at[0], solution_ref, sems.at[0])]
    copies[0].start()
    for part in range(2):
        stored = slice(128 * part, 128 * part + 128)
        held[1, stored, :] = to_stored(choose[stored], get(sum_ref, slice(0, 512)))
        copies.append(pltpu.make_async_copy(held.at[1, stored], residual_ref.at[stored], sems.at[1 + part]))
        copies[-1].start()
    for copy in copies:
        copy.wait()


def call(kernel, outs, scratch=(), sems=0, cost=None, in_place=None, hbm_in=(), hbm_out=(), inputs=0):
    def specs(count, far):
        return [pl.BlockSpec(memory_space=pltpu.HBM if k in far else pltpu.VMEM) for k in range(count)]

    more = {"in_specs": specs(inputs, hbm_in)} if hbm_in else {}
    return pl.pallas_call(
        kernel,
        out_shape=[jax.ShapeDtypeStruct(*(s if isinstance(s[0], tuple) else (s, F32))) for s in outs],
        out_specs=specs(len(outs), hbm_out),
        scratch_shapes=[pltpu.VMEM(*(s if isinstance(s[0], tuple) else (s, F32))) for s in scratch]
        + ([pltpu.SemaphoreType.DMA((sems,))] if sems else []),
        compiler_params=pltpu.CompilerParams(vmem_limit_bytes=12 * 1024 * 1024),
        cost_estimate=cost,
        input_output_aliases=in_place or {},
        **more,
    )


def swapped(x, far):
    size = lax.axis_size(AXES)
    return lax.ppermute(x, AXES, [(i, (i + (1 if (i % 2 == 0) != far else -1)) % size) for i in range(size)])


def everyone(payload, shape):
    devices = lax.axis_size(AXES)
    return lax.all_to_all(payload.reshape((devices,) + shape), AXES, 0, 0, tiled=True).reshape(-1, 128)


def per_device(forcing, kappa, elem_order):
    devices = lax.axis_size(AXES)
    nodes, face, face_row = (2, 512, 128), (2, 56, 128), (2, 64, 128)
    plane, grid, flat = (8, PLANE), (devices, PLANE), (512, PLANE)
    edge, stored, choice = (2, 128, 128), (PLANE, 512), ((PLANE, PLANE), jnp.bfloat16)
    table = jnp.asarray(np.stack(STIFF_PARTS), jnp.bfloat16)
    long = pl.CostEstimate(flops=10**11, bytes_accessed=2**28, transcendentals=0)
    payload_rows = (devices * 6, 128)
    load, far, near, own, payload = call(
        opening,
        [nodes, face_row, face_row, plane, payload_rows],
        [(2, PLANE, 256), (1, PLANE), ((1, PLANE), jnp.int32), payload_rows],
        5,
        hbm_in=(0, 1, 2),
        hbm_out=(4,),
        inputs=3,
    )(*(pltpu.with_memory_space_constraint(x, pltpu.HBM) for x in (forcing, kappa.reshape(1, PLANE), elem_order)))
    far, near = swapped(far, True), swapped(near, False)
    (payload,) = call(
        late_payload, [payload_rows], [payload_rows], 1, in_place={2: 0}, hbm_in=(2,), hbm_out=(0,), inputs=3
    )(load, own, payload)
    gather = everyone(payload, (3, 2, 128))
    resid, scaled, image, layers, lower, far, near = call(
        first_faces, [nodes, nodes, nodes, plane, plane, face_row, face_row], [flat], cost=long, in_place={0: 0}
    )(load, far, near, own, table)
    far, near = swapped(far, True), swapped(near, False)
    vert, target, scale, coeff, smooth = call(first_coarse, [grid] * 4 + [nodes], [edge])(gather, layers)
    scaled_change, change, sums, planes, column_planes, outer = call(
        second_rough, [nodes] * 2 + [(48, PLANE), plane, (128, PLANE), (128, PLANE)], [flat, nodes], in_place={1: 0}
    )(image, smooth, layers, table, resid, scaled)
    added, next_far, next_near, payload = call(
        second_faces, [(128, PLANE), face, face, (devices * 7, 128)], [edge, (64, 2 * PLANE)]
    )(image, scaled_change, change, outer, far, near, layers, table, scaled, lower, sums, planes, column_planes)
    step = everyone(payload, (7, 1, 128))
    next_far, next_near = swapped(next_far, True), swapped(next_near, False)
    image, scaled_change, change, choose, applied, first_modes = call(
        complete, [nodes] * 3 + [choice, grid, (24, PLANE)], [(2, 256, 128)], in_place={0: 0, 1: 1, 2: 2}
    )(image, scaled_change, change, far, near, added, layers, coeff, vert)
    modes, scalars = call(second_coarse, [(24, PLANE), (8, 128)], [grid])(
        coeff, step, vert, applied, target, scale, first_modes
    )
    found, left = call(closing, [stored, stored], [flat, nodes, edge, (2,) + stored], 3, hbm_out=(0, 1))(
        resid, scaled, image, scaled_change, change, next_far, next_near, modes, layers, scalars, choose
    )
    return found, left


def solution(mesh):
    in_specs = (P(AXES, None), P(AXES), P(AXES, None))
    out_specs = (P(AXES, None), P(AXES, None))
    return jax.shard_map(
        per_device, mesh=mesh, in_specs=in_specs, out_specs=out_specs, check_vma=False
    )
```

```python
import functools
import math

import jax
import jax.numpy as jnp
import ml_dtypes
import numpy as np
from jax import lax
from jax.experimental import pallas as pl
from jax.experimental.pallas import tpu as pltpu
from jax.sharding import PartitionSpec as P

EX = 8
EY = 32
PLANE = EX * EY
SWEEPS = 4
REACT = 0.02
OMEGA = 0.6
AXES = ("elem", "face")
F32 = jnp.float32


def legendre_seven(points):
    before = np.ones(8)
    current = np.array(points)
    for degree in range(1, 7):
        following = ((2 * degree + 1) * points * current - degree * before) / (degree + 1)
        before = current
        current = following
    return current


def line_tables():
    points = np.array(
        [
            -1.0,
            -0.8717401485096066,
            -0.5917001814331423,
            -0.2092992179024789,
            0.2092992179024789,
            0.5917001814331423,
            0.8717401485096066,
            1.0,
        ]
    )
    weights = np.array(
        [
            1.0 / 28.0,
            0.2107042271435061,
            0.3411226924835044,
            0.4124587946587038,
            0.4124587946587038,
            0.3411226924835044,
            0.2107042271435061,
            1.0 / 28.0,
        ]
    )
    legendre = legendre_seven(points)
    derivative = np.zeros((8, 8))
    for left_node in range(8):
        for right_node in range(8):
            if left_node != right_node:
                derivative[left_node, right_node] = legendre[left_node] / (
                    legendre[right_node] * (points[left_node] - points[right_node])
                )
    derivative[0, 0] = -14.0
    derivative[7, 7] = 14.0
    stiffness = derivative.T @ (weights[:, None] * derivative)
    return points, weights, stiffness


POINTS, WEIGHTS, STIFF = line_tables()
DIAG = np.diag(STIFF)
ENDS = np.array([2.0] + [1.0] * 6 + [2.0])
MASS = np.diag(WEIGHTS)
STIFF_XY = np.kron(MASS, STIFF) + np.kron(STIFF, MASS)
STIFF_PARTS = []
for part in range(3):
    STIFF_PARTS.append((STIFF_XY - sum(STIFF_PARTS)).astype(ml_dtypes.bfloat16).astype(np.float64))
INTERP = np.stack([(1.0 - POINTS) / 2.0, (1.0 + POINTS) / 2.0], 1)
LINE_MASS = INTERP.T @ (WEIGHTS[:, None] * INTERP)
LINE_STIFF = INTERP.T @ STIFF @ INTERP
MASS_SUM = (LINE_MASS[0, 0] + LINE_MASS[0, 1]) / 2.0
MASS_DIF = (LINE_MASS[0, 0] - LINE_MASS[0, 1]) / 2.0
STIFF_DIF = LINE_STIFF[0, 0]
MODE_STIFF = [
    0.0,
    STIFF_DIF * MASS_SUM**2,
    2.0 * STIFF_DIF * MASS_DIF * MASS_SUM,
    3.0 * STIFF_DIF * MASS_DIF**2,
]
MODE_MASS = [MASS_SUM ** (3 - j) * MASS_DIF**j for j in range(4)]
CORNER_STIFF = 3.0 * LINE_STIFF[0, 0] * LINE_MASS[0, 0] ** 2
CORNER_MASS = LINE_MASS[0, 0] ** 3


def lane(shape):
    return lax.broadcasted_iota(jnp.int32, shape, len(shape) - 1)


def next_x(v):
    return jnp.where(lane(v.shape) % EX == EX - 1, pltpu.roll(v, EX - 1, 1), pltpu.roll(v, PLANE - 1, 1))


def prev_x(v):
    return jnp.where(lane(v.shape) % EX == 0, pltpu.roll(v, PLANE - EX + 1, 1), pltpu.roll(v, 1, 1))


def next_y(v):
    return pltpu.roll(v, PLANE - EX, 1)


def prev_y(v):
    return pltpu.roll(v, EX, 1)


def next_xy(v):
    return jnp.where(lane(v.shape) % EX == EX - 1, pltpu.roll(v, PLANE - 1, 1), pltpu.roll(v, PLANE - EX - 1, 1))


def prev_xy(v):
    return jnp.where(lane(v.shape) % EX == 0, pltpu.roll(v, 1, 1), pltpu.roll(v, EX + 1, 1))


def next_z(v):
    half = v.shape[0] // 2
    return jnp.concatenate([v[half:], pltpu.roll(v[:half], half - 1, 0)], axis=0)


def prev_z(v):
    half = v.shape[0] // 2
    return jnp.concatenate([pltpu.roll(v[half:], 1, 0), v[:half]], axis=0)


def plane_row(layer, planes):
    layer = lax.rem(layer + planes, planes)
    return pl.ds(lax.div(layer, 2) + lax.rem(layer, 2) * (planes // 2), 1)


def column(values):
    row = lax.broadcasted_iota(jnp.int32, (8, PLANE), 0)
    out = jnp.full((8, PLANE), float(values[0]), F32)
    for k in range(1, 8):
        out = jnp.where(row == k, float(values[k]), out)
    return out


def rows_of(nz, ny):
    start = (nz * 8 + ny) * 8
    return slice(start, start + 8)


def get(ref, rows):
    return jnp.concatenate([ref[0, rows, :], ref[1, rows, :]], axis=1)


def put(ref, rows, value):
    ref[0, rows, :] = value[:, :128]
    ref[1, rows, :] = value[:, 128:]


def sum_xy(ref):
    planes = ref.shape[1] // 64
    first, last = pl.ds(0, planes * 8, stride=8), pl.ds(7, planes * 8, stride=8)
    shared = get(ref, last) + next_x(get(ref, first))
    put(ref, last, shared)
    put(ref, first, prev_x(shared))
    for nz in range(planes):
        shared = get(ref, rows_of(nz, 7)) + next_y(get(ref, rows_of(nz, 0)))
        put(ref, rows_of(nz, 7), shared)
        put(ref, rows_of(nz, 0), prev_y(shared))


def restrict(ref, points):
    sums_z, difs_z = [], []
    for ny in range(8):
        tiles = [get(ref, rows_of(nz, ny)) for nz in range(8)]
        sums_z.append(functools.reduce(lambda a, b: a + b, tiles))
        difs_z.append(sum(float(POINTS[7 - k]) * (tiles[7 - k] - tiles[k]) for k in range(4)))
    return restrict_xy(sums_z, difs_z, points)


def restrict_summed(ref, points):
    inv_ends = column(1.0 / ENDS)
    sums_z, difs_z = [], []
    for ny in range(8):
        tiles = [get(ref, rows_of(nz, ny)) for nz in range(8)]
        share = inv_ends * float(1.0 / ENDS[ny])
        sums_z.append(functools.reduce(lambda a, b: a + b, tiles) * share)
        difs_z.append(sum(float(POINTS[7 - k]) * (tiles[7 - k] - tiles[k]) for k in range(4)) * share)
    return restrict_xy(sums_z, difs_z, points)


def restrict_xy(sums_z, difs_z, points):
    planes = []
    for parts in (sums_z, difs_z):
        total = functools.reduce(lambda a, b: a + b, parts)
        slope = sum(float(POINTS[7 - k]) * (parts[7 - k] - parts[k]) for k in range(4))
        in_y = []
        for part in (total, slope):
            flat = jnp.sum(part, axis=0, keepdims=True)
            steep = jnp.sum(part * points, axis=0, keepdims=True)
            in_y.append((flat - steep) + prev_x(flat + steep))
        planes.append((in_y[0] - in_y[1]) + prev_y(in_y[0] + in_y[1]))
    return (planes[0] - planes[1]) * 0.125, (planes[0] + planes[1]) * 0.125


def both(v, following):
    after = following(v)
    return after + v, after - v


def both_back(total, dif, preceding):
    return (total - dif) + preceding(total + dif)


def coarse_modes(coeff):
    return [float(REACT * MODE_MASS[0])] + [
        float(MODE_STIFF[j]) * coeff + float(REACT * MODE_MASS[j]) for j in range(1, 4)
    ]


def coarse_tables(coeff):
    near = coeff + prev_x(coeff)
    near = near + prev_y(near)
    near = near + prev_z(near)
    scale = float(OMEGA) / (float(CORNER_STIFF) * near + float(8.0 * REACT * CORNER_MASS))
    return coarse_modes(coeff), scale


def coarse_apply(vert, modes):
    after_x, after_y, after_xy = next_x(vert), next_y(vert), next_xy(vert)
    in_x = [(after_x + vert, after_xy + after_y), (after_x - vert, after_xy - after_y)]
    back = []
    for jx in range(2):
        first, second = in_x[jx]
        for jy, in_y in enumerate((second + first, second - first)):
            in_z = both(in_y, next_z)
            scaled = [modes[jx + jy + jz] * in_z[jz] for jz in range(2)]
            back.append(both_back(scaled[0], scaled[1], prev_z))
    ss, sd, ds, dd = back
    low, high = (ss - sd, ss + sd), (ds - dd, ds + dd)
    return ((low[0] - high[0]) + prev_x(low[0] + high[0])) + (prev_y(low[1] - high[1]) + prev_xy(low[1] + high[1]))


def coarse_solve(target, modes, scale):
    vert = scale * target
    for _ in range(SWEEPS - 1):
        vert = vert + scale * (target - coarse_apply(vert, modes))
    return vert


def gathered_rows(ref, row, size):
    chips = ref.shape[0] // (2 * size)
    return jnp.concatenate([ref[pl.ds(core * size + row, chips, stride=2 * size), :] for core in range(2)], axis=0)


def gathered(ref, k, size):
    return jnp.concatenate([gathered_rows(ref, 2 * k + h, size) for h in range(2)], axis=1)


def halves(row):
    return [row[:, :128], row[:, 128:]]


def send(ref, rows):
    count = len(rows)
    times = 8 // math.gcd(count, 8)
    block = jnp.concatenate(rows * times, axis=0)
    for k in range(0, ref.shape[0], count * times):
        ref[k : k + count * times, :] = block


def layer_modes(vert_ref, shift):
    me, devices = my_layer(), vert_ref.shape[0]
    lower, upper = (vert_ref[plane_row(me + shift + k, devices), :] for k in range(2))
    modes = []
    for along_z in (upper + lower, upper - lower):
        for along_y in both(along_z, next_y):
            modes += both(along_y, next_x)
    return 0.125 * jnp.concatenate(modes, axis=0)


class Smooth:
    def __init__(self, modes, coeff, points, weight_x):
        row = lax.broadcasted_iota(jnp.int32, (8, PLANE), 0)
        ends = jnp.where(row == 0, -1.0, jnp.where(row == 7, 1.0, 0.0))
        m = [[[modes[4 * z + 2 * y + x : 4 * z + 2 * y + x + 1] for x in range(2)] for y in range(2)] for z in range(2)]
        self.xy = [[m[z][y][0] + m[z][y][1] * points for y in range(2)] for z in range(2)]
        self.dx = [[m[z][y][1] for y in range(2)] for z in range(2)]
        self.ends_coeff = ends * coeff
        self.weight_coeff = weight_x * coeff
        self.mass = float(REACT) * weight_x

    def value(self, nz, ny):
        by_y = [self.xy[z][0] + float(POINTS[ny]) * self.xy[z][1] for z in range(2)]
        return by_y[0] + float(POINTS[nz]) * by_y[1]

    def operated(self, nz, ny, value):
        wy, wz, py, pz = (float(t) for t in (WEIGHTS[ny], WEIGHTS[nz], POINTS[ny], POINTS[nz]))
        slope = (self.dx[0][0] + py * self.dx[0][1]) + pz * (self.dx[1][0] + py * self.dx[1][1])
        out = self.ends_coeff * (slope * (wy * wz)) + (self.mass * (wy * wz)) * value
        flux = None
        if ny in (0, 7):
            flux = (self.xy[0][1] + pz * self.xy[1][1]) * (wz * py)
        if nz in (0, 7):
            along = (self.xy[1][0] + py * self.xy[1][1]) * (wy * pz)
            flux = along if flux is None else flux + along
        return out if flux is None else out + self.weight_coeff * flux


def kappa_sums(own, below, above):
    row = lax.broadcasted_iota(jnp.int32, (8, PLANE), 0)
    table = []
    for along_z in (own + below, own, own + above):
        in_z = []
        for along_y in (along_z + prev_y(along_z), along_z, along_z + next_y(along_z)):
            first = along_y + prev_x(along_y)
            last = along_y + next_x(along_y)
            in_z.append(jnp.where(row == 0, first, jnp.where(row == 7, last, along_y)))
        table.append(in_z)
    return table


def kind(node):
    return 0 if node == 0 else (2 if node == 7 else 1)


def product(table, values):
    low, middle, high = pieces(values)
    stacked = jnp.concatenate([high, middle, high, middle, low, high], axis=0)
    return jnp.dot(table, stacked, preferred_element_type=F32)


def operate(z_ref, xy_ref, out_ref, table_ref, coeff, weight_x):
    for nz in range(8):
        rows = slice(64 * nz, 64 * nz + 64)
        xy_ref[rows, :] = product(table_ref[...], get(z_ref, rows))
    for ny in range(8):
        tiles = [get(z_ref, rows_of(nz, ny)) for nz in range(8)]
        even = [tiles[k] + tiles[7 - k] for k in range(4)]
        odd = [tiles[k] - tiles[7 - k] for k in range(4)]
        for nz in range(4):
            even_part = sum(float((STIFF[nz, k] + STIFF[nz, 7 - k]) / 2) * even[k] for k in range(4))
            odd_part = sum(float((STIFF[nz, k] - STIFF[nz, 7 - k]) / 2) * odd[k] for k in range(4))
            for node, term in ((nz, even_part + odd_part), (7 - nz, even_part - odd_part)):
                area = weight_x * float(WEIGHTS[ny])
                local = coeff * (
                    float(WEIGHTS[node]) * xy_ref[rows_of(node, ny), :] + area * term
                ) + (float(REACT * WEIGHTS[node]) * area) * tiles[node]
                put(out_ref, rows_of(node, ny), local)


def fine_diag(sums, nz, ny, weight_x, diag_x, ends_x):
    wy, wz, ky, kz = (float(t) for t in (WEIGHTS[ny], WEIGHTS[nz], DIAG[ny], DIAG[nz]))
    stiff = diag_x * (wy * wz) + weight_x * (ky * wz + wy * kz)
    mass = (weight_x * ends_x) * float(REACT * wy * wz * ENDS[ny] * ENDS[nz])
    return sums[kind(nz)][kind(ny)] * stiff + mass


def my_layer():
    return lax.axis_index("elem") * lax.axis_size("face") + lax.axis_index("face")


def face_rows(ref):
    even = lax.rem(my_layer(), 2) == 0
    last = ref.shape[1] - 64
    near = pl.multiple_of(jnp.where(even, last, 0), 64)
    far = pl.multiple_of(jnp.where(even, 0, last), 64)
    return pl.ds(near, 64), pl.ds(far, 64)


def faces_out(ref, near_ref, far_ref):
    for rows, out_ref in zip(face_rows(ref), (near_ref, far_ref)):
        out_ref[:, 0:56, :] = ref[:, pl.ds(rows.start, 56), :]


def face_in(ref):
    return jnp.concatenate([get(ref, slice(0, 56)), next_y(get(ref, slice(0, 8)))], axis=0)


def faces_in(ref, near_ref, far_ref):
    for rows, in_ref in zip(face_rows(ref), (near_ref, far_ref)):
        put(ref, rows, get(ref, rows) + face_in(in_ref))


def columns_of_nodes():
    return column(POINTS), column(WEIGHTS), column(DIAG), column(ENDS)


def pieces(v):
    high = v.astype(jnp.bfloat16)
    rest = v - high.astype(F32)
    middle = rest.astype(jnp.bfloat16)
    low = (rest - middle.astype(F32)).astype(jnp.bfloat16)
    return low, middle, high


def selection(order):
    place = lax.broadcasted_iota(jnp.int32, (PLANE, PLANE), 0).astype(order.dtype)
    return jnp.where(place == order, 1.0, 0.0).astype(jnp.bfloat16)


def opening(
    forcing_ref, kappa_ref, order_ref, load_ref, far_ref, near_ref, own_ref, payload_ref,
    held, held_kappa, held_order, held_payload, sems,
):
    small = [
        pltpu.make_async_copy(order_ref, held_order, sems.at[0]),
        pltpu.make_async_copy(kappa_ref, held_kappa, sems.at[1]),
    ]
    parts = [
        pltpu.make_async_copy(forcing_ref.at[:, pl.ds(256 * k, 256)], held.at[k], sems.at[2 + k]) for k in range(2)
    ]
    for copy in small + parts:
        copy.start()
    for copy in small:
        copy.wait()
    order = held_order[...]
    choose = selection(order)
    coeff = jnp.zeros((8, PLANE), F32)
    for piece in pieces(jnp.broadcast_to(held_kappa[...], (8, PLANE))):
        coeff = coeff + lax.dot_general(piece, choose, (((1,), (1,)), ((), ())), preferred_element_type=F32)
    own = jnp.concatenate([coeff[0:3], order.astype(F32), coeff[4:8]], axis=0)
    own_ref[...] = own
    for k, copy in enumerate(parts):
        copy.wait()
        load = jnp.zeros((PLANE, 256), F32)
        for piece in pieces(held[k]):
            load = load + jnp.dot(choose, piece, preferred_element_type=F32)
        put(load_ref, slice(256 * k, 256 * k + 256), load.T)
    sum_xy(load_ref)
    faces_out(load_ref, near_ref, far_ref)
    put(near_ref, slice(56, 64), own)
    put(far_ref, slice(56, 64), own)


    @pl.when(starts_early())
    def _():
        write_payload(load_ref, own_ref, payload_ref, held_payload, sems.at[4])


def starts_early():
    return my_layer() < lax.axis_size("elem") * lax.axis_size("face") // 2


def write_payload(load_ref, own_ref, payload_ref, held, sem):
    lower, upper = restrict_summed(load_ref, column(POINTS))
    send(held, halves(lower) + halves(upper) + halves(own_ref[0:1, :]))
    copy = pltpu.make_async_copy(held, payload_ref, sem)
    copy.start()
    copy.wait()


def late_payload(load_ref, own_ref, _, payload_ref, held, sems):
    @pl.when(jnp.logical_not(starts_early()))
    def _():
        write_payload(load_ref, own_ref, payload_ref, held, sems.at[0])


def below_above(near, far):
    even = lax.rem(my_layer(), 2) == 0
    return jnp.where(even, far, near), jnp.where(even, near, far)


def row_after_face(ref):
    return get(ref, slice(56, 64))[0:1]


def first_faces(
    load_ref, far_in_ref, near_in_ref, own_ref, table_ref,
    resid_ref, scaled_ref, image_ref, layers_ref, lower_ref, far_ref, near_ref, xy_ref,
):
    points, weight_x, _, _ = columns_of_nodes()
    own = own_ref[0:1, :]
    below, above = below_above(row_after_face(near_in_ref), row_after_face(far_in_ref))
    layers_ref[...] = jnp.concatenate([own, below, above, own_ref[3:8, :]], axis=0)
    resid_ref[...] = load_ref[...]
    faces_in(resid_ref, near_in_ref, far_in_ref)
    over_diag(functools.partial(get, resid_ref), scaled_ref, layers_ref)
    operate(scaled_ref, xy_ref, image_ref, table_ref, own, weight_x)
    lower, upper = restrict(image_ref, points)
    sum_xy(image_ref)
    faces_out(image_ref, near_ref, far_ref)
    lower_ref[...] = jnp.broadcast_to(lower, lower_ref.shape)
    put(near_ref, slice(56, 64), jnp.broadcast_to(upper, (8, PLANE)))
    put(far_ref, slice(56, 64), jnp.broadcast_to(upper, (8, PLANE)))


def over_diag(resid, scaled_ref, layers_ref):
    _, weight_x, diag_x, ends_x = columns_of_nodes()
    sums = kappa_sums(*(layers_ref[k : k + 1, :] for k in range(3)))
    for nz in range(8):
        for ny in range(8):
            rows = rows_of(nz, ny)
            put(scaled_ref, rows, resid(rows) / fine_diag(sums, nz, ny, weight_x, diag_x, ends_x))


def three_modes(vert_ref):
    return jnp.concatenate([layer_modes(vert_ref, shift) for shift in (0, -1, 1)], axis=0)


def smooths_of(modes, layers_ref):
    points, weight_x, _, _ = columns_of_nodes()
    return [Smooth(modes[8 * k : 8 * k + 8], layers_ref[k : k + 1, :], points, weight_x) for k in range(3)]


def smooth_image(smooths, out_ref, edge_ref):
    own, below, above = smooths
    for nz in range(8):
        for ny in range(8):
            put(out_ref, rows_of(nz, ny), own.operated(nz, ny, own.value(nz, ny)))
    sum_xy(out_ref)
    for plane, (smooth, nz) in enumerate(((below, 7), (above, 0))):
        for ny in range(8):
            put(edge_ref, rows_of(plane, ny), smooth.operated(nz, ny, smooth.value(nz, ny)))
    sum_xy(edge_ref)
    out_ref[:, 0:64, :] += edge_ref[:, 0:64, :]
    out_ref[:, 448:512, :] += edge_ref[:, 64:128, :]


def first_coarse(coarse_ref, layers_ref, vert_ref, target_ref, scale_ref, coeff_ref, smooth_ref, edge_ref):
    coeff = gathered(coarse_ref, 2, 6)
    coeff_ref[...] = coeff
    modes, scale = coarse_tables(coeff)
    target = gathered(coarse_ref, 0, 6) + prev_z(gathered(coarse_ref, 1, 6))
    vert = coarse_solve(target, modes, scale)
    vert_ref[...] = vert
    target_ref[...] = target
    scale_ref[...] = scale
    smooth_image(smooths_of(three_modes(vert_ref), layers_ref), smooth_ref, edge_ref)


def pack(sums):
    place = lane((8, 128)) // 16
    packed = jnp.zeros((8, 128), F32)
    for k, total in enumerate(sums):
        total = total[:, :128] + total[:, 128:]
        for by in (64, 32, 16):
            total = total + pltpu.roll(total, by, 1)
        packed = jnp.where(place == k, total, packed)
    return jnp.sum(packed, axis=0, keepdims=True)


def second_rough(
    image_ref, smooth_ref, layers_ref, table_ref, resid_ref, scaled_ref,
    scaled_change_ref, change_ref, sums_ref, planes_ref, column_ref, outer_ref, xy_ref, whole_ref,
):
    points, weight_x, _, _ = columns_of_nodes()
    inv_ends = column(1.0 / ENDS)
    whole_ref[...] = image_ref[...] + smooth_ref[...]
    over_diag(functools.partial(get, whole_ref), scaled_change_ref, layers_ref)
    operate(scaled_change_ref, xy_ref, change_ref, table_ref, layers_ref[0:1, :], weight_x)
    planes_ref[...] = jnp.concatenate(list(restrict(change_ref, points)) * 4, axis=0)
    sum_xy(change_ref)
    sums = [jnp.zeros((8, PLANE), F32)] * 6
    for ny in range(8):
        along = [jnp.zeros((8, PLANE), F32)] * 2
        for nz in range(8):
            rows = rows_of(nz, ny)
            share = float(1.0 / (ENDS[nz] * ENDS[ny]))
            scaled, change = get(scaled_ref, rows) * share, get(scaled_change_ref, rows)
            along = [total + float(STIFF[nz, node]) * change for total, node in zip(along, (0, 7))]
            change = change * share
            whole, image = get(whole_ref, rows), get(image_ref, rows)
            terms = [
                scaled * get(resid_ref, rows), scaled * whole, change * whole, scaled * image, change * image,
                change * (get(change_ref, rows) * float(ENDS[nz])),
            ]
            sums = [total + term for total, term in zip(sums, terms)]
        for k in range(2):
            column_ref[64 * k + 8 * ny : 64 * k + 8 * ny + 8, :] = along[k]
    sums_ref[...] = jnp.concatenate([total * inv_ends for total in sums], axis=0)
    for k, rows in enumerate((slice(0, 64), slice(448, 512))):
        outer_ref[64 * k : 64 * k + 64, :] = get(whole_ref, rows)


def second_faces(
    image_ref, scaled_change_ref, change_ref, outer_ref, far_in_ref, near_in_ref, layers_ref, table_ref,
    scaled_ref, lower_ref, sums_ref, planes_ref, column_ref,
    added_ref, far_ref, near_ref, payload_ref, edge_ref, xy_ref,
):
    points, weight_x, _, _ = columns_of_nodes()
    inv_ends = column(1.0 / ENDS)
    even = lax.rem(my_layer(), 2) == 0
    own = layers_ref[0:1, :]
    kappas = kappa_sums(*(layers_ref[k : k + 1, :] for k in range(3)))
    faces = below_above(face_in(near_in_ref), face_in(far_in_ref))
    tiles = [slice(8 * ny, 8 * ny + 8) for ny in range(8)]
    added = added_by(faces, kappas, columns_of_nodes())
    xy_ref[...] = product(table_ref[...], jnp.concatenate(added, axis=1))
    along, at_face = [], []
    for k in range(2):
        along.append(local_along(own, weight_x, added[k]))
        flux = own * xy_ref[:, PLANE * k : PLANE * k + PLANE]
        at_face.append(float(WEIGHTS[0]) * jnp.concatenate(
            [flux[t] + (float(REACT * WEIGHTS[ny]) * weight_x) * added[k][t] for ny, t in enumerate(tiles)], axis=0
        ))
    local = [
        (float(STIFF[nz, 0]) * along[0] + float(STIFF[nz, 7]) * along[1]) + at_face[k] for k, nz in enumerate((0, 7))
    ]
    flat = at_face[0] + at_face[1]
    slope = (along[1] + at_face[1]) - (along[0] + at_face[0])
    lower, upper = restrict_xy([flat[t] for t in tiles], [slope[t] for t in tiles], points)
    lower, upper = lower + planes_ref[0:1, :], upper + planes_ref[1:2, :]
    sums = [jnp.zeros((8, PLANE), F32)] * 5
    energy = jnp.zeros((8, PLANE), F32)
    planes = [slice(0, 64), slice(448, 512)]
    for k in range(2):
        s_plane, q_plane, i_plane, c_plane = (
            get(ref, planes[k]) for ref in (scaled_ref, scaled_change_ref, image_ref, change_ref)
        )
        w_plane = outer_ref[64 * k : 64 * k + 64, :]
        for ny in range(8):
            tile = tiles[ny]
            share = float(1.0 / ENDS[ny])
            half = share * float(1.0 / ENDS[0])
            face = faces[k][tile]
            s, q, dq = s_plane[tile] * half, q_plane[tile] * half, added[k][tile] * half
            sums[0] = sums[0] + s * face
            sums[1] = sums[1] + (q * face + dq * (w_plane[tile] + face))
            sums[2] = sums[2] + s * face
            sums[3] = sums[3] + (q * face + dq * (i_plane[tile] + face))
            sums[4] = sums[4] + (added[k][tile] * c_plane[tile]) * share
            energy = energy + (
                column_ref[64 * k + 8 * ny : 64 * k + 8 * ny + 8, :] * along[k][tile]
                + q_plane[tile] * at_face[k][tile]
                + added[k][tile] * local[k][tile]
            )
    sums = [sums_ref[8 * k + 8 : 8 * k + 16, :] + sums[k] * inv_ends for k in range(5)]
    sums = pack([sums_ref[0:8, :]] + sums[:4] + [sums[4] + energy])
    below, _ = below_above(row_after_face(near_in_ref), row_after_face(far_in_ref))
    send(payload_ref, halves(lower_ref[0:1, :] + below) + halves(lower) + halves(upper) + [sums])
    for k in range(2):
        put(edge_ref, slice(64 * k, 64 * k + 64), local[k])
        added_ref[64 * k : 64 * k + 64, :] = at_face[k]
    sum_xy(edge_ref)
    change = [(get(change_ref, planes[k]) + get(edge_ref, slice(64 * k, 64 * k + 64)))[0:56] for k in range(2)]
    put(far_ref, slice(0, 56), jnp.where(even, change[0], change[1]))
    put(near_ref, slice(0, 56), jnp.where(even, change[1], change[0]))


def local_along(own, weight_x, added):
    return own * jnp.concatenate(
        [(weight_x * float(WEIGHTS[ny])) * added[8 * ny : 8 * ny + 8] for ny in range(8)], axis=0
    )


def added_by(faces, kappas, columns):
    _, weight_x, diag_x, ends_x = columns
    return [
        jnp.concatenate(
            [
                face[8 * ny : 8 * ny + 8] / fine_diag(kappas, nz, ny, weight_x, diag_x, ends_x)
                for ny in range(8)
            ],
            axis=0,
        )
        for nz, face in zip((0, 7), faces)
    ]


def complete(
    first_ref, first_scaled_ref, first_change_ref, far_in_ref, near_in_ref, at_face_ref, layers_ref, coeff_ref, vert_ref,
    image_ref, scaled_change_ref, change_ref, choose_ref, applied_ref, modes_ref, edge_ref,
):
    columns = columns_of_nodes()
    applied_ref[...] = coarse_apply(vert_ref[...], coarse_modes(coeff_ref[...]))
    modes_ref[...] = three_modes(vert_ref)
    choose_ref[...] = selection(layers_ref[3:4, :]).astype(F32).T.astype(jnp.bfloat16)
    image_ref[...] = first_ref[...]
    scaled_change_ref[...] = first_scaled_ref[...]
    faces_in(image_ref, near_in_ref, far_in_ref)
    kappas = kappa_sums(*(layers_ref[k : k + 1, :] for k in range(3)))
    added = added_by(below_above(face_in(near_in_ref), face_in(far_in_ref)), kappas, columns)
    for k, rows in enumerate((slice(0, 64), slice(448, 512))):
        put(scaled_change_ref, rows, get(scaled_change_ref, rows) + added[k])
        put(edge_ref, slice(64 * k, 64 * k + 64), local_along(layers_ref[0:1, :], columns[1], added[k]))
        put(edge_ref, slice(128 + 64 * k, 192 + 64 * k), at_face_ref[64 * k : 64 * k + 64, :])
    sum_xy(edge_ref)
    along = [get(edge_ref, slice(64 * k, 64 * k + 64)) for k in range(2)]
    for nz in range(8):
        rows = slice(64 * nz, 64 * nz + 64)
        new = get(first_change_ref, rows) + (float(STIFF[nz, 0]) * along[0] + float(STIFF[nz, 7]) * along[1])
        if nz in (0, 7):
            new = new + get(edge_ref, slice(128 + 64 * (nz // 7), 192 + 64 * (nz // 7)))
        put(change_ref, rows, new)


def folded(value):
    return functools.reduce(lambda a, b: a + b, [value[k : k + 8] for k in range(0, value.shape[0], 8)])


def second_coarse(
    coeff_ref, step_ref, first_ref, applied_ref, target_ref, scale_ref, first_modes_ref, modes_ref, scalars_ref, vert_ref
):
    modes = coarse_modes(coeff_ref[...])
    target, first, applied = target_ref[...], first_ref[...], applied_ref[...]
    rough, rough_change = gathered(step_ref, 0, 7), gathered(step_ref, 1, 7) + prev_z(gathered(step_ref, 2, 7))
    parts = folded(gathered_rows(step_ref, 6, 7))
    sums = [parts] + [pltpu.roll(parts, 128 - 16 * k, 1) for k in range(1, 6)]
    used = lane(parts.shape) < 16

    def total(fine, coarse):
        coarse = folded(coarse)
        return jnp.sum(jnp.where(used, fine, 0.0) + (coarse[:, :128] + coarse[:, 128:]), keepdims=True)

    image = rough + applied
    change = coarse_solve(image, modes, scale_ref[...])
    vert_ref[...] = change
    change_modes = three_modes(vert_ref)
    change_applied = coarse_apply(change, modes)
    gamma = total(sums[0], target * first)
    energy = total(sums[3], first * (2.0 * rough + applied))
    alpha = gamma / energy
    vert = first - alpha * change
    progress = total(sums[0] - alpha * (2.0 * sums[1] - alpha * sums[2]), (target - alpha * image) * vert)
    second = total(
        sums[3] - alpha * (2.0 * sums[4] - alpha * sums[5]),
        vert * (2.0 * (rough - alpha * rough_change) + (applied - alpha * change_applied)),
    )
    cross = total(sums[1] - alpha * sums[2], vert * image)
    beta = progress / gamma
    alpha_next = progress / (second + beta * (2.0 * cross + beta * energy))
    scalars = [alpha + alpha_next * beta + alpha_next, alpha_next * alpha]
    modes_ref[...] = scalars[0] * first_modes_ref[...] - scalars[1] * change_modes
    scalars_ref[...] = jnp.concatenate([jnp.broadcast_to(t, (1, 128)) for t in scalars * 4], axis=0)


def to_stored(choose, value):
    total = jnp.zeros((choose.shape[0], value.shape[0]), F32)
    for piece in pieces(value)[1:]:
        total = total + lax.dot_general(choose, piece, (((1,), (1,)), ((), ())), preferred_element_type=F32)
    return total


def combine(
    first_scaled_ref, first_resid_ref, scaled_change_ref, image_ref, change_ref, modes_ref, layers_ref, scalars_ref,
    found_ref, rest_ref, smooth_ref, edge_ref,
):
    smooths = smooths_of(modes_ref[...], layers_ref)
    first, second = scalars_ref[0:1, 0:1], scalars_ref[1:2, 0:1]
    smooth_image(smooths, smooth_ref, edge_ref)
    for nz in range(8):
        for ny in range(8):
            rows = rows_of(nz, ny)
            rough = first * get(first_scaled_ref, rows) - second * get(scaled_change_ref, rows)
            put(found_ref, rows, rough + smooths[0].value(nz, ny))
    first, second = first[None], second[None]
    rest_ref[...] = first_resid_ref[...] - first * image_ref[...] + second * change_ref[...] - smooth_ref[...]


def closing(
    found_ref, rest_ref, far_ref, near_ref, scalars_ref, choose_ref, solution_ref, residual_ref, sum_ref, held, sems
):
    choose, every = choose_ref[...], slice(0, 512)
    second = scalars_ref[1:2, 0:1]
    sum_ref[...] = rest_ref[...]
    for rows, ref in zip(face_rows(sum_ref), (near_ref, far_ref)):
        put(sum_ref, rows, get(sum_ref, rows) + second * face_in(ref))
    copies = []
    for k, (ref, out_ref) in enumerate(((found_ref, solution_ref), (sum_ref, residual_ref))):
        held[k] = to_stored(choose, get(ref, every))
        copies.append(pltpu.make_async_copy(held.at[k], out_ref, sems.at[k]))
        copies[-1].start()
    for copy in copies:
        copy.wait()


def call(kernel, outs, scratch=(), sems=0, cost=None, in_place=None, hbm_in=(), hbm_out=(), inputs=0):
    def specs(count, far):
        return [pl.BlockSpec(memory_space=pltpu.HBM if k in far else pltpu.VMEM) for k in range(count)]

    more = {"in_specs": specs(inputs, hbm_in)} if hbm_in else {}
    return pl.pallas_call(
        kernel,
        out_shape=[jax.ShapeDtypeStruct(*(s if isinstance(s[0], tuple) else (s, F32))) for s in outs],
        out_specs=specs(len(outs), hbm_out),
        scratch_shapes=[pltpu.VMEM(*(s if isinstance(s[0], tuple) else (s, F32))) for s in scratch]
        + ([pltpu.SemaphoreType.DMA((sems,))] if sems else []),
        compiler_params=pltpu.CompilerParams(vmem_limit_bytes=12 * 1024 * 1024),
        cost_estimate=cost,
        input_output_aliases=in_place or {},
        **more,
    )


def swapped(x, far):
    size = lax.axis_size(AXES)
    return lax.ppermute(x, AXES, [(i, (i + (1 if (i % 2 == 0) != far else -1)) % size) for i in range(size)])


def everyone(payload, shape):
    devices = lax.axis_size(AXES)
    return lax.all_to_all(payload.reshape((devices,) + shape), AXES, 0, 0, tiled=True).reshape(-1, 128)


def per_device(forcing, kappa, elem_order):
    devices = lax.axis_size(AXES)
    nodes, face, face_row = (2, 512, 128), (2, 56, 128), (2, 64, 128)
    plane, grid, flat = (8, PLANE), (devices, PLANE), (512, PLANE)
    edge, stored, choice = (2, 128, 128), (PLANE, 512), ((PLANE, PLANE), jnp.bfloat16)
    table = jnp.asarray(np.concatenate([STIFF_PARTS[k] for k in (0, 0, 1, 1, 0, 2)], 1), jnp.bfloat16)
    long = pl.CostEstimate(flops=10**11, bytes_accessed=2**28, transcendentals=0)
    payload_rows = (devices * 6, 128)
    load, far, near, own, payload = call(
        opening,
        [nodes, face_row, face_row, plane, payload_rows],
        [(2, PLANE, 256), (1, PLANE), ((1, PLANE), jnp.int32), payload_rows],
        5,
        hbm_in=(0, 1, 2),
        hbm_out=(4,),
        inputs=3,
    )(*(pltpu.with_memory_space_constraint(x, pltpu.HBM) for x in (forcing, kappa.reshape(1, PLANE), elem_order)))
    far, near = swapped(far, True), swapped(near, False)
    (payload,) = call(
        late_payload, [payload_rows], [payload_rows], 1, in_place={2: 0}, hbm_in=(2,), hbm_out=(0,), inputs=3
    )(load, own, payload)
    gather = everyone(payload, (3, 2, 128))
    resid, scaled, image, layers, lower, far, near = call(
        first_faces, [nodes, nodes, nodes, plane, plane, face_row, face_row], [flat], cost=long, in_place={0: 0}
    )(load, far, near, own, table)
    far, near = swapped(far, True), swapped(near, False)
    vert, target, scale, coeff, smooth = call(first_coarse, [grid] * 4 + [nodes], [edge])(gather, layers)
    scaled_change, change, sums, planes, column_planes, outer = call(
        second_rough, [nodes] * 2 + [(48, PLANE), plane, (128, PLANE), (128, PLANE)], [flat, nodes], in_place={1: 0}
    )(image, smooth, layers, table, resid, scaled)
    added, next_far, next_near, payload = call(
        second_faces, [(128, PLANE), face, face, (devices * 7, 128)], [edge, (64, 2 * PLANE)]
    )(image, scaled_change, change, outer, far, near, layers, table, scaled, lower, sums, planes, column_planes)
    step = everyone(payload, (7, 1, 128))
    next_far, next_near = swapped(next_far, True), swapped(next_near, False)
    image, scaled_change, change, choose, applied, first_modes = call(
        complete, [nodes] * 3 + [choice, grid, (24, PLANE)], [(2, 256, 128)], in_place={0: 0, 1: 1, 2: 2}
    )(image, scaled_change, change, far, near, added, layers, coeff, vert)
    modes, scalars = call(second_coarse, [(24, PLANE), (8, 128)], [grid])(
        coeff, step, vert, applied, target, scale, first_modes
    )
    found, rest = call(combine, [nodes, nodes], [nodes, edge], in_place={0: 0, 1: 1})(
        scaled, resid, scaled_change, image, change, modes, layers, scalars
    )
    found, left = call(closing, [stored, stored], [nodes, (2,) + stored], 2, hbm_out=(0, 1))(
        found, rest, next_far, next_near, scalars, choose
    )
    return found, left


def solution(mesh):
    in_specs = (P(AXES, None), P(AXES), P(AXES, None))
    out_specs = (P(AXES, None), P(AXES, None))
    return jax.shard_map(
        per_device, mesh=mesh, in_specs=in_specs, out_specs=out_specs, check_vma=False
    )
```

```python
import functools
import math

import jax
import jax.numpy as jnp
import ml_dtypes
import numpy as np
from jax import lax
from jax.experimental import pallas as pl
from jax.experimental.pallas import tpu as pltpu
from jax.sharding import PartitionSpec as P

EX = 8
EY = 32
PLANE = EX * EY
SWEEPS = 4
REACT = 0.02
OMEGA = 0.6
AXES = ("elem", "face")
F32 = jnp.float32


def legendre_seven(points):
    before = np.ones(8)
    current = np.array(points)
    for degree in range(1, 7):
        following = ((2 * degree + 1) * points * current - degree * before) / (degree + 1)
        before = current
        current = following
    return current


def line_tables():
    points = np.array(
        [
            -1.0,
            -0.8717401485096066,
            -0.5917001814331423,
            -0.2092992179024789,
            0.2092992179024789,
            0.5917001814331423,
            0.8717401485096066,
            1.0,
        ]
    )
    weights = np.array(
        [
            1.0 / 28.0,
            0.2107042271435061,
            0.3411226924835044,
            0.4124587946587038,
            0.4124587946587038,
            0.3411226924835044,
            0.2107042271435061,
            1.0 / 28.0,
        ]
    )
    legendre = legendre_seven(points)
    derivative = np.zeros((8, 8))
    for left_node in range(8):
        for right_node in range(8):
            if left_node != right_node:
                derivative[left_node, right_node] = legendre[left_node] / (
                    legendre[right_node] * (points[left_node] - points[right_node])
                )
    derivative[0, 0] = -14.0
    derivative[7, 7] = 14.0
    stiffness = derivative.T @ (weights[:, None] * derivative)
    return points, weights, stiffness


POINTS, WEIGHTS, STIFF = line_tables()
DIAG = np.diag(STIFF)
ENDS = np.array([2.0] + [1.0] * 6 + [2.0])
MASS = np.diag(WEIGHTS)
STIFF_XY = np.kron(MASS, STIFF) + np.kron(STIFF, MASS)
STIFF_PARTS = []
for part in range(3):
    STIFF_PARTS.append((STIFF_XY - sum(STIFF_PARTS)).astype(ml_dtypes.bfloat16).astype(np.float64))
INTERP = np.stack([(1.0 - POINTS) / 2.0, (1.0 + POINTS) / 2.0], 1)
LINE_MASS = INTERP.T @ (WEIGHTS[:, None] * INTERP)
LINE_STIFF = INTERP.T @ STIFF @ INTERP
MASS_SUM = (LINE_MASS[0, 0] + LINE_MASS[0, 1]) / 2.0
MASS_DIF = (LINE_MASS[0, 0] - LINE_MASS[0, 1]) / 2.0
STIFF_DIF = LINE_STIFF[0, 0]
MODE_STIFF = [
    0.0,
    STIFF_DIF * MASS_SUM**2,
    2.0 * STIFF_DIF * MASS_DIF * MASS_SUM,
    3.0 * STIFF_DIF * MASS_DIF**2,
]
MODE_MASS = [MASS_SUM ** (3 - j) * MASS_DIF**j for j in range(4)]
CORNER_STIFF = 3.0 * LINE_STIFF[0, 0] * LINE_MASS[0, 0] ** 2
CORNER_MASS = LINE_MASS[0, 0] ** 3


def lane(shape):
    return lax.broadcasted_iota(jnp.int32, shape, len(shape) - 1)


def next_x(v):
    return jnp.where(lane(v.shape) % EX == EX - 1, pltpu.roll(v, EX - 1, 1), pltpu.roll(v, PLANE - 1, 1))


def prev_x(v):
    return jnp.where(lane(v.shape) % EX == 0, pltpu.roll(v, PLANE - EX + 1, 1), pltpu.roll(v, 1, 1))


def next_y(v):
    return pltpu.roll(v, PLANE - EX, 1)


def prev_y(v):
    return pltpu.roll(v, EX, 1)


def next_xy(v):
    return jnp.where(lane(v.shape) % EX == EX - 1, pltpu.roll(v, PLANE - 1, 1), pltpu.roll(v, PLANE - EX - 1, 1))


def prev_xy(v):
    return jnp.where(lane(v.shape) % EX == 0, pltpu.roll(v, 1, 1), pltpu.roll(v, EX + 1, 1))


def next_z(v):
    half = v.shape[0] // 2
    return jnp.concatenate([v[half:], pltpu.roll(v[:half], half - 1, 0)], axis=0)


def prev_z(v):
    half = v.shape[0] // 2
    return jnp.concatenate([pltpu.roll(v[half:], 1, 0), v[:half]], axis=0)


def plane_row(layer, planes):
    layer = lax.rem(layer + planes, planes)
    return pl.ds(lax.div(layer, 2) + lax.rem(layer, 2) * (planes // 2), 1)


def column(values):
    row = lax.broadcasted_iota(jnp.int32, (8, PLANE), 0)
    out = jnp.full((8, PLANE), float(values[0]), F32)
    for k in range(1, 8):
        out = jnp.where(row == k, float(values[k]), out)
    return out


def rows_of(nz, ny):
    start = (nz * 8 + ny) * 8
    return slice(start, start + 8)


def get(ref, rows):
    return jnp.concatenate([ref[0, rows, :], ref[1, rows, :]], axis=1)


def put(ref, rows, value):
    ref[0, rows, :] = value[:, :128]
    ref[1, rows, :] = value[:, 128:]


def sum_xy(ref):
    planes = ref.shape[1] // 64
    first, last = pl.ds(0, planes * 8, stride=8), pl.ds(7, planes * 8, stride=8)
    shared = get(ref, last) + next_x(get(ref, first))
    put(ref, last, shared)
    put(ref, first, prev_x(shared))
    for nz in range(planes):
        shared = get(ref, rows_of(nz, 7)) + next_y(get(ref, rows_of(nz, 0)))
        put(ref, rows_of(nz, 7), shared)
        put(ref, rows_of(nz, 0), prev_y(shared))


def restrict(ref, points):
    sums_z, difs_z = [], []
    for ny in range(8):
        tiles = [get(ref, rows_of(nz, ny)) for nz in range(8)]
        sums_z.append(functools.reduce(lambda a, b: a + b, tiles))
        difs_z.append(sum(float(POINTS[7 - k]) * (tiles[7 - k] - tiles[k]) for k in range(4)))
    return restrict_xy(sums_z, difs_z, points)


def restrict_summed(ref, points):
    inv_ends = column(1.0 / ENDS)
    sums_z, difs_z = [], []
    for ny in range(8):
        tiles = [get(ref, rows_of(nz, ny)) for nz in range(8)]
        share = inv_ends * float(1.0 / ENDS[ny])
        sums_z.append(functools.reduce(lambda a, b: a + b, tiles) * share)
        difs_z.append(sum(float(POINTS[7 - k]) * (tiles[7 - k] - tiles[k]) for k in range(4)) * share)
    return restrict_xy(sums_z, difs_z, points)


def restrict_xy(sums_z, difs_z, points):
    planes = []
    for parts in (sums_z, difs_z):
        total = functools.reduce(lambda a, b: a + b, parts)
        slope = sum(float(POINTS[7 - k]) * (parts[7 - k] - parts[k]) for k in range(4))
        in_y = []
        for part in (total, slope):
            flat = jnp.sum(part, axis=0, keepdims=True)
            steep = jnp.sum(part * points, axis=0, keepdims=True)
            in_y.append((flat - steep) + prev_x(flat + steep))
        planes.append((in_y[0] - in_y[1]) + prev_y(in_y[0] + in_y[1]))
    return (planes[0] - planes[1]) * 0.125, (planes[0] + planes[1]) * 0.125


def both(v, following):
    after = following(v)
    return after + v, after - v


def both_back(total, dif, preceding):
    return (total - dif) + preceding(total + dif)


def coarse_modes(coeff):
    return [float(REACT * MODE_MASS[0])] + [
        float(MODE_STIFF[j]) * coeff + float(REACT * MODE_MASS[j]) for j in range(1, 4)
    ]


def coarse_tables(coeff):
    near = coeff + prev_x(coeff)
    near = near + prev_y(near)
    near = near + prev_z(near)
    scale = float(OMEGA) / (float(CORNER_STIFF) * near + float(8.0 * REACT * CORNER_MASS))
    return coarse_modes(coeff), scale


def coarse_apply(vert, modes):
    after_x, after_y, after_xy = next_x(vert), next_y(vert), next_xy(vert)
    in_x = [(after_x + vert, after_xy + after_y), (after_x - vert, after_xy - after_y)]
    back = []
    for jx in range(2):
        first, second = in_x[jx]
        for jy, in_y in enumerate((second + first, second - first)):
            in_z = both(in_y, next_z)
            scaled = [modes[jx + jy + jz] * in_z[jz] for jz in range(2)]
            back.append(both_back(scaled[0], scaled[1], prev_z))
    ss, sd, ds, dd = back
    low, high = (ss - sd, ss + sd), (ds - dd, ds + dd)
    return ((low[0] - high[0]) + prev_x(low[0] + high[0])) + (prev_y(low[1] - high[1]) + prev_xy(low[1] + high[1]))


def coarse_solve(target, modes, scale):
    vert = scale * target
    for _ in range(SWEEPS - 1):
        vert = vert + scale * (target - coarse_apply(vert, modes))
    return vert


def gathered_rows(ref, row, size):
    chips = ref.shape[0] // (2 * size)
    return jnp.concatenate([ref[pl.ds(core * size + row, chips, stride=2 * size), :] for core in range(2)], axis=0)


def gathered(ref, k, size):
    return jnp.concatenate([gathered_rows(ref, 2 * k + h, size) for h in range(2)], axis=1)


def halves(row):
    return [row[:, :128], row[:, 128:]]


def send(ref, rows):
    count = len(rows)
    times = 8 // math.gcd(count, 8)
    block = jnp.concatenate(rows * times, axis=0)
    for k in range(0, ref.shape[0], count * times):
        ref[k : k + count * times, :] = block


def layer_modes(vert_ref, shift):
    me, devices = my_layer(), vert_ref.shape[0]
    lower, upper = (vert_ref[plane_row(me + shift + k, devices), :] for k in range(2))
    modes = []
    for along_z in (upper + lower, upper - lower):
        for along_y in both(along_z, next_y):
            modes += both(along_y, next_x)
    return 0.125 * jnp.concatenate(modes, axis=0)


class Smooth:
    def __init__(self, modes, coeff, points, weight_x):
        row = lax.broadcasted_iota(jnp.int32, (8, PLANE), 0)
        ends = jnp.where(row == 0, -1.0, jnp.where(row == 7, 1.0, 0.0))
        m = [[[modes[4 * z + 2 * y + x : 4 * z + 2 * y + x + 1] for x in range(2)] for y in range(2)] for z in range(2)]
        self.xy = [[m[z][y][0] + m[z][y][1] * points for y in range(2)] for z in range(2)]
        self.dx = [[m[z][y][1] for y in range(2)] for z in range(2)]
        self.ends_coeff = ends * coeff
        self.weight_coeff = weight_x * coeff
        self.mass = float(REACT) * weight_x

    def value(self, nz, ny):
        by_y = [self.xy[z][0] + float(POINTS[ny]) * self.xy[z][1] for z in range(2)]
        return by_y[0] + float(POINTS[nz]) * by_y[1]

    def operated(self, nz, ny, value):
        wy, wz, py, pz = (float(t) for t in (WEIGHTS[ny], WEIGHTS[nz], POINTS[ny], POINTS[nz]))
        slope = (self.dx[0][0] + py * self.dx[0][1]) + pz * (self.dx[1][0] + py * self.dx[1][1])
        out = self.ends_coeff * (slope * (wy * wz)) + (self.mass * (wy * wz)) * value
        flux = None
        if ny in (0, 7):
            flux = (self.xy[0][1] + pz * self.xy[1][1]) * (wz * py)
        if nz in (0, 7):
            along = (self.xy[1][0] + py * self.xy[1][1]) * (wy * pz)
            flux = along if flux is None else flux + along
        return out if flux is None else out + self.weight_coeff * flux


def kappa_sums(own, below, above):
    row = lax.broadcasted_iota(jnp.int32, (8, PLANE), 0)
    table = []
    for along_z in (own + below, own, own + above):
        in_z = []
        for along_y in (along_z + prev_y(along_z), along_z, along_z + next_y(along_z)):
            first = along_y + prev_x(along_y)
            last = along_y + next_x(along_y)
            in_z.append(jnp.where(row == 0, first, jnp.where(row == 7, last, along_y)))
        table.append(in_z)
    return table


def kind(node):
    return 0 if node == 0 else (2 if node == 7 else 1)


def product(table, values):
    low, middle, high = pieces(values)
    stacked = jnp.concatenate([high, middle, high, middle, low, high], axis=0)
    return jnp.dot(table, stacked, preferred_element_type=F32)


def operate(z_ref, xy_ref, out_ref, table_ref, coeff, weight_x):
    for nz in range(8):
        rows = slice(64 * nz, 64 * nz + 64)
        xy_ref[rows, :] = product(table_ref[...], get(z_ref, rows))
    for ny in range(8):
        tiles = [get(z_ref, rows_of(nz, ny)) for nz in range(8)]
        even = [tiles[k] + tiles[7 - k] for k in range(4)]
        odd = [tiles[k] - tiles[7 - k] for k in range(4)]
        for nz in range(4):
            even_part = sum(float((STIFF[nz, k] + STIFF[nz, 7 - k]) / 2) * even[k] for k in range(4))
            odd_part = sum(float((STIFF[nz, k] - STIFF[nz, 7 - k]) / 2) * odd[k] for k in range(4))
            for node, term in ((nz, even_part + odd_part), (7 - nz, even_part - odd_part)):
                area = weight_x * float(WEIGHTS[ny])
                local = coeff * (
                    float(WEIGHTS[node]) * xy_ref[rows_of(node, ny), :] + area * term
                ) + (float(REACT * WEIGHTS[node]) * area) * tiles[node]
                put(out_ref, rows_of(node, ny), local)


def fine_diag(sums, nz, ny, weight_x, diag_x, ends_x):
    wy, wz, ky, kz = (float(t) for t in (WEIGHTS[ny], WEIGHTS[nz], DIAG[ny], DIAG[nz]))
    stiff = diag_x * (wy * wz) + weight_x * (ky * wz + wy * kz)
    mass = (weight_x * ends_x) * float(REACT * wy * wz * ENDS[ny] * ENDS[nz])
    return sums[kind(nz)][kind(ny)] * stiff + mass


def my_layer():
    return lax.axis_index("elem") * lax.axis_size("face") + lax.axis_index("face")


def face_rows(ref):
    even = lax.rem(my_layer(), 2) == 0
    last = ref.shape[1] - 64
    near = pl.multiple_of(jnp.where(even, last, 0), 64)
    far = pl.multiple_of(jnp.where(even, 0, last), 64)
    return pl.ds(near, 64), pl.ds(far, 64)


def faces_out(ref, near_ref, far_ref):
    for rows, out_ref in zip(face_rows(ref), (near_ref, far_ref)):
        out_ref[:, 0:56, :] = ref[:, pl.ds(rows.start, 56), :]


def face_in(ref):
    return jnp.concatenate([get(ref, slice(0, 56)), next_y(get(ref, slice(0, 8)))], axis=0)


def faces_in(ref, near_ref, far_ref):
    for rows, in_ref in zip(face_rows(ref), (near_ref, far_ref)):
        put(ref, rows, get(ref, rows) + face_in(in_ref))


def columns_of_nodes():
    return column(POINTS), column(WEIGHTS), column(DIAG), column(ENDS)


def pieces(v):
    high = v.astype(jnp.bfloat16)
    rest = v - high.astype(F32)
    middle = rest.astype(jnp.bfloat16)
    low = (rest - middle.astype(F32)).astype(jnp.bfloat16)
    return low, middle, high


def selection(order):
    place = lax.broadcasted_iota(jnp.int32, (PLANE, PLANE), 0).astype(order.dtype)
    return jnp.where(place == order, 1.0, 0.0).astype(jnp.bfloat16)


def opening(
    forcing_ref, kappa_ref, order_ref, load_ref, far_ref, near_ref, own_ref, payload_ref,
    held, held_kappa, held_order, held_payload, sems,
):
    small = [
        pltpu.make_async_copy(order_ref, held_order, sems.at[0]),
        pltpu.make_async_copy(kappa_ref, held_kappa, sems.at[1]),
    ]
    parts = [
        pltpu.make_async_copy(forcing_ref.at[:, pl.ds(256 * k, 256)], held.at[k], sems.at[2 + k]) for k in range(2)
    ]
    for copy in small + parts:
        copy.start()
    for copy in small:
        copy.wait()
    order = held_order[...]
    choose = selection(order)
    coeff = jnp.zeros((8, PLANE), F32)
    for piece in pieces(jnp.broadcast_to(held_kappa[...], (8, PLANE))):
        coeff = coeff + lax.dot_general(piece, choose, (((1,), (1,)), ((), ())), preferred_element_type=F32)
    own = jnp.concatenate([coeff[0:3], order.astype(F32), coeff[4:8]], axis=0)
    own_ref[...] = own
    for k, copy in enumerate(parts):
        copy.wait()
        load = jnp.zeros((PLANE, 256), F32)
        for piece in pieces(held[k]):
            load = load + jnp.dot(choose, piece, preferred_element_type=F32)
        put(load_ref, slice(256 * k, 256 * k + 256), load.T)
    sum_xy(load_ref)
    faces_out(load_ref, near_ref, far_ref)
    put(near_ref, slice(56, 64), own)
    put(far_ref, slice(56, 64), own)


    @pl.when(starts_early())
    def _():
        write_payload(load_ref, own_ref, payload_ref, held_payload, sems.at[4])


def starts_early():
    return my_layer() < lax.axis_size("elem") * lax.axis_size("face") // 2


def write_payload(load_ref, own_ref, payload_ref, held, sem):
    lower, upper = restrict_summed(load_ref, column(POINTS))
    send(held, halves(lower) + halves(upper) + halves(own_ref[0:1, :]))
    copy = pltpu.make_async_copy(held, payload_ref, sem)
    copy.start()
    copy.wait()


def late_payload(load_ref, own_ref, _, payload_ref, held, sems):
    @pl.when(jnp.logical_not(starts_early()))
    def _():
        write_payload(load_ref, own_ref, payload_ref, held, sems.at[0])


def below_above(near, far):
    even = lax.rem(my_layer(), 2) == 0
    return jnp.where(even, far, near), jnp.where(even, near, far)


def row_after_face(ref):
    return get(ref, slice(56, 64))[0:1]


def first_faces(
    load_ref, far_in_ref, near_in_ref, own_ref, table_ref,
    resid_ref, scaled_ref, image_ref, layers_ref, lower_ref, far_ref, near_ref, xy_ref,
):
    points, weight_x, _, _ = columns_of_nodes()
    own = own_ref[0:1, :]
    below, above = below_above(row_after_face(near_in_ref), row_after_face(far_in_ref))
    layers_ref[...] = jnp.concatenate([own, below, above, own_ref[3:8, :]], axis=0)
    resid_ref[...] = load_ref[...]
    faces_in(resid_ref, near_in_ref, far_in_ref)
    over_diag(functools.partial(get, resid_ref), scaled_ref, layers_ref)
    operate(scaled_ref, xy_ref, image_ref, table_ref, own, weight_x)
    lower, upper = restrict(image_ref, points)
    sum_xy(image_ref)
    faces_out(image_ref, near_ref, far_ref)
    lower_ref[...] = jnp.broadcast_to(lower, lower_ref.shape)
    put(near_ref, slice(56, 64), jnp.broadcast_to(upper, (8, PLANE)))
    put(far_ref, slice(56, 64), jnp.broadcast_to(upper, (8, PLANE)))


def over_diag(resid, scaled_ref, layers_ref):
    _, weight_x, diag_x, ends_x = columns_of_nodes()
    sums = kappa_sums(*(layers_ref[k : k + 1, :] for k in range(3)))
    for nz in range(8):
        for ny in range(8):
            rows = rows_of(nz, ny)
            put(scaled_ref, rows, resid(rows) / fine_diag(sums, nz, ny, weight_x, diag_x, ends_x))


def three_modes(vert_ref):
    return jnp.concatenate([layer_modes(vert_ref, shift) for shift in (0, -1, 1)], axis=0)


def smooths_of(modes, layers_ref):
    points, weight_x, _, _ = columns_of_nodes()
    return [Smooth(modes[8 * k : 8 * k + 8], layers_ref[k : k + 1, :], points, weight_x) for k in range(3)]


def smooth_image(smooths, out_ref, edge_ref):
    own, below, above = smooths
    for nz in range(8):
        for ny in range(8):
            put(out_ref, rows_of(nz, ny), own.operated(nz, ny, own.value(nz, ny)))
    sum_xy(out_ref)
    for plane, (smooth, nz) in enumerate(((below, 7), (above, 0))):
        for ny in range(8):
            put(edge_ref, rows_of(plane, ny), smooth.operated(nz, ny, smooth.value(nz, ny)))
    sum_xy(edge_ref)
    out_ref[:, 0:64, :] += edge_ref[:, 0:64, :]
    out_ref[:, 448:512, :] += edge_ref[:, 64:128, :]


def first_coarse(coarse_ref, layers_ref, vert_ref, target_ref, scale_ref, coeff_ref, smooth_ref, edge_ref):
    coeff = gathered(coarse_ref, 2, 6)
    coeff_ref[...] = coeff
    modes, scale = coarse_tables(coeff)
    target = gathered(coarse_ref, 0, 6) + prev_z(gathered(coarse_ref, 1, 6))
    vert = coarse_solve(target, modes, scale)
    vert_ref[...] = vert
    target_ref[...] = target
    scale_ref[...] = scale
    smooth_image(smooths_of(three_modes(vert_ref), layers_ref), smooth_ref, edge_ref)


def pack(sums):
    place = lane((8, 128)) // 16
    packed = jnp.zeros((8, 128), F32)
    for k, total in enumerate(sums):
        total = total[:, :128] + total[:, 128:]
        for by in (64, 32, 16):
            total = total + pltpu.roll(total, by, 1)
        packed = jnp.where(place == k, total, packed)
    return jnp.sum(packed, axis=0, keepdims=True)


def second_rough(
    image_ref, smooth_ref, layers_ref, table_ref, resid_ref, scaled_ref,
    scaled_change_ref, change_ref, sums_ref, planes_ref, column_ref, outer_ref, xy_ref, whole_ref,
):
    points, weight_x, _, _ = columns_of_nodes()
    inv_ends = column(1.0 / ENDS)
    whole_ref[...] = image_ref[...] + smooth_ref[...]
    over_diag(functools.partial(get, whole_ref), scaled_change_ref, layers_ref)
    operate(scaled_change_ref, xy_ref, change_ref, table_ref, layers_ref[0:1, :], weight_x)
    planes_ref[...] = jnp.concatenate(list(restrict(change_ref, points)) * 4, axis=0)
    sum_xy(change_ref)
    sums = [jnp.zeros((8, PLANE), F32)] * 6
    for ny in range(8):
        along = [jnp.zeros((8, PLANE), F32)] * 2
        for nz in range(8):
            rows = rows_of(nz, ny)
            share = float(1.0 / (ENDS[nz] * ENDS[ny]))
            scaled, change = get(scaled_ref, rows) * share, get(scaled_change_ref, rows)
            along = [total + float(STIFF[nz, node]) * change for total, node in zip(along, (0, 7))]
            change = change * share
            whole, image = get(whole_ref, rows), get(image_ref, rows)
            terms = [
                scaled * get(resid_ref, rows), scaled * whole, change * whole, scaled * image, change * image,
                change * (get(change_ref, rows) * float(ENDS[nz])),
            ]
            sums = [total + term for total, term in zip(sums, terms)]
        for k in range(2):
            column_ref[64 * k + 8 * ny : 64 * k + 8 * ny + 8, :] = along[k]
    sums_ref[...] = jnp.concatenate([total * inv_ends for total in sums], axis=0)
    for k, rows in enumerate((slice(0, 64), slice(448, 512))):
        outer_ref[64 * k : 64 * k + 64, :] = get(whole_ref, rows)


def second_faces(
    image_ref, scaled_change_ref, change_ref, outer_ref, far_in_ref, near_in_ref, layers_ref, table_ref,
    scaled_ref, lower_ref, sums_ref, planes_ref, column_ref,
    added_ref, far_ref, near_ref, payload_ref, edge_ref, xy_ref,
):
    points, weight_x, _, _ = columns_of_nodes()
    inv_ends = column(1.0 / ENDS)
    even = lax.rem(my_layer(), 2) == 0
    own = layers_ref[0:1, :]
    kappas = kappa_sums(*(layers_ref[k : k + 1, :] for k in range(3)))
    faces = below_above(face_in(near_in_ref), face_in(far_in_ref))
    tiles = [slice(8 * ny, 8 * ny + 8) for ny in range(8)]
    added = added_by(faces, kappas, columns_of_nodes())
    xy_ref[...] = product(table_ref[...], jnp.concatenate(added, axis=1))
    along, at_face = [], []
    for k in range(2):
        along.append(local_along(own, weight_x, added[k]))
        flux = own * xy_ref[:, PLANE * k : PLANE * k + PLANE]
        at_face.append(float(WEIGHTS[0]) * jnp.concatenate(
            [flux[t] + (float(REACT * WEIGHTS[ny]) * weight_x) * added[k][t] for ny, t in enumerate(tiles)], axis=0
        ))
    local = [
        (float(STIFF[nz, 0]) * along[0] + float(STIFF[nz, 7]) * along[1]) + at_face[k] for k, nz in enumerate((0, 7))
    ]
    flat = at_face[0] + at_face[1]
    slope = (along[1] + at_face[1]) - (along[0] + at_face[0])
    lower, upper = restrict_xy([flat[t] for t in tiles], [slope[t] for t in tiles], points)
    lower, upper = lower + planes_ref[0:1, :], upper + planes_ref[1:2, :]
    sums = [jnp.zeros((8, PLANE), F32)] * 5
    energy = jnp.zeros((8, PLANE), F32)
    planes = [slice(0, 64), slice(448, 512)]
    for k in range(2):
        s_plane, q_plane, i_plane, c_plane = (
            get(ref, planes[k]) for ref in (scaled_ref, scaled_change_ref, image_ref, change_ref)
        )
        w_plane = outer_ref[64 * k : 64 * k + 64, :]
        for ny in range(8):
            tile = tiles[ny]
            share = float(1.0 / ENDS[ny])
            half = share * float(1.0 / ENDS[0])
            face = faces[k][tile]
            s, q, dq = s_plane[tile] * half, q_plane[tile] * half, added[k][tile] * half
            sums[0] = sums[0] + s * face
            sums[1] = sums[1] + (q * face + dq * (w_plane[tile] + face))
            sums[2] = sums[2] + s * face
            sums[3] = sums[3] + (q * face + dq * (i_plane[tile] + face))
            sums[4] = sums[4] + (added[k][tile] * c_plane[tile]) * share
            energy = energy + (
                column_ref[64 * k + 8 * ny : 64 * k + 8 * ny + 8, :] * along[k][tile]
                + q_plane[tile] * at_face[k][tile]
                + added[k][tile] * local[k][tile]
            )
    sums = [sums_ref[8 * k + 8 : 8 * k + 16, :] + sums[k] * inv_ends for k in range(5)]
    sums = pack([sums_ref[0:8, :]] + sums[:4] + [sums[4] + energy])
    below, _ = below_above(row_after_face(near_in_ref), row_after_face(far_in_ref))
    send(payload_ref, halves(lower_ref[0:1, :] + below) + halves(lower) + halves(upper) + [sums])
    for k in range(2):
        put(edge_ref, slice(64 * k, 64 * k + 64), local[k])
        added_ref[64 * k : 64 * k + 64, :] = at_face[k]
    sum_xy(edge_ref)
    change = [(get(change_ref, planes[k]) + get(edge_ref, slice(64 * k, 64 * k + 64)))[0:56] for k in range(2)]
    put(far_ref, slice(0, 56), jnp.where(even, change[0], change[1]))
    put(near_ref, slice(0, 56), jnp.where(even, change[1], change[0]))


def local_along(own, weight_x, added):
    return own * jnp.concatenate(
        [(weight_x * float(WEIGHTS[ny])) * added[8 * ny : 8 * ny + 8] for ny in range(8)], axis=0
    )


def added_by(faces, kappas, columns):
    _, weight_x, diag_x, ends_x = columns
    return [
        jnp.concatenate(
            [
                face[8 * ny : 8 * ny + 8] / fine_diag(kappas, nz, ny, weight_x, diag_x, ends_x)
                for ny in range(8)
            ],
            axis=0,
        )
        for nz, face in zip((0, 7), faces)
    ]


def complete(
    first_ref, first_scaled_ref, first_change_ref, rough_ref, far_in_ref, near_in_ref, at_face_ref, layers_ref, coeff_ref,
    vert_ref, image_ref, scaled_change_ref, change_ref, z_ref, choose_ref, applied_ref, edge_ref, smooth_ref, sides_ref,
):
    columns = columns_of_nodes()
    applied_ref[...] = coarse_apply(vert_ref[...], coarse_modes(coeff_ref[...]))
    smooths = smooths_of(three_modes(vert_ref), layers_ref)
    for nz in range(8):
        for ny in range(8):
            rows = rows_of(nz, ny)
            put(z_ref, rows, get(rough_ref, rows) + smooths[0].value(nz, ny))
    smooth_image(smooths, smooth_ref, sides_ref)
    choose_ref[...] = selection(layers_ref[3:4, :]).astype(F32).T.astype(jnp.bfloat16)
    image_ref[...] = first_ref[...] + smooth_ref[...]
    scaled_change_ref[...] = first_scaled_ref[...]
    faces_in(image_ref, near_in_ref, far_in_ref)
    kappas = kappa_sums(*(layers_ref[k : k + 1, :] for k in range(3)))
    added = added_by(below_above(face_in(near_in_ref), face_in(far_in_ref)), kappas, columns)
    for k, rows in enumerate((slice(0, 64), slice(448, 512))):
        put(scaled_change_ref, rows, get(scaled_change_ref, rows) + added[k])
        put(edge_ref, slice(64 * k, 64 * k + 64), local_along(layers_ref[0:1, :], columns[1], added[k]))
        put(edge_ref, slice(128 + 64 * k, 192 + 64 * k), at_face_ref[64 * k : 64 * k + 64, :])
    sum_xy(edge_ref)
    along = [get(edge_ref, slice(64 * k, 64 * k + 64)) for k in range(2)]
    for nz in range(8):
        rows = slice(64 * nz, 64 * nz + 64)
        new = get(first_change_ref, rows) + (float(STIFF[nz, 0]) * along[0] + float(STIFF[nz, 7]) * along[1])
        if nz in (0, 7):
            new = new + get(edge_ref, slice(128 + 64 * (nz // 7), 192 + 64 * (nz // 7)))
        put(change_ref, rows, new)


def folded(value):
    return functools.reduce(lambda a, b: a + b, [value[k : k + 8] for k in range(0, value.shape[0], 8)])


def to_stored(choose, value):
    total = jnp.zeros((choose.shape[0], value.shape[0]), F32)
    for piece in pieces(value)[1:]:
        total = total + lax.dot_general(choose, piece, (((1,), (1,)), ((), ())), preferred_element_type=F32)
    return total


def closing(
    coeff_ref, step_ref, first_ref, applied_ref, target_ref, scale_ref, layers_ref,
    resid_ref, z_ref, image_ref, scaled_change_ref, change_ref, far_ref, near_ref, choose_ref,
    solution_ref, residual_ref, vert_ref, grid_ref, sum_ref, edge_ref, held, sems,
):
    modes = coarse_modes(coeff_ref[...])
    target, first, applied = target_ref[...], first_ref[...], applied_ref[...]
    rough, rough_change = gathered(step_ref, 0, 7), gathered(step_ref, 1, 7) + prev_z(gathered(step_ref, 2, 7))
    parts = folded(gathered_rows(step_ref, 6, 7))
    sums = [parts] + [pltpu.roll(parts, 128 - 16 * k, 1) for k in range(1, 6)]
    used = lane(parts.shape) < 16

    def total(fine, coarse):
        coarse = folded(coarse)
        return jnp.sum(jnp.where(used, fine, 0.0) + (coarse[:, :128] + coarse[:, 128:]), keepdims=True)

    image = rough + applied
    change = coarse_solve(image, modes, scale_ref[...])
    vert_ref[...] = change
    smooths = smooths_of(three_modes(vert_ref), layers_ref)
    change_applied = coarse_apply(change, modes)
    gamma = total(sums[0], target * first)
    energy = total(sums[3], first * (2.0 * rough + applied))
    alpha = gamma / energy
    vert = first - alpha * change
    progress = total(sums[0] - alpha * (2.0 * sums[1] - alpha * sums[2]), (target - alpha * image) * vert)
    second = total(
        sums[3] - alpha * (2.0 * sums[4] - alpha * sums[5]),
        vert * (2.0 * (rough - alpha * rough_change) + (applied - alpha * change_applied)),
    )
    cross = total(sums[1] - alpha * sums[2], vert * image)
    smooth_image(smooths, sum_ref, edge_ref)
    sum_ref[...] += change_ref[...]
    faces_in(sum_ref, near_ref, far_ref)
    beta = progress / gamma
    alpha_next = progress / (second + beta * (2.0 * cross + beta * energy))
    share, change_share = alpha + alpha_next * beta + alpha_next, alpha_next * alpha
    choose, every = choose_ref[...], slice(0, 512)
    for nz in range(8):
        for ny in range(8):
            rows = rows_of(nz, ny)
            other = get(scaled_change_ref, rows) + smooths[0].value(nz, ny)
            grid_ref[rows, :] = share * get(z_ref, rows) - change_share * other
    held[0] = to_stored(choose, grid_ref[...])
    sum_ref[...] = resid_ref[...] - share[None] * image_ref[...] + change_share[None] * sum_ref[...]
    copies = [pltpu.make_async_copy(held.at[0], solution_ref, sems.at[0])]
    copies[0].start()
    held[1] = to_stored(choose, get(sum_ref, every))
    copies.append(pltpu.make_async_copy(held.at[1], residual_ref, sems.at[1]))
    copies[1].start()
    for copy in copies:
        copy.wait()


def call(kernel, outs, scratch=(), sems=0, cost=None, in_place=None, hbm_in=(), hbm_out=(), inputs=0):
    def specs(count, far):
        return [pl.BlockSpec(memory_space=pltpu.HBM if k in far else pltpu.VMEM) for k in range(count)]

    more = {"in_specs": specs(inputs, hbm_in)} if hbm_in else {}
    return pl.pallas_call(
        kernel,
        out_shape=[jax.ShapeDtypeStruct(*(s if isinstance(s[0], tuple) else (s, F32))) for s in outs],
        out_specs=specs(len(outs), hbm_out),
        scratch_shapes=[pltpu.VMEM(*(s if isinstance(s[0], tuple) else (s, F32))) for s in scratch]
        + ([pltpu.SemaphoreType.DMA((sems,))] if sems else []),
        compiler_params=pltpu.CompilerParams(vmem_limit_bytes=12 * 1024 * 1024),
        cost_estimate=cost,
        input_output_aliases=in_place or {},
        **more,
    )


def swapped(x, far):
    size = lax.axis_size(AXES)
    return lax.ppermute(x, AXES, [(i, (i + (1 if (i % 2 == 0) != far else -1)) % size) for i in range(size)])


def everyone(payload, shape):
    devices = lax.axis_size(AXES)
    return lax.all_to_all(payload.reshape((devices,) + shape), AXES, 0, 0, tiled=True).reshape(-1, 128)


def per_device(forcing, kappa, elem_order):
    devices = lax.axis_size(AXES)
    nodes, face, face_row = (2, 512, 128), (2, 56, 128), (2, 64, 128)
    plane, grid, flat = (8, PLANE), (devices, PLANE), (512, PLANE)
    edge, stored, choice = (2, 128, 128), (PLANE, 512), ((PLANE, PLANE), jnp.bfloat16)
    table = jnp.asarray(np.concatenate([STIFF_PARTS[k] for k in (0, 0, 1, 1, 0, 2)], 1), jnp.bfloat16)
    long = pl.CostEstimate(flops=10**11, bytes_accessed=2**28, transcendentals=0)
    payload_rows = (devices * 6, 128)
    load, far, near, own, payload = call(
        opening,
        [nodes, face_row, face_row, plane, payload_rows],
        [(2, PLANE, 256), (1, PLANE), ((1, PLANE), jnp.int32), payload_rows],
        5,
        hbm_in=(0, 1, 2),
        hbm_out=(4,),
        inputs=3,
    )(*(pltpu.with_memory_space_constraint(x, pltpu.HBM) for x in (forcing, kappa.reshape(1, PLANE), elem_order)))
    far, near = swapped(far, True), swapped(near, False)
    (payload,) = call(
        late_payload, [payload_rows], [payload_rows], 1, in_place={2: 0}, hbm_in=(2,), hbm_out=(0,), inputs=3
    )(load, own, payload)
    gather = everyone(payload, (3, 2, 128))
    resid, scaled, image, layers, lower, far, near = call(
        first_faces, [nodes, nodes, nodes, plane, plane, face_row, face_row], [flat], cost=long, in_place={0: 0}
    )(load, far, near, own, table)
    far, near = swapped(far, True), swapped(near, False)
    vert, target, scale, coeff, smooth = call(first_coarse, [grid] * 4 + [nodes], [edge])(gather, layers)
    scaled_change, change, sums, planes, column_planes, outer = call(
        second_rough, [nodes] * 2 + [(48, PLANE), plane, (128, PLANE), (128, PLANE)], [flat, nodes], in_place={1: 0}
    )(image, smooth, layers, table, resid, scaled)
    added, next_far, next_near, payload = call(
        second_faces, [(128, PLANE), face, face, (devices * 7, 128)], [edge, (64, 2 * PLANE)]
    )(image, scaled_change, change, outer, far, near, layers, table, scaled, lower, sums, planes, column_planes)
    step = everyone(payload, (7, 1, 128))
    next_far, next_near = swapped(next_far, True), swapped(next_near, False)
    image, scaled_change, change, z, choose, applied = call(
        complete,
        [nodes] * 4 + [choice, grid],
        [(2, 256, 128), nodes, edge],
        in_place={0: 0, 1: 1, 2: 2, 3: 3},
    )(image, scaled_change, change, scaled, far, near, added, layers, coeff, vert)
    found, left = call(closing, [stored, stored], [grid, flat, nodes, edge, (2,) + stored], 2, hbm_out=(0, 1))(
        coeff, step, vert, applied, target, scale, layers,
        resid, z, image, scaled_change, change, next_far, next_near, choose,
    )
    return found, left


def solution(mesh):
    in_specs = (P(AXES, None), P(AXES), P(AXES, None))
    out_specs = (P(AXES, None), P(AXES, None))
    return jax.shard_map(
        per_device, mesh=mesh, in_specs=in_specs, out_specs=out_specs, check_vma=False
    )
```

```python
import functools
import math

import jax
import jax.numpy as jnp
import ml_dtypes
import numpy as np
from jax import lax
from jax.experimental import pallas as pl
from jax.experimental.pallas import tpu as pltpu
from jax.sharding import PartitionSpec as P

EX = 8
EY = 32
PLANE = EX * EY
SWEEPS = 4
REACT = 0.02
OMEGA = 0.6
AXES = ("elem", "face")
F32 = jnp.float32


def legendre_seven(points):
    before = np.ones(8)
    current = np.array(points)
    for degree in range(1, 7):
        following = ((2 * degree + 1) * points * current - degree * before) / (degree + 1)
        before = current
        current = following
    return current


def line_tables():
    points = np.array(
        [
            -1.0,
            -0.8717401485096066,
            -0.5917001814331423,
            -0.2092992179024789,
            0.2092992179024789,
            0.5917001814331423,
            0.8717401485096066,
            1.0,
        ]
    )
    weights = np.array(
        [
            1.0 / 28.0,
            0.2107042271435061,
            0.3411226924835044,
            0.4124587946587038,
            0.4124587946587038,
            0.3411226924835044,
            0.2107042271435061,
            1.0 / 28.0,
        ]
    )
    legendre = legendre_seven(points)
    derivative = np.zeros((8, 8))
    for left_node in range(8):
        for right_node in range(8):
            if left_node != right_node:
                derivative[left_node, right_node] = legendre[left_node] / (
                    legendre[right_node] * (points[left_node] - points[right_node])
                )
    derivative[0, 0] = -14.0
    derivative[7, 7] = 14.0
    stiffness = derivative.T @ (weights[:, None] * derivative)
    return points, weights, stiffness


POINTS, WEIGHTS, STIFF = line_tables()
DIAG = np.diag(STIFF)
ENDS = np.array([2.0] + [1.0] * 6 + [2.0])
MASS = np.diag(WEIGHTS)
STIFF_XY = np.kron(MASS, STIFF) + np.kron(STIFF, MASS)
STIFF_PARTS = []
for part in range(3):
    STIFF_PARTS.append((STIFF_XY - sum(STIFF_PARTS)).astype(ml_dtypes.bfloat16).astype(np.float64))
INTERP = np.stack([(1.0 - POINTS) / 2.0, (1.0 + POINTS) / 2.0], 1)
LINE_MASS = INTERP.T @ (WEIGHTS[:, None] * INTERP)
LINE_STIFF = INTERP.T @ STIFF @ INTERP
MASS_SUM = (LINE_MASS[0, 0] + LINE_MASS[0, 1]) / 2.0
MASS_DIF = (LINE_MASS[0, 0] - LINE_MASS[0, 1]) / 2.0
STIFF_DIF = LINE_STIFF[0, 0]
MODE_STIFF = [
    0.0,
    STIFF_DIF * MASS_SUM**2,
    2.0 * STIFF_DIF * MASS_DIF * MASS_SUM,
    3.0 * STIFF_DIF * MASS_DIF**2,
]
MODE_MASS = [MASS_SUM ** (3 - j) * MASS_DIF**j for j in range(4)]
CORNER_STIFF = 3.0 * LINE_STIFF[0, 0] * LINE_MASS[0, 0] ** 2
CORNER_MASS = LINE_MASS[0, 0] ** 3


def lane(shape):
    return lax.broadcasted_iota(jnp.int32, shape, len(shape) - 1)


def next_x(v):
    return jnp.where(lane(v.shape) % EX == EX - 1, pltpu.roll(v, EX - 1, 1), pltpu.roll(v, PLANE - 1, 1))


def prev_x(v):
    return jnp.where(lane(v.shape) % EX == 0, pltpu.roll(v, PLANE - EX + 1, 1), pltpu.roll(v, 1, 1))


def next_y(v):
    return pltpu.roll(v, PLANE - EX, 1)


def prev_y(v):
    return pltpu.roll(v, EX, 1)


def next_xy(v):
    return jnp.where(lane(v.shape) % EX == EX - 1, pltpu.roll(v, PLANE - 1, 1), pltpu.roll(v, PLANE - EX - 1, 1))


def prev_xy(v):
    return jnp.where(lane(v.shape) % EX == 0, pltpu.roll(v, 1, 1), pltpu.roll(v, EX + 1, 1))


def next_z(v):
    half = v.shape[0] // 2
    return jnp.concatenate([v[half:], pltpu.roll(v[:half], half - 1, 0)], axis=0)


def prev_z(v):
    half = v.shape[0] // 2
    return jnp.concatenate([pltpu.roll(v[half:], 1, 0), v[:half]], axis=0)


def plane_row(layer, planes):
    layer = lax.rem(layer + planes, planes)
    return pl.ds(lax.div(layer, 2) + lax.rem(layer, 2) * (planes // 2), 1)


def column(values):
    row = lax.broadcasted_iota(jnp.int32, (8, PLANE), 0)
    out = jnp.full((8, PLANE), float(values[0]), F32)
    for k in range(1, 8):
        out = jnp.where(row == k, float(values[k]), out)
    return out


def rows_of(nz, ny):
    start = (nz * 8 + ny) * 8
    return slice(start, start + 8)


def get(ref, rows):
    return jnp.concatenate([ref[0, rows, :], ref[1, rows, :]], axis=1)


def put(ref, rows, value):
    ref[0, rows, :] = value[:, :128]
    ref[1, rows, :] = value[:, 128:]


def sum_xy(ref):
    planes = ref.shape[1] // 64
    first, last = pl.ds(0, planes * 8, stride=8), pl.ds(7, planes * 8, stride=8)
    shared = get(ref, last) + next_x(get(ref, first))
    put(ref, last, shared)
    put(ref, first, prev_x(shared))
    for nz in range(planes):
        shared = get(ref, rows_of(nz, 7)) + next_y(get(ref, rows_of(nz, 0)))
        put(ref, rows_of(nz, 7), shared)
        put(ref, rows_of(nz, 0), prev_y(shared))


def restrict(ref, points):
    sums_z, difs_z = [], []
    for ny in range(8):
        tiles = [get(ref, rows_of(nz, ny)) for nz in range(8)]
        sums_z.append(functools.reduce(lambda a, b: a + b, tiles))
        difs_z.append(sum(float(POINTS[7 - k]) * (tiles[7 - k] - tiles[k]) for k in range(4)))
    return restrict_xy(sums_z, difs_z, points)


def restrict_summed(ref, points):
    inv_ends = column(1.0 / ENDS)
    sums_z, difs_z = [], []
    for ny in range(8):
        tiles = [get(ref, rows_of(nz, ny)) for nz in range(8)]
        share = inv_ends * float(1.0 / ENDS[ny])
        sums_z.append(functools.reduce(lambda a, b: a + b, tiles) * share)
        difs_z.append(sum(float(POINTS[7 - k]) * (tiles[7 - k] - tiles[k]) for k in range(4)) * share)
    return restrict_xy(sums_z, difs_z, points)


def restrict_xy(sums_z, difs_z, points):
    planes = []
    for parts in (sums_z, difs_z):
        total = functools.reduce(lambda a, b: a + b, parts)
        slope = sum(float(POINTS[7 - k]) * (parts[7 - k] - parts[k]) for k in range(4))
        in_y = []
        for part in (total, slope):
            flat = jnp.sum(part, axis=0, keepdims=True)
            steep = jnp.sum(part * points, axis=0, keepdims=True)
            in_y.append((flat - steep) + prev_x(flat + steep))
        planes.append((in_y[0] - in_y[1]) + prev_y(in_y[0] + in_y[1]))
    return (planes[0] - planes[1]) * 0.125, (planes[0] + planes[1]) * 0.125


def both(v, following):
    after = following(v)
    return after + v, after - v


def both_back(total, dif, preceding):
    return (total - dif) + preceding(total + dif)


def coarse_modes(coeff):
    return [float(REACT * MODE_MASS[0])] + [
        float(MODE_STIFF[j]) * coeff + float(REACT * MODE_MASS[j]) for j in range(1, 4)
    ]


def coarse_tables(coeff):
    near = coeff + prev_x(coeff)
    near = near + prev_y(near)
    near = near + prev_z(near)
    scale = float(OMEGA) / (float(CORNER_STIFF) * near + float(8.0 * REACT * CORNER_MASS))
    return coarse_modes(coeff), scale


def coarse_apply(vert, modes):
    after_x, after_y, after_xy = next_x(vert), next_y(vert), next_xy(vert)
    in_x = [(after_x + vert, after_xy + after_y), (after_x - vert, after_xy - after_y)]
    back = []
    for jx in range(2):
        first, second = in_x[jx]
        for jy, in_y in enumerate((second + first, second - first)):
            in_z = both(in_y, next_z)
            scaled = [modes[jx + jy + jz] * in_z[jz] for jz in range(2)]
            back.append(both_back(scaled[0], scaled[1], prev_z))
    ss, sd, ds, dd = back
    low, high = (ss - sd, ss + sd), (ds - dd, ds + dd)
    return ((low[0] - high[0]) + prev_x(low[0] + high[0])) + (prev_y(low[1] - high[1]) + prev_xy(low[1] + high[1]))


def coarse_solve(target, modes, scale):
    vert = scale * target
    for _ in range(SWEEPS - 1):
        vert = vert + scale * (target - coarse_apply(vert, modes))
    return vert


def gathered_rows(ref, row, size):
    chips = ref.shape[0] // (2 * size)
    return jnp.concatenate([ref[pl.ds(core * size + row, chips, stride=2 * size), :] for core in range(2)], axis=0)


def gathered(ref, k, size):
    return jnp.concatenate([gathered_rows(ref, 2 * k + h, size) for h in range(2)], axis=1)


def halves(row):
    return [row[:, :128], row[:, 128:]]


def send(ref, rows):
    count = len(rows)
    times = 8 // math.gcd(count, 8)
    block = jnp.concatenate(rows * times, axis=0)
    for k in range(0, ref.shape[0], count * times):
        ref[k : k + count * times, :] = block


def layer_modes(vert_ref, shift):
    me, devices = my_layer(), vert_ref.shape[0]
    lower, upper = (vert_ref[plane_row(me + shift + k, devices), :] for k in range(2))
    modes = []
    for along_z in (upper + lower, upper - lower):
        for along_y in both(along_z, next_y):
            modes += both(along_y, next_x)
    return 0.125 * jnp.concatenate(modes, axis=0)


class Smooth:
    def __init__(self, modes, coeff, points, weight_x):
        row = lax.broadcasted_iota(jnp.int32, (8, PLANE), 0)
        ends = jnp.where(row == 0, -1.0, jnp.where(row == 7, 1.0, 0.0))
        m = [[[modes[4 * z + 2 * y + x : 4 * z + 2 * y + x + 1] for x in range(2)] for y in range(2)] for z in range(2)]
        self.xy = [[m[z][y][0] + m[z][y][1] * points for y in range(2)] for z in range(2)]
        self.dx = [[m[z][y][1] for y in range(2)] for z in range(2)]
        self.ends_coeff = ends * coeff
        self.weight_coeff = weight_x * coeff
        self.mass = float(REACT) * weight_x

    def value(self, nz, ny):
        by_y = [self.xy[z][0] + float(POINTS[ny]) * self.xy[z][1] for z in range(2)]
        return by_y[0] + float(POINTS[nz]) * by_y[1]

    def operated(self, nz, ny, value):
        wy, wz, py, pz = (float(t) for t in (WEIGHTS[ny], WEIGHTS[nz], POINTS[ny], POINTS[nz]))
        slope = (self.dx[0][0] + py * self.dx[0][1]) + pz * (self.dx[1][0] + py * self.dx[1][1])
        out = self.ends_coeff * (slope * (wy * wz)) + (self.mass * (wy * wz)) * value
        flux = None
        if ny in (0, 7):
            flux = (self.xy[0][1] + pz * self.xy[1][1]) * (wz * py)
        if nz in (0, 7):
            along = (self.xy[1][0] + py * self.xy[1][1]) * (wy * pz)
            flux = along if flux is None else flux + along
        return out if flux is None else out + self.weight_coeff * flux


def kappa_sums(own, below, above):
    row = lax.broadcasted_iota(jnp.int32, (8, PLANE), 0)
    table = []
    for along_z in (own + below, own, own + above):
        in_z = []
        for along_y in (along_z + prev_y(along_z), along_z, along_z + next_y(along_z)):
            first = along_y + prev_x(along_y)
            last = along_y + next_x(along_y)
            in_z.append(jnp.where(row == 0, first, jnp.where(row == 7, last, along_y)))
        table.append(in_z)
    return table


def kind(node):
    return 0 if node == 0 else (2 if node == 7 else 1)


def product(table, values):
    low, middle, high = pieces(values)
    stacked = jnp.concatenate([high, middle, high, middle, low, high], axis=0)
    return jnp.dot(table, stacked, preferred_element_type=F32)


def operate(z_ref, xy_ref, out_ref, table_ref, coeff, weight_x):
    for nz in range(8):
        rows = slice(64 * nz, 64 * nz + 64)
        xy_ref[rows, :] = product(table_ref[...], get(z_ref, rows))
    for ny in range(8):
        tiles = [get(z_ref, rows_of(nz, ny)) for nz in range(8)]
        even = [tiles[k] + tiles[7 - k] for k in range(4)]
        odd = [tiles[k] - tiles[7 - k] for k in range(4)]
        for nz in range(4):
            even_part = sum(float((STIFF[nz, k] + STIFF[nz, 7 - k]) / 2) * even[k] for k in range(4))
            odd_part = sum(float((STIFF[nz, k] - STIFF[nz, 7 - k]) / 2) * odd[k] for k in range(4))
            for node, term in ((nz, even_part + odd_part), (7 - nz, even_part - odd_part)):
                area = weight_x * float(WEIGHTS[ny])
                local = coeff * (
                    float(WEIGHTS[node]) * xy_ref[rows_of(node, ny), :] + area * term
                ) + (float(REACT * WEIGHTS[node]) * area) * tiles[node]
                put(out_ref, rows_of(node, ny), local)


def fine_diag(sums, nz, ny, weight_x, diag_x, ends_x):
    wy, wz, ky, kz = (float(t) for t in (WEIGHTS[ny], WEIGHTS[nz], DIAG[ny], DIAG[nz]))
    stiff = diag_x * (wy * wz) + weight_x * (ky * wz + wy * kz)
    mass = (weight_x * ends_x) * float(REACT * wy * wz * ENDS[ny] * ENDS[nz])
    return sums[kind(nz)][kind(ny)] * stiff + mass


def my_layer():
    return lax.axis_index("elem") * lax.axis_size("face") + lax.axis_index("face")


def face_rows(ref):
    even = lax.rem(my_layer(), 2) == 0
    last = ref.shape[1] - 64
    near = pl.multiple_of(jnp.where(even, last, 0), 64)
    far = pl.multiple_of(jnp.where(even, 0, last), 64)
    return pl.ds(near, 64), pl.ds(far, 64)


def faces_out(ref, near_ref, far_ref):
    for rows, out_ref in zip(face_rows(ref), (near_ref, far_ref)):
        out_ref[:, 0:56, :] = ref[:, pl.ds(rows.start, 56), :]


def face_in(ref):
    return jnp.concatenate([get(ref, slice(0, 56)), next_y(get(ref, slice(0, 8)))], axis=0)


def faces_in(ref, near_ref, far_ref):
    for rows, in_ref in zip(face_rows(ref), (near_ref, far_ref)):
        put(ref, rows, get(ref, rows) + face_in(in_ref))


def columns_of_nodes():
    return column(POINTS), column(WEIGHTS), column(DIAG), column(ENDS)


def pieces(v):
    high = v.astype(jnp.bfloat16)
    rest = v - high.astype(F32)
    middle = rest.astype(jnp.bfloat16)
    low = (rest - middle.astype(F32)).astype(jnp.bfloat16)
    return low, middle, high


def selection(order):
    place = lax.broadcasted_iota(jnp.int32, (PLANE, PLANE), 0).astype(order.dtype)
    return jnp.where(place == order, 1.0, 0.0).astype(jnp.bfloat16)


def opening(
    forcing_ref, kappa_ref, order_ref, load_ref, far_ref, near_ref, own_ref, payload_ref,
    held, held_kappa, held_order, held_payload, sems,
):
    small = [
        pltpu.make_async_copy(order_ref, held_order, sems.at[0]),
        pltpu.make_async_copy(kappa_ref, held_kappa, sems.at[1]),
    ]
    parts = [
        pltpu.make_async_copy(forcing_ref.at[:, pl.ds(256 * k, 256)], held.at[k], sems.at[2 + k]) for k in range(2)
    ]
    for copy in small + parts:
        copy.start()
    for copy in small + parts:
        copy.wait()
    order = held_order[...]
    choose = selection(order)
    choose = jnp.concatenate([choose] * 3, axis=1)
    coeff = lax.dot_general(
        jnp.concatenate(pieces(jnp.broadcast_to(held_kappa[...], (8, PLANE))), axis=1),
        choose,
        (((1,), (1,)), ((), ())),
        preferred_element_type=F32,
    )
    own = jnp.concatenate([coeff[0:3], order.astype(F32), coeff[4:8]], axis=0)
    own_ref[...] = own
    for k in range(2):
        load = jnp.dot(choose, jnp.concatenate(pieces(held[k]), axis=0), preferred_element_type=F32)
        put(load_ref, slice(256 * k, 256 * k + 256), load.T)
    sum_xy(load_ref)
    faces_out(load_ref, near_ref, far_ref)
    put(near_ref, slice(56, 64), own)
    put(far_ref, slice(56, 64), own)


    @pl.when(starts_early())
    def _():
        write_payload(load_ref, own_ref, payload_ref, held_payload, sems.at[4])


def starts_early():
    return my_layer() < lax.axis_size("elem") * lax.axis_size("face") // 2


def write_payload(load_ref, own_ref, payload_ref, held, sem):
    lower, upper = restrict_summed(load_ref, column(POINTS))
    send(held, halves(lower) + halves(upper) + halves(own_ref[0:1, :]))
    copy = pltpu.make_async_copy(held, payload_ref, sem)
    copy.start()
    copy.wait()


def late_payload(load_ref, own_ref, _, payload_ref, held, sems):
    @pl.when(jnp.logical_not(starts_early()))
    def _():
        write_payload(load_ref, own_ref, payload_ref, held, sems.at[0])


def below_above(near, far):
    even = lax.rem(my_layer(), 2) == 0
    return jnp.where(even, far, near), jnp.where(even, near, far)


def row_after_face(ref):
    return get(ref, slice(56, 64))[0:1]


def first_faces(
    load_ref, far_in_ref, near_in_ref, own_ref, table_ref,
    resid_ref, scaled_ref, image_ref, layers_ref, lower_ref, far_ref, near_ref, xy_ref,
):
    points, weight_x, _, _ = columns_of_nodes()
    own = own_ref[0:1, :]
    below, above = below_above(row_after_face(near_in_ref), row_after_face(far_in_ref))
    layers_ref[...] = jnp.concatenate([own, below, above, own_ref[3:8, :]], axis=0)
    resid_ref[...] = load_ref[...]
    faces_in(resid_ref, near_in_ref, far_in_ref)
    over_diag(functools.partial(get, resid_ref), scaled_ref, layers_ref)
    operate(scaled_ref, xy_ref, image_ref, table_ref, own, weight_x)
    lower, upper = restrict(image_ref, points)
    sum_xy(image_ref)
    faces_out(image_ref, near_ref, far_ref)
    lower_ref[...] = jnp.broadcast_to(lower, lower_ref.shape)
    put(near_ref, slice(56, 64), jnp.broadcast_to(upper, (8, PLANE)))
    put(far_ref, slice(56, 64), jnp.broadcast_to(upper, (8, PLANE)))


def over_diag(resid, scaled_ref, layers_ref):
    _, weight_x, diag_x, ends_x = columns_of_nodes()
    sums = kappa_sums(*(layers_ref[k : k + 1, :] for k in range(3)))
    for nz in range(8):
        for ny in range(8):
            rows = rows_of(nz, ny)
            put(scaled_ref, rows, resid(rows) / fine_diag(sums, nz, ny, weight_x, diag_x, ends_x))


def three_modes(vert_ref):
    return jnp.concatenate([layer_modes(vert_ref, shift) for shift in (0, -1, 1)], axis=0)


def smooths_of(modes, layers_ref):
    points, weight_x, _, _ = columns_of_nodes()
    return [Smooth(modes[8 * k : 8 * k + 8], layers_ref[k : k + 1, :], points, weight_x) for k in range(3)]


def smooth_image(smooths, out_ref, edge_ref):
    own, below, above = smooths
    for nz in range(8):
        for ny in range(8):
            put(out_ref, rows_of(nz, ny), own.operated(nz, ny, own.value(nz, ny)))
    sum_xy(out_ref)
    for plane, (smooth, nz) in enumerate(((below, 7), (above, 0))):
        for ny in range(8):
            put(edge_ref, rows_of(plane, ny), smooth.operated(nz, ny, smooth.value(nz, ny)))
    sum_xy(edge_ref)
    out_ref[:, 0:64, :] += edge_ref[:, 0:64, :]
    out_ref[:, 448:512, :] += edge_ref[:, 64:128, :]


def first_coarse(coarse_ref, layers_ref, vert_ref, target_ref, scale_ref, coeff_ref, smooth_ref, edge_ref):
    coeff = gathered(coarse_ref, 2, 6)
    coeff_ref[...] = coeff
    modes, scale = coarse_tables(coeff)
    target = gathered(coarse_ref, 0, 6) + prev_z(gathered(coarse_ref, 1, 6))
    vert = coarse_solve(target, modes, scale)
    vert_ref[...] = vert
    target_ref[...] = target
    scale_ref[...] = scale
    smooth_image(smooths_of(three_modes(vert_ref), layers_ref), smooth_ref, edge_ref)


def pack(sums):
    place = lane((8, 128)) // 16
    packed = jnp.zeros((8, 128), F32)
    for k, total in enumerate(sums):
        total = total[:, :128] + total[:, 128:]
        for by in (64, 32, 16):
            total = total + pltpu.roll(total, by, 1)
        packed = jnp.where(place == k, total, packed)
    return jnp.sum(packed, axis=0, keepdims=True)


def second_rough(
    image_ref, smooth_ref, layers_ref, table_ref, resid_ref, scaled_ref,
    scaled_change_ref, change_ref, sums_ref, planes_ref, column_ref, outer_ref, xy_ref, whole_ref,
):
    points, weight_x, _, _ = columns_of_nodes()
    inv_ends = column(1.0 / ENDS)
    whole_ref[...] = image_ref[...] + smooth_ref[...]
    over_diag(functools.partial(get, whole_ref), scaled_change_ref, layers_ref)
    operate(scaled_change_ref, xy_ref, change_ref, table_ref, layers_ref[0:1, :], weight_x)
    planes_ref[...] = jnp.concatenate(list(restrict(change_ref, points)) * 4, axis=0)
    sum_xy(change_ref)
    sums = [jnp.zeros((8, PLANE), F32)] * 6
    for ny in range(8):
        along = [jnp.zeros((8, PLANE), F32)] * 2
        for nz in range(8):
            rows = rows_of(nz, ny)
            share = float(1.0 / (ENDS[nz] * ENDS[ny]))
            scaled, change = get(scaled_ref, rows) * share, get(scaled_change_ref, rows)
            along = [total + float(STIFF[nz, node]) * change for total, node in zip(along, (0, 7))]
            change = change * share
            whole, image = get(whole_ref, rows), get(image_ref, rows)
            terms = [
                scaled * get(resid_ref, rows), scaled * whole, change * whole, scaled * image, change * image,
                change * (get(change_ref, rows) * float(ENDS[nz])),
            ]
            sums = [total + term for total, term in zip(sums, terms)]
        for k in range(2):
            column_ref[64 * k + 8 * ny : 64 * k + 8 * ny + 8, :] = along[k]
    sums_ref[...] = jnp.concatenate([total * inv_ends for total in sums], axis=0)
    for k, rows in enumerate((slice(0, 64), slice(448, 512))):
        outer_ref[64 * k : 64 * k + 64, :] = get(whole_ref, rows)


def second_faces(
    image_ref, scaled_change_ref, change_ref, outer_ref, far_in_ref, near_in_ref, layers_ref, table_ref,
    scaled_ref, lower_ref, sums_ref, planes_ref, column_ref,
    added_ref, far_ref, near_ref, payload_ref, edge_ref, xy_ref,
):
    points, weight_x, _, _ = columns_of_nodes()
    inv_ends = column(1.0 / ENDS)
    even = lax.rem(my_layer(), 2) == 0
    own = layers_ref[0:1, :]
    kappas = kappa_sums(*(layers_ref[k : k + 1, :] for k in range(3)))
    faces = below_above(face_in(near_in_ref), face_in(far_in_ref))
    tiles = [slice(8 * ny, 8 * ny + 8) for ny in range(8)]
    added = added_by(faces, kappas, columns_of_nodes())
    xy_ref[...] = product(table_ref[...], jnp.concatenate(added, axis=1))
    along, at_face = [], []
    for k in range(2):
        along.append(local_along(own, weight_x, added[k]))
        flux = own * xy_ref[:, PLANE * k : PLANE * k + PLANE]
        at_face.append(float(WEIGHTS[0]) * jnp.concatenate(
            [flux[t] + (float(REACT * WEIGHTS[ny]) * weight_x) * added[k][t] for ny, t in enumerate(tiles)], axis=0
        ))
    local = [
        (float(STIFF[nz, 0]) * along[0] + float(STIFF[nz, 7]) * along[1]) + at_face[k] for k, nz in enumerate((0, 7))
    ]
    flat = at_face[0] + at_face[1]
    slope = (along[1] + at_face[1]) - (along[0] + at_face[0])
    lower, upper = restrict_xy([flat[t] for t in tiles], [slope[t] for t in tiles], points)
    lower, upper = lower + planes_ref[0:1, :], upper + planes_ref[1:2, :]
    sums = [jnp.zeros((8, PLANE), F32)] * 5
    energy = jnp.zeros((8, PLANE), F32)
    planes = [slice(0, 64), slice(448, 512)]
    for k in range(2):
        s_plane, q_plane, i_plane, c_plane = (
            get(ref, planes[k]) for ref in (scaled_ref, scaled_change_ref, image_ref, change_ref)
        )
        w_plane = outer_ref[64 * k : 64 * k + 64, :]
        for ny in range(8):
            tile = tiles[ny]
            share = float(1.0 / ENDS[ny])
            half = share * float(1.0 / ENDS[0])
            face = faces[k][tile]
            s, q, dq = s_plane[tile] * half, q_plane[tile] * half, added[k][tile] * half
            sums[0] = sums[0] + s * face
            sums[1] = sums[1] + (q * face + dq * (w_plane[tile] + face))
            sums[2] = sums[2] + s * face
            sums[3] = sums[3] + (q * face + dq * (i_plane[tile] + face))
            sums[4] = sums[4] + (added[k][tile] * c_plane[tile]) * share
            energy = energy + (
                column_ref[64 * k + 8 * ny : 64 * k + 8 * ny + 8, :] * along[k][tile]
                + q_plane[tile] * at_face[k][tile]
                + added[k][tile] * local[k][tile]
            )
    sums = [sums_ref[8 * k + 8 : 8 * k + 16, :] + sums[k] * inv_ends for k in range(5)]
    sums = pack([sums_ref[0:8, :]] + sums[:4] + [sums[4] + energy])
    below, _ = below_above(row_after_face(near_in_ref), row_after_face(far_in_ref))
    send(payload_ref, halves(lower_ref[0:1, :] + below) + halves(lower) + halves(upper) + [sums])
    for k in range(2):
        put(edge_ref, slice(64 * k, 64 * k + 64), local[k])
        added_ref[64 * k : 64 * k + 64, :] = at_face[k]
    sum_xy(edge_ref)
    change = [(get(change_ref, planes[k]) + get(edge_ref, slice(64 * k, 64 * k + 64)))[0:56] for k in range(2)]
    put(far_ref, slice(0, 56), jnp.where(even, change[0], change[1]))
    put(near_ref, slice(0, 56), jnp.where(even, change[1], change[0]))


def local_along(own, weight_x, added):
    return own * jnp.concatenate(
        [(weight_x * float(WEIGHTS[ny])) * added[8 * ny : 8 * ny + 8] for ny in range(8)], axis=0
    )


def added_by(faces, kappas, columns):
    _, weight_x, diag_x, ends_x = columns
    return [
        jnp.concatenate(
            [
                face[8 * ny : 8 * ny + 8] / fine_diag(kappas, nz, ny, weight_x, diag_x, ends_x)
                for ny in range(8)
            ],
            axis=0,
        )
        for nz, face in zip((0, 7), faces)
    ]


def complete(
    first_ref, first_scaled_ref, first_change_ref, rough_ref, far_in_ref, near_in_ref, at_face_ref, layers_ref, coeff_ref,
    vert_ref, image_ref, scaled_change_ref, change_ref, z_ref, choose_ref, applied_ref, edge_ref, smooth_ref, sides_ref,
):
    columns = columns_of_nodes()
    applied_ref[...] = coarse_apply(vert_ref[...], coarse_modes(coeff_ref[...]))
    smooths = smooths_of(three_modes(vert_ref), layers_ref)
    for nz in range(8):
        for ny in range(8):
            rows = rows_of(nz, ny)
            put(z_ref, rows, get(rough_ref, rows) + smooths[0].value(nz, ny))
    smooth_image(smooths, smooth_ref, sides_ref)
    choose_ref[...] = selection(layers_ref[3:4, :]).astype(F32).T.astype(jnp.bfloat16)
    image_ref[...] = first_ref[...] + smooth_ref[...]
    scaled_change_ref[...] = first_scaled_ref[...]
    faces_in(image_ref, near_in_ref, far_in_ref)
    kappas = kappa_sums(*(layers_ref[k : k + 1, :] for k in range(3)))
    added = added_by(below_above(face_in(near_in_ref), face_in(far_in_ref)), kappas, columns)
    for k, rows in enumerate((slice(0, 64), slice(448, 512))):
        put(scaled_change_ref, rows, get(scaled_change_ref, rows) + added[k])
        put(edge_ref, slice(64 * k, 64 * k + 64), local_along(layers_ref[0:1, :], columns[1], added[k]))
        put(edge_ref, slice(128 + 64 * k, 192 + 64 * k), at_face_ref[64 * k : 64 * k + 64, :])
    sum_xy(edge_ref)
    along = [get(edge_ref, slice(64 * k, 64 * k + 64)) for k in range(2)]
    for nz in range(8):
        rows = slice(64 * nz, 64 * nz + 64)
        new = get(first_change_ref, rows) + (float(STIFF[nz, 0]) * along[0] + float(STIFF[nz, 7]) * along[1])
        if nz in (0, 7):
            new = new + get(edge_ref, slice(128 + 64 * (nz // 7), 192 + 64 * (nz // 7)))
        put(change_ref, rows, new)


def folded(value):
    return functools.reduce(lambda a, b: a + b, [value[k : k + 8] for k in range(0, value.shape[0], 8)])


def to_stored(choose, value):
    return lax.dot_general(
        jnp.concatenate([choose] * 2, axis=1),
        jnp.concatenate(pieces(value)[1:], axis=1),
        (((1,), (1,)), ((), ())),
        preferred_element_type=F32,
    )


def second_step(
    resid_ref, coeff_ref, step_ref, first_ref, applied_ref, target_ref, scale_ref, layers_ref,
    z_ref, image_ref, scaled_change_ref, change_ref, choose_ref,
    rest_ref, found_ref, scalars_ref, vert_ref, grid_ref, sum_ref, edge_ref,
):
    modes = coarse_modes(coeff_ref[...])
    target, first, applied = target_ref[...], first_ref[...], applied_ref[...]
    rough, rough_change = gathered(step_ref, 0, 7), gathered(step_ref, 1, 7) + prev_z(gathered(step_ref, 2, 7))
    parts = folded(gathered_rows(step_ref, 6, 7))
    sums = [parts] + [pltpu.roll(parts, 128 - 16 * k, 1) for k in range(1, 6)]
    used = lane(parts.shape) < 16

    def total(fine, coarse):
        coarse = folded(coarse)
        return jnp.sum(jnp.where(used, fine, 0.0) + (coarse[:, :128] + coarse[:, 128:]), keepdims=True)

    image = rough + applied
    change = coarse_solve(image, modes, scale_ref[...])
    vert_ref[...] = change
    smooths = smooths_of(three_modes(vert_ref), layers_ref)
    change_applied = coarse_apply(change, modes)
    gamma = total(sums[0], target * first)
    energy = total(sums[3], first * (2.0 * rough + applied))
    alpha = gamma / energy
    vert = first - alpha * change
    progress = total(sums[0] - alpha * (2.0 * sums[1] - alpha * sums[2]), (target - alpha * image) * vert)
    second = total(
        sums[3] - alpha * (2.0 * sums[4] - alpha * sums[5]),
        vert * (2.0 * (rough - alpha * rough_change) + (applied - alpha * change_applied)),
    )
    cross = total(sums[1] - alpha * sums[2], vert * image)
    smooth_image(smooths, sum_ref, edge_ref)
    beta = progress / gamma
    alpha_next = progress / (second + beta * (2.0 * cross + beta * energy))
    share, change_share = alpha + alpha_next * beta + alpha_next, alpha_next * alpha
    scalars_ref[...] = jnp.broadcast_to(change_share, scalars_ref.shape)
    for nz in range(8):
        for ny in range(8):
            rows = rows_of(nz, ny)
            other = get(scaled_change_ref, rows) + smooths[0].value(nz, ny)
            grid_ref[rows, :] = share * get(z_ref, rows) - change_share * other
    found_ref[...] = to_stored(choose_ref[...], grid_ref[...])
    rest_ref[...] = (
        resid_ref[...] - share[None] * image_ref[...] + change_share[None] * (change_ref[...] + sum_ref[...])
    )


def closing(
    found_ref, rest_ref, far_ref, near_ref, scalars_ref, choose_ref, solution_ref, residual_ref, sum_ref, held, sems
):
    copies = [pltpu.make_async_copy(found_ref, solution_ref, sems.at[0])]
    copies[0].start()
    sum_ref[...] = rest_ref[...]
    for rows, ref in zip(face_rows(sum_ref), (near_ref, far_ref)):
        put(sum_ref, rows, get(sum_ref, rows) + scalars_ref[0:1, 0:1] * face_in(ref))
    held[...] = to_stored(choose_ref[...], get(sum_ref, slice(0, 512)))
    copies.append(pltpu.make_async_copy(held, residual_ref, sems.at[1]))
    copies[1].start()
    for copy in copies:
        copy.wait()


def call(kernel, outs, scratch=(), sems=0, cost=None, in_place=None, hbm_in=(), hbm_out=(), inputs=0):
    def specs(count, far):
        return [pl.BlockSpec(memory_space=pltpu.HBM if k in far else pltpu.VMEM) for k in range(count)]

    more = {"in_specs": specs(inputs, hbm_in)} if hbm_in else {}
    return pl.pallas_call(
        kernel,
        out_shape=[jax.ShapeDtypeStruct(*(s if isinstance(s[0], tuple) else (s, F32))) for s in outs],
        out_specs=specs(len(outs), hbm_out),
        scratch_shapes=[pltpu.VMEM(*(s if isinstance(s[0], tuple) else (s, F32))) for s in scratch]
        + ([pltpu.SemaphoreType.DMA((sems,))] if sems else []),
        compiler_params=pltpu.CompilerParams(vmem_limit_bytes=12 * 1024 * 1024),
        cost_estimate=cost,
        input_output_aliases=in_place or {},
        **more,
    )


def swapped(x, far):
    size = lax.axis_size(AXES)
    return lax.ppermute(x, AXES, [(i, (i + (1 if (i % 2 == 0) != far else -1)) % size) for i in range(size)])


def everyone(payload, shape):
    devices = lax.axis_size(AXES)
    return lax.all_to_all(payload.reshape((devices,) + shape), AXES, 0, 0, tiled=True).reshape(-1, 128)


def per_device(forcing, kappa, elem_order):
    devices = lax.axis_size(AXES)
    nodes, face, face_row = (2, 512, 128), (2, 56, 128), (2, 64, 128)
    plane, grid, flat = (8, PLANE), (devices, PLANE), (512, PLANE)
    edge, stored, choice = (2, 128, 128), (PLANE, 512), ((PLANE, PLANE), jnp.bfloat16)
    table = jnp.asarray(np.concatenate([STIFF_PARTS[k] for k in (0, 0, 1, 1, 0, 2)], 1), jnp.bfloat16)
    long = pl.CostEstimate(flops=10**11, bytes_accessed=2**28, transcendentals=0)
    payload_rows = (devices * 6, 128)
    load, far, near, own, payload = call(
        opening,
        [nodes, face_row, face_row, plane, payload_rows],
        [(2, PLANE, 256), (1, PLANE), ((1, PLANE), jnp.int32), payload_rows],
        5,
        hbm_in=(0, 1, 2),
        hbm_out=(4,),
        inputs=3,
    )(*(pltpu.with_memory_space_constraint(x, pltpu.HBM) for x in (forcing, kappa.reshape(1, PLANE), elem_order)))
    far, near = swapped(far, True), swapped(near, False)
    (payload,) = call(
        late_payload, [payload_rows], [payload_rows], 1, in_place={2: 0}, hbm_in=(2,), hbm_out=(0,), inputs=3
    )(load, own, payload)
    gather = everyone(payload, (3, 2, 128))
    resid, scaled, image, layers, lower, far, near = call(
        first_faces, [nodes, nodes, nodes, plane, plane, face_row, face_row], [flat], cost=long, in_place={0: 0}
    )(load, far, near, own, table)
    far, near = swapped(far, True), swapped(near, False)
    vert, target, scale, coeff, smooth = call(first_coarse, [grid] * 4 + [nodes], [edge])(gather, layers)
    scaled_change, change, sums, planes, column_planes, outer = call(
        second_rough, [nodes] * 2 + [(48, PLANE), plane, (128, PLANE), (128, PLANE)], [flat, nodes], in_place={1: 0}
    )(image, smooth, layers, table, resid, scaled)
    added, next_far, next_near, payload = call(
        second_faces, [(128, PLANE), face, face, (devices * 7, 128)], [edge, (64, 2 * PLANE)]
    )(image, scaled_change, change, outer, far, near, layers, table, scaled, lower, sums, planes, column_planes)
    step = everyone(payload, (7, 1, 128))
    next_far, next_near = swapped(next_far, True), swapped(next_near, False)
    image, scaled_change, change, z, choose, applied = call(
        complete,
        [nodes] * 4 + [choice, grid],
        [(2, 256, 128), nodes, edge],
        in_place={0: 0, 1: 1, 2: 2, 3: 3},
    )(image, scaled_change, change, scaled, far, near, added, layers, coeff, vert)
    rest, found, scalars = call(
        second_step, [nodes, stored, (8, 128)], [grid, flat, nodes, edge], in_place={0: 0}
    )(resid, coeff, step, vert, applied, target, scale, layers, z, image, scaled_change, change, choose)
    found, left = call(closing, [stored, stored], [nodes, stored], 2, hbm_out=(0, 1))(
        found, rest, next_far, next_near, scalars, choose
    )
    return found, left


def solution(mesh):
    in_specs = (P(AXES, None), P(AXES), P(AXES, None))
    out_specs = (P(AXES, None), P(AXES, None))
    return jax.shard_map(
        per_device, mesh=mesh, in_specs=in_specs, out_specs=out_specs, check_vma=False
    )
```

```python
import functools
import math

import jax
import jax.numpy as jnp
import ml_dtypes
import numpy as np
from jax import lax
from jax.experimental import pallas as pl
from jax.experimental.pallas import tpu as pltpu
from jax.sharding import PartitionSpec as P

EX = 8
EY = 32
PLANE = EX * EY
SWEEPS = 4
REACT = 0.02
OMEGA = 0.6
AXES = ("elem", "face")
F32 = jnp.float32


def legendre_seven(points):
    before = np.ones(8)
    current = np.array(points)
    for degree in range(1, 7):
        following = ((2 * degree + 1) * points * current - degree * before) / (degree + 1)
        before = current
        current = following
    return current


def line_tables():
    points = np.array(
        [
            -1.0,
            -0.8717401485096066,
            -0.5917001814331423,
            -0.2092992179024789,
            0.2092992179024789,
            0.5917001814331423,
            0.8717401485096066,
            1.0,
        ]
    )
    weights = np.array(
        [
            1.0 / 28.0,
            0.2107042271435061,
            0.3411226924835044,
            0.4124587946587038,
            0.4124587946587038,
            0.3411226924835044,
            0.2107042271435061,
            1.0 / 28.0,
        ]
    )
    legendre = legendre_seven(points)
    derivative = np.zeros((8, 8))
    for left_node in range(8):
        for right_node in range(8):
            if left_node != right_node:
                derivative[left_node, right_node] = legendre[left_node] / (
                    legendre[right_node] * (points[left_node] - points[right_node])
                )
    derivative[0, 0] = -14.0
    derivative[7, 7] = 14.0
    stiffness = derivative.T @ (weights[:, None] * derivative)
    return points, weights, stiffness


POINTS, WEIGHTS, STIFF = line_tables()
DIAG = np.diag(STIFF)
ENDS = np.array([2.0] + [1.0] * 6 + [2.0])
MASS = np.diag(WEIGHTS)
STIFF_XY = np.kron(MASS, STIFF) + np.kron(STIFF, MASS)
STIFF_PARTS = []
for part in range(3):
    STIFF_PARTS.append((STIFF_XY - sum(STIFF_PARTS)).astype(ml_dtypes.bfloat16).astype(np.float64))
INTERP = np.stack([(1.0 - POINTS) / 2.0, (1.0 + POINTS) / 2.0], 1)
LINE_MASS = INTERP.T @ (WEIGHTS[:, None] * INTERP)
LINE_STIFF = INTERP.T @ STIFF @ INTERP
MASS_SUM = (LINE_MASS[0, 0] + LINE_MASS[0, 1]) / 2.0
MASS_DIF = (LINE_MASS[0, 0] - LINE_MASS[0, 1]) / 2.0
STIFF_DIF = LINE_STIFF[0, 0]
MODE_STIFF = [
    0.0,
    STIFF_DIF * MASS_SUM**2,
    2.0 * STIFF_DIF * MASS_DIF * MASS_SUM,
    3.0 * STIFF_DIF * MASS_DIF**2,
]
MODE_MASS = [MASS_SUM ** (3 - j) * MASS_DIF**j for j in range(4)]
CORNER_STIFF = 3.0 * LINE_STIFF[0, 0] * LINE_MASS[0, 0] ** 2
CORNER_MASS = LINE_MASS[0, 0] ** 3


def lane(shape):
    return lax.broadcasted_iota(jnp.int32, shape, len(shape) - 1)


def next_x(v):
    return jnp.where(lane(v.shape) % EX == EX - 1, pltpu.roll(v, EX - 1, 1), pltpu.roll(v, PLANE - 1, 1))


def prev_x(v):
    return jnp.where(lane(v.shape) % EX == 0, pltpu.roll(v, PLANE - EX + 1, 1), pltpu.roll(v, 1, 1))


def next_y(v):
    return pltpu.roll(v, PLANE - EX, 1)


def prev_y(v):
    return pltpu.roll(v, EX, 1)


def next_xy(v):
    return jnp.where(lane(v.shape) % EX == EX - 1, pltpu.roll(v, PLANE - 1, 1), pltpu.roll(v, PLANE - EX - 1, 1))


def prev_xy(v):
    return jnp.where(lane(v.shape) % EX == 0, pltpu.roll(v, 1, 1), pltpu.roll(v, EX + 1, 1))


def next_z(v):
    half = v.shape[0] // 2
    return jnp.concatenate([v[half:], pltpu.roll(v[:half], half - 1, 0)], axis=0)


def prev_z(v):
    half = v.shape[0] // 2
    return jnp.concatenate([pltpu.roll(v[half:], 1, 0), v[:half]], axis=0)


def plane_row(layer, planes):
    layer = lax.rem(layer + planes, planes)
    return pl.ds(lax.div(layer, 2) + lax.rem(layer, 2) * (planes // 2), 1)


def column(values):
    row = lax.broadcasted_iota(jnp.int32, (8, PLANE), 0)
    out = jnp.full((8, PLANE), float(values[0]), F32)
    for k in range(1, 8):
        out = jnp.where(row == k, float(values[k]), out)
    return out


def rows_of(nz, ny):
    start = (nz * 8 + ny) * 8
    return slice(start, start + 8)


def get(ref, rows):
    return jnp.concatenate([ref[0, rows, :], ref[1, rows, :]], axis=1)


def put(ref, rows, value):
    ref[0, rows, :] = value[:, :128]
    ref[1, rows, :] = value[:, 128:]


def sum_xy(ref):
    planes = ref.shape[1] // 64
    first, last = pl.ds(0, planes * 8, stride=8), pl.ds(7, planes * 8, stride=8)
    shared = get(ref, last) + next_x(get(ref, first))
    put(ref, last, shared)
    put(ref, first, prev_x(shared))
    for nz in range(planes):
        shared = get(ref, rows_of(nz, 7)) + next_y(get(ref, rows_of(nz, 0)))
        put(ref, rows_of(nz, 7), shared)
        put(ref, rows_of(nz, 0), prev_y(shared))


def restrict(ref, points):
    sums_z, difs_z = [], []
    for ny in range(8):
        tiles = [get(ref, rows_of(nz, ny)) for nz in range(8)]
        sums_z.append(functools.reduce(lambda a, b: a + b, tiles))
        difs_z.append(sum(float(POINTS[7 - k]) * (tiles[7 - k] - tiles[k]) for k in range(4)))
    return restrict_xy(sums_z, difs_z, points)


def restrict_summed(ref, points):
    inv_ends = column(1.0 / ENDS)
    sums_z, difs_z = [], []
    for ny in range(8):
        tiles = [get(ref, rows_of(nz, ny)) for nz in range(8)]
        share = inv_ends * float(1.0 / ENDS[ny])
        sums_z.append(functools.reduce(lambda a, b: a + b, tiles) * share)
        difs_z.append(sum(float(POINTS[7 - k]) * (tiles[7 - k] - tiles[k]) for k in range(4)) * share)
    return restrict_xy(sums_z, difs_z, points)


def restrict_xy(sums_z, difs_z, points):
    planes = []
    for parts in (sums_z, difs_z):
        total = functools.reduce(lambda a, b: a + b, parts)
        slope = sum(float(POINTS[7 - k]) * (parts[7 - k] - parts[k]) for k in range(4))
        in_y = []
        for part in (total, slope):
            flat = jnp.sum(part, axis=0, keepdims=True)
            steep = jnp.sum(part * points, axis=0, keepdims=True)
            in_y.append((flat - steep) + prev_x(flat + steep))
        planes.append((in_y[0] - in_y[1]) + prev_y(in_y[0] + in_y[1]))
    return (planes[0] - planes[1]) * 0.125, (planes[0] + planes[1]) * 0.125


def both(v, following):
    after = following(v)
    return after + v, after - v


def both_back(total, dif, preceding):
    return (total - dif) + preceding(total + dif)


def coarse_modes(coeff):
    return [float(REACT * MODE_MASS[0])] + [
        float(MODE_STIFF[j]) * coeff + float(REACT * MODE_MASS[j]) for j in range(1, 4)
    ]


def coarse_tables(coeff):
    near = coeff + prev_x(coeff)
    near = near + prev_y(near)
    near = near + prev_z(near)
    scale = float(OMEGA) / (float(CORNER_STIFF) * near + float(8.0 * REACT * CORNER_MASS))
    return coarse_modes(coeff), scale


def coarse_apply(vert, modes):
    after_x, after_y, after_xy = next_x(vert), next_y(vert), next_xy(vert)
    in_x = [(after_x + vert, after_xy + after_y), (after_x - vert, after_xy - after_y)]
    back = []
    for jx in range(2):
        first, second = in_x[jx]
        for jy, in_y in enumerate((second + first, second - first)):
            in_z = both(in_y, next_z)
            scaled = [modes[jx + jy + jz] * in_z[jz] for jz in range(2)]
            back.append(both_back(scaled[0], scaled[1], prev_z))
    ss, sd, ds, dd = back
    low, high = (ss - sd, ss + sd), (ds - dd, ds + dd)
    return ((low[0] - high[0]) + prev_x(low[0] + high[0])) + (prev_y(low[1] - high[1]) + prev_xy(low[1] + high[1]))


def coarse_solve(target, modes, scale):
    vert = scale * target
    for _ in range(SWEEPS - 1):
        vert = vert + scale * (target - coarse_apply(vert, modes))
    return vert


def gathered_rows(ref, row, size):
    chips = ref.shape[0] // (2 * size)
    return jnp.concatenate([ref[pl.ds(core * size + row, chips, stride=2 * size), :] for core in range(2)], axis=0)


def gathered(ref, k, size):
    return jnp.concatenate([gathered_rows(ref, 2 * k + h, size) for h in range(2)], axis=1)


def halves(row):
    return [row[:, :128], row[:, 128:]]


def send(ref, rows):
    count = len(rows)
    times = 8 // math.gcd(count, 8)
    block = jnp.concatenate(rows * times, axis=0)
    for k in range(0, ref.shape[0], count * times):
        ref[k : k + count * times, :] = block


def layer_modes(vert_ref, shift):
    me, devices = my_layer(), vert_ref.shape[0]
    lower, upper = (vert_ref[plane_row(me + shift + k, devices), :] for k in range(2))
    modes = []
    for along_z in (upper + lower, upper - lower):
        for along_y in both(along_z, next_y):
            modes += both(along_y, next_x)
    return 0.125 * jnp.concatenate(modes, axis=0)


class Smooth:
    def __init__(self, modes, coeff, points, weight_x):
        row = lax.broadcasted_iota(jnp.int32, (8, PLANE), 0)
        ends = jnp.where(row == 0, -1.0, jnp.where(row == 7, 1.0, 0.0))
        m = [[[modes[4 * z + 2 * y + x : 4 * z + 2 * y + x + 1] for x in range(2)] for y in range(2)] for z in range(2)]
        self.xy = [[m[z][y][0] + m[z][y][1] * points for y in range(2)] for z in range(2)]
        self.dx = [[m[z][y][1] for y in range(2)] for z in range(2)]
        self.ends_coeff = ends * coeff
        self.weight_coeff = weight_x * coeff
        self.mass = float(REACT) * weight_x

    def value(self, nz, ny):
        by_y = [self.xy[z][0] + float(POINTS[ny]) * self.xy[z][1] for z in range(2)]
        return by_y[0] + float(POINTS[nz]) * by_y[1]

    def operated(self, nz, ny, value):
        wy, wz, py, pz = (float(t) for t in (WEIGHTS[ny], WEIGHTS[nz], POINTS[ny], POINTS[nz]))
        slope = (self.dx[0][0] + py * self.dx[0][1]) + pz * (self.dx[1][0] + py * self.dx[1][1])
        out = self.ends_coeff * (slope * (wy * wz)) + (self.mass * (wy * wz)) * value
        flux = None
        if ny in (0, 7):
            flux = (self.xy[0][1] + pz * self.xy[1][1]) * (wz * py)
        if nz in (0, 7):
            along = (self.xy[1][0] + py * self.xy[1][1]) * (wy * pz)
            flux = along if flux is None else flux + along
        return out if flux is None else out + self.weight_coeff * flux


def kappa_sums(own, below, above):
    row = lax.broadcasted_iota(jnp.int32, (8, PLANE), 0)
    table = []
    for along_z in (own + below, own, own + above):
        in_z = []
        for along_y in (along_z + prev_y(along_z), along_z, along_z + next_y(along_z)):
            first = along_y + prev_x(along_y)
            last = along_y + next_x(along_y)
            in_z.append(jnp.where(row == 0, first, jnp.where(row == 7, last, along_y)))
        table.append(in_z)
    return table


def kind(node):
    return 0 if node == 0 else (2 if node == 7 else 1)


def product(table, values):
    low, middle, high = pieces(values)
    stacked = jnp.concatenate([high, middle, high, middle, low, high], axis=0)
    return jnp.dot(table, stacked, preferred_element_type=F32)


def operate(z_ref, xy_ref, out_ref, table_ref, coeff, weight_x):
    for nz in range(8):
        rows = slice(64 * nz, 64 * nz + 64)
        xy_ref[rows, :] = product(table_ref[...], get(z_ref, rows))
    for ny in range(8):
        tiles = [get(z_ref, rows_of(nz, ny)) for nz in range(8)]
        even = [tiles[k] + tiles[7 - k] for k in range(4)]
        odd = [tiles[k] - tiles[7 - k] for k in range(4)]
        for nz in range(4):
            even_part = sum(float((STIFF[nz, k] + STIFF[nz, 7 - k]) / 2) * even[k] for k in range(4))
            odd_part = sum(float((STIFF[nz, k] - STIFF[nz, 7 - k]) / 2) * odd[k] for k in range(4))
            for node, term in ((nz, even_part + odd_part), (7 - nz, even_part - odd_part)):
                area = weight_x * float(WEIGHTS[ny])
                local = coeff * (
                    float(WEIGHTS[node]) * xy_ref[rows_of(node, ny), :] + area * term
                ) + (float(REACT * WEIGHTS[node]) * area) * tiles[node]
                put(out_ref, rows_of(node, ny), local)


def fine_diag(sums, nz, ny, weight_x, diag_x, ends_x):
    wy, wz, ky, kz = (float(t) for t in (WEIGHTS[ny], WEIGHTS[nz], DIAG[ny], DIAG[nz]))
    stiff = diag_x * (wy * wz) + weight_x * (ky * wz + wy * kz)
    mass = (weight_x * ends_x) * float(REACT * wy * wz * ENDS[ny] * ENDS[nz])
    return sums[kind(nz)][kind(ny)] * stiff + mass


def my_layer():
    return lax.axis_index("elem") * lax.axis_size("face") + lax.axis_index("face")


def face_rows(ref):
    even = lax.rem(my_layer(), 2) == 0
    last = ref.shape[1] - 64
    near = pl.multiple_of(jnp.where(even, last, 0), 64)
    far = pl.multiple_of(jnp.where(even, 0, last), 64)
    return pl.ds(near, 64), pl.ds(far, 64)


def faces_out(ref, near_ref, far_ref):
    for rows, out_ref in zip(face_rows(ref), (near_ref, far_ref)):
        out_ref[:, 0:56, :] = ref[:, pl.ds(rows.start, 56), :]


def face_in(ref):
    return jnp.concatenate([get(ref, slice(0, 56)), next_y(get(ref, slice(0, 8)))], axis=0)


def faces_in(ref, near_ref, far_ref):
    for rows, in_ref in zip(face_rows(ref), (near_ref, far_ref)):
        put(ref, rows, get(ref, rows) + face_in(in_ref))


def columns_of_nodes():
    return column(POINTS), column(WEIGHTS), column(DIAG), column(ENDS)


def pieces(v):
    high = v.astype(jnp.bfloat16)
    rest = v - high.astype(F32)
    middle = rest.astype(jnp.bfloat16)
    low = (rest - middle.astype(F32)).astype(jnp.bfloat16)
    return low, middle, high


def selection(order):
    place = lax.broadcasted_iota(jnp.int32, (PLANE, PLANE), 0).astype(order.dtype)
    return jnp.where(place == order, 1.0, 0.0).astype(jnp.bfloat16)


def opening(
    forcing_ref, kappa_ref, order_ref, load_ref, far_ref, near_ref, own_ref, payload_ref,
    held, held_kappa, held_order, held_payload, sems,
):
    small = [
        pltpu.make_async_copy(order_ref, held_order, sems.at[0]),
        pltpu.make_async_copy(kappa_ref, held_kappa, sems.at[1]),
    ]
    parts = [
        pltpu.make_async_copy(forcing_ref.at[:, pl.ds(256 * k, 256)], held.at[k], sems.at[2 + k]) for k in range(2)
    ]
    for copy in small + parts:
        copy.start()
    for copy in small + parts:
        copy.wait()
    order = held_order[...]
    choose = selection(order)
    choose = jnp.concatenate([choose] * 3, axis=1)
    coeff = lax.dot_general(
        jnp.concatenate(pieces(jnp.broadcast_to(held_kappa[...], (8, PLANE))), axis=1),
        choose,
        (((1,), (1,)), ((), ())),
        preferred_element_type=F32,
    )
    own = jnp.concatenate([coeff[0:3], order.astype(F32), coeff[4:8]], axis=0)
    own_ref[...] = own
    for k in range(2):
        load = jnp.dot(choose, jnp.concatenate(pieces(held[k]), axis=0), preferred_element_type=F32)
        put(load_ref, slice(256 * k, 256 * k + 256), load.T)
    sum_xy(load_ref)
    faces_out(load_ref, near_ref, far_ref)
    put(near_ref, slice(56, 64), own)
    put(far_ref, slice(56, 64), own)


    @pl.when(starts_early())
    def _():
        write_payload(load_ref, own_ref, payload_ref, held_payload, sems.at[4])


def starts_early():
    return my_layer() < lax.axis_size("elem") * lax.axis_size("face") // 2


def write_payload(load_ref, own_ref, payload_ref, held, sem):
    lower, upper = restrict_summed(load_ref, column(POINTS))
    send(held, halves(lower) + halves(upper) + halves(own_ref[0:1, :]))
    copy = pltpu.make_async_copy(held, payload_ref, sem)
    copy.start()
    copy.wait()


def late_payload(load_ref, own_ref, _, payload_ref, held, sems):
    @pl.when(jnp.logical_not(starts_early()))
    def _():
        write_payload(load_ref, own_ref, payload_ref, held, sems.at[0])


def below_above(near, far):
    even = lax.rem(my_layer(), 2) == 0
    return jnp.where(even, far, near), jnp.where(even, near, far)


def row_after_face(ref):
    return get(ref, slice(56, 64))[0:1]


def first_faces(
    load_ref, far_in_ref, near_in_ref, own_ref, table_ref,
    resid_ref, scaled_ref, image_ref, layers_ref, lower_ref, far_ref, near_ref, xy_ref,
):
    points, weight_x, _, _ = columns_of_nodes()
    own = own_ref[0:1, :]
    below, above = below_above(row_after_face(near_in_ref), row_after_face(far_in_ref))
    layers_ref[...] = jnp.concatenate([own, below, above, own_ref[3:8, :]], axis=0)
    resid_ref[...] = load_ref[...]
    faces_in(resid_ref, near_in_ref, far_in_ref)
    over_diag(functools.partial(get, resid_ref), scaled_ref, layers_ref)
    operate(scaled_ref, xy_ref, image_ref, table_ref, own, weight_x)
    lower, upper = restrict(image_ref, points)
    sum_xy(image_ref)
    faces_out(image_ref, near_ref, far_ref)
    lower_ref[...] = jnp.broadcast_to(lower, lower_ref.shape)
    put(near_ref, slice(56, 64), jnp.broadcast_to(upper, (8, PLANE)))
    put(far_ref, slice(56, 64), jnp.broadcast_to(upper, (8, PLANE)))


def over_diag(resid, scaled_ref, layers_ref):
    _, weight_x, diag_x, ends_x = columns_of_nodes()
    sums = kappa_sums(*(layers_ref[k : k + 1, :] for k in range(3)))
    for nz in range(8):
        for ny in range(8):
            rows = rows_of(nz, ny)
            put(scaled_ref, rows, resid(rows) / fine_diag(sums, nz, ny, weight_x, diag_x, ends_x))


def three_modes(vert_ref):
    return jnp.concatenate([layer_modes(vert_ref, shift) for shift in (0, -1, 1)], axis=0)


def smooths_of(modes, layers_ref):
    points, weight_x, _, _ = columns_of_nodes()
    return [Smooth(modes[8 * k : 8 * k + 8], layers_ref[k : k + 1, :], points, weight_x) for k in range(3)]


def smooth_image(smooths, out_ref, edge_ref):
    own, below, above = smooths
    for nz in range(8):
        for ny in range(8):
            put(out_ref, rows_of(nz, ny), own.operated(nz, ny, own.value(nz, ny)))
    sum_xy(out_ref)
    for plane, (smooth, nz) in enumerate(((below, 7), (above, 0))):
        for ny in range(8):
            put(edge_ref, rows_of(plane, ny), smooth.operated(nz, ny, smooth.value(nz, ny)))
    sum_xy(edge_ref)
    out_ref[:, 0:64, :] += edge_ref[:, 0:64, :]
    out_ref[:, 448:512, :] += edge_ref[:, 64:128, :]


def first_coarse(coarse_ref, layers_ref, vert_ref, target_ref, scale_ref, coeff_ref, smooth_ref, edge_ref):
    coeff = gathered(coarse_ref, 2, 6)
    coeff_ref[...] = coeff
    modes, scale = coarse_tables(coeff)
    target = gathered(coarse_ref, 0, 6) + prev_z(gathered(coarse_ref, 1, 6))
    vert = coarse_solve(target, modes, scale)
    vert_ref[...] = vert
    target_ref[...] = target
    scale_ref[...] = scale
    smooth_image(smooths_of(three_modes(vert_ref), layers_ref), smooth_ref, edge_ref)


def pack(sums):
    place = lane((8, 128)) // 16
    packed = jnp.zeros((8, 128), F32)
    for k, total in enumerate(sums):
        total = total[:, :128] + total[:, 128:]
        for by in (64, 32, 16):
            total = total + pltpu.roll(total, by, 1)
        packed = jnp.where(place == k, total, packed)
    return jnp.sum(packed, axis=0, keepdims=True)


def second_rough(
    image_ref, smooth_ref, layers_ref, table_ref, resid_ref, scaled_ref,
    scaled_change_ref, change_ref, sums_ref, planes_ref, column_ref, outer_ref, xy_ref, whole_ref,
):
    points, weight_x, _, _ = columns_of_nodes()
    inv_ends = column(1.0 / ENDS)
    whole_ref[...] = image_ref[...] + smooth_ref[...]
    over_diag(functools.partial(get, whole_ref), scaled_change_ref, layers_ref)
    operate(scaled_change_ref, xy_ref, change_ref, table_ref, layers_ref[0:1, :], weight_x)
    planes_ref[...] = jnp.concatenate(list(restrict(change_ref, points)) * 4, axis=0)
    sum_xy(change_ref)
    sums = [jnp.zeros((8, PLANE), F32)] * 6
    for ny in range(8):
        along = [jnp.zeros((8, PLANE), F32)] * 2
        for nz in range(8):
            rows = rows_of(nz, ny)
            share = float(1.0 / (ENDS[nz] * ENDS[ny]))
            scaled, change = get(scaled_ref, rows) * share, get(scaled_change_ref, rows)
            along = [total + float(STIFF[nz, node]) * change for total, node in zip(along, (0, 7))]
            change = change * share
            whole, image = get(whole_ref, rows), get(image_ref, rows)
            terms = [
                scaled * get(resid_ref, rows), scaled * whole, change * whole, scaled * image, change * image,
                change * (get(change_ref, rows) * float(ENDS[nz])),
            ]
            sums = [total + term for total, term in zip(sums, terms)]
        for k in range(2):
            column_ref[64 * k + 8 * ny : 64 * k + 8 * ny + 8, :] = along[k]
    sums_ref[...] = jnp.concatenate([total * inv_ends for total in sums], axis=0)
    for k, rows in enumerate((slice(0, 64), slice(448, 512))):
        outer_ref[64 * k : 64 * k + 64, :] = get(whole_ref, rows)


def second_faces(
    image_ref, scaled_change_ref, change_ref, outer_ref, far_in_ref, near_in_ref, layers_ref, table_ref,
    scaled_ref, lower_ref, sums_ref, planes_ref, column_ref,
    added_ref, far_ref, near_ref, payload_ref, edge_ref, xy_ref,
):
    points, weight_x, _, _ = columns_of_nodes()
    inv_ends = column(1.0 / ENDS)
    even = lax.rem(my_layer(), 2) == 0
    own = layers_ref[0:1, :]
    kappas = kappa_sums(*(layers_ref[k : k + 1, :] for k in range(3)))
    faces = below_above(face_in(near_in_ref), face_in(far_in_ref))
    tiles = [slice(8 * ny, 8 * ny + 8) for ny in range(8)]
    added = added_by(faces, kappas, columns_of_nodes())
    xy_ref[...] = product(table_ref[...], jnp.concatenate(added, axis=1))
    along, at_face = [], []
    for k in range(2):
        along.append(local_along(own, weight_x, added[k]))
        flux = own * xy_ref[:, PLANE * k : PLANE * k + PLANE]
        at_face.append(float(WEIGHTS[0]) * jnp.concatenate(
            [flux[t] + (float(REACT * WEIGHTS[ny]) * weight_x) * added[k][t] for ny, t in enumerate(tiles)], axis=0
        ))
    local = [
        (float(STIFF[nz, 0]) * along[0] + float(STIFF[nz, 7]) * along[1]) + at_face[k] for k, nz in enumerate((0, 7))
    ]
    flat = at_face[0] + at_face[1]
    slope = (along[1] + at_face[1]) - (along[0] + at_face[0])
    lower, upper = restrict_xy([flat[t] for t in tiles], [slope[t] for t in tiles], points)
    lower, upper = lower + planes_ref[0:1, :], upper + planes_ref[1:2, :]
    sums = [jnp.zeros((8, PLANE), F32)] * 5
    energy = jnp.zeros((8, PLANE), F32)
    planes = [slice(0, 64), slice(448, 512)]
    for k in range(2):
        s_plane, q_plane, i_plane, c_plane = (
            get(ref, planes[k]) for ref in (scaled_ref, scaled_change_ref, image_ref, change_ref)
        )
        w_plane = outer_ref[64 * k : 64 * k + 64, :]
        for ny in range(8):
            tile = tiles[ny]
            share = float(1.0 / ENDS[ny])
            half = share * float(1.0 / ENDS[0])
            face = faces[k][tile]
            s, q, dq = s_plane[tile] * half, q_plane[tile] * half, added[k][tile] * half
            sums[0] = sums[0] + s * face
            sums[1] = sums[1] + (q * face + dq * (w_plane[tile] + face))
            sums[2] = sums[2] + s * face
            sums[3] = sums[3] + (q * face + dq * (i_plane[tile] + face))
            sums[4] = sums[4] + (added[k][tile] * c_plane[tile]) * share
            energy = energy + (
                column_ref[64 * k + 8 * ny : 64 * k + 8 * ny + 8, :] * along[k][tile]
                + q_plane[tile] * at_face[k][tile]
                + added[k][tile] * local[k][tile]
            )
    sums = [sums_ref[8 * k + 8 : 8 * k + 16, :] + sums[k] * inv_ends for k in range(5)]
    sums = pack([sums_ref[0:8, :]] + sums[:4] + [sums[4] + energy])
    below, _ = below_above(row_after_face(near_in_ref), row_after_face(far_in_ref))
    send(payload_ref, halves(lower_ref[0:1, :] + below) + halves(lower) + halves(upper) + [sums])
    for k in range(2):
        put(edge_ref, slice(64 * k, 64 * k + 64), local[k])
        added_ref[64 * k : 64 * k + 64, :] = at_face[k]
    sum_xy(edge_ref)
    change = [(get(change_ref, planes[k]) + get(edge_ref, slice(64 * k, 64 * k + 64)))[0:56] for k in range(2)]
    put(far_ref, slice(0, 56), jnp.where(even, change[0], change[1]))
    put(near_ref, slice(0, 56), jnp.where(even, change[1], change[0]))


def local_along(own, weight_x, added):
    return own * jnp.concatenate(
        [(weight_x * float(WEIGHTS[ny])) * added[8 * ny : 8 * ny + 8] for ny in range(8)], axis=0
    )


def added_by(faces, kappas, columns):
    _, weight_x, diag_x, ends_x = columns
    return [
        jnp.concatenate(
            [
                face[8 * ny : 8 * ny + 8] / fine_diag(kappas, nz, ny, weight_x, diag_x, ends_x)
                for ny in range(8)
            ],
            axis=0,
        )
        for nz, face in zip((0, 7), faces)
    ]


def complete(
    first_ref, first_scaled_ref, first_change_ref, far_in_ref, near_in_ref, at_face_ref, layers_ref, coeff_ref, vert_ref,
    image_ref, scaled_change_ref, change_ref, choose_ref, applied_ref, modes_ref, edge_ref,
):
    columns = columns_of_nodes()
    applied_ref[...] = coarse_apply(vert_ref[...], coarse_modes(coeff_ref[...]))
    modes_ref[...] = three_modes(vert_ref)
    choose_ref[...] = selection(layers_ref[3:4, :]).astype(F32).T.astype(jnp.bfloat16)
    image_ref[...] = first_ref[...]
    scaled_change_ref[...] = first_scaled_ref[...]
    faces_in(image_ref, near_in_ref, far_in_ref)
    kappas = kappa_sums(*(layers_ref[k : k + 1, :] for k in range(3)))
    added = added_by(below_above(face_in(near_in_ref), face_in(far_in_ref)), kappas, columns)
    for k, rows in enumerate((slice(0, 64), slice(448, 512))):
        put(scaled_change_ref, rows, get(scaled_change_ref, rows) + added[k])
        put(edge_ref, slice(64 * k, 64 * k + 64), local_along(layers_ref[0:1, :], columns[1], added[k]))
        put(edge_ref, slice(128 + 64 * k, 192 + 64 * k), at_face_ref[64 * k : 64 * k + 64, :])
    sum_xy(edge_ref)
    along = [get(edge_ref, slice(64 * k, 64 * k + 64)) for k in range(2)]
    for nz in range(8):
        rows = slice(64 * nz, 64 * nz + 64)
        new = get(first_change_ref, rows) + (float(STIFF[nz, 0]) * along[0] + float(STIFF[nz, 7]) * along[1])
        if nz in (0, 7):
            new = new + get(edge_ref, slice(128 + 64 * (nz // 7), 192 + 64 * (nz // 7)))
        put(change_ref, rows, new)


def folded(value):
    return functools.reduce(lambda a, b: a + b, [value[k : k + 8] for k in range(0, value.shape[0], 8)])


def second_coarse(
    coeff_ref, step_ref, first_ref, applied_ref, target_ref, scale_ref, first_modes_ref, modes_ref, scalars_ref, vert_ref
):
    modes = coarse_modes(coeff_ref[...])
    target, first, applied = target_ref[...], first_ref[...], applied_ref[...]
    rough, rough_change = gathered(step_ref, 0, 7), gathered(step_ref, 1, 7) + prev_z(gathered(step_ref, 2, 7))
    parts = folded(gathered_rows(step_ref, 6, 7))
    sums = [parts] + [pltpu.roll(parts, 128 - 16 * k, 1) for k in range(1, 6)]
    used = lane(parts.shape) < 16

    def total(fine, coarse):
        coarse = folded(coarse)
        return jnp.sum(jnp.where(used, fine, 0.0) + (coarse[:, :128] + coarse[:, 128:]), keepdims=True)

    image = rough + applied
    change = coarse_solve(image, modes, scale_ref[...])
    vert_ref[...] = change
    change_modes = three_modes(vert_ref)
    change_applied = coarse_apply(change, modes)
    gamma = total(sums[0], target * first)
    energy = total(sums[3], first * (2.0 * rough + applied))
    alpha = gamma / energy
    vert = first - alpha * change
    progress = total(sums[0] - alpha * (2.0 * sums[1] - alpha * sums[2]), (target - alpha * image) * vert)
    second = total(
        sums[3] - alpha * (2.0 * sums[4] - alpha * sums[5]),
        vert * (2.0 * (rough - alpha * rough_change) + (applied - alpha * change_applied)),
    )
    cross = total(sums[1] - alpha * sums[2], vert * image)
    beta = progress / gamma
    alpha_next = progress / (second + beta * (2.0 * cross + beta * energy))
    scalars = [alpha + alpha_next * beta + alpha_next, alpha_next * alpha]
    modes_ref[...] = scalars[0] * first_modes_ref[...] - scalars[1] * change_modes
    scalars_ref[...] = jnp.concatenate([jnp.broadcast_to(t, (1, 128)) for t in scalars * 4], axis=0)


def to_stored(choose, value):
    return lax.dot_general(
        jnp.concatenate([choose] * 2, axis=1),
        jnp.concatenate(pieces(value)[1:], axis=1),
        (((1,), (1,)), ((), ())),
        preferred_element_type=F32,
    )


def closing(
    resid_ref, scaled_ref, image_ref, scaled_change_ref, change_ref, far_ref, near_ref, modes_ref, layers_ref, scalars_ref,
    choose_ref, solution_ref, residual_ref, grid_ref, sum_ref, edge_ref, held, sems,
):
    smooths = smooths_of(modes_ref[...], layers_ref)
    first, second = scalars_ref[0:1, 0:1], scalars_ref[1:2, 0:1]
    choose = choose_ref[...]
    for nz in range(8):
        for ny in range(8):
            rows = rows_of(nz, ny)
            rough = first * get(scaled_ref, rows) - second * get(scaled_change_ref, rows)
            grid_ref[rows, :] = rough + smooths[0].value(nz, ny)
    held[0] = to_stored(choose, grid_ref[...])
    smooth_image(smooths, sum_ref, edge_ref)
    first, second = first[None], second[None]
    sum_ref[...] = resid_ref[...] - first * image_ref[...] + second * change_ref[...] - sum_ref[...]
    for rows, ref in zip(face_rows(sum_ref), (near_ref, far_ref)):
        put(sum_ref, rows, get(sum_ref, rows) + second[0] * face_in(ref))
    copies = [pltpu.make_async_copy(held.at[0], solution_ref, sems.at[0])]
    copies[0].start()
    held[1] = to_stored(choose, get(sum_ref, slice(0, 512)))
    copies.append(pltpu.make_async_copy(held.at[1], residual_ref, sems.at[1]))
    copies[1].start()
    for copy in copies:
        copy.wait()


def call(kernel, outs, scratch=(), sems=0, cost=None, in_place=None, hbm_in=(), hbm_out=(), inputs=0):
    def specs(count, far):
        return [pl.BlockSpec(memory_space=pltpu.HBM if k in far else pltpu.VMEM) for k in range(count)]

    more = {"in_specs": specs(inputs, hbm_in)} if hbm_in else {}
    return pl.pallas_call(
        kernel,
        out_shape=[jax.ShapeDtypeStruct(*(s if isinstance(s[0], tuple) else (s, F32))) for s in outs],
        out_specs=specs(len(outs), hbm_out),
        scratch_shapes=[pltpu.VMEM(*(s if isinstance(s[0], tuple) else (s, F32))) for s in scratch]
        + ([pltpu.SemaphoreType.DMA((sems,))] if sems else []),
        compiler_params=pltpu.CompilerParams(vmem_limit_bytes=12 * 1024 * 1024),
        cost_estimate=cost,
        input_output_aliases=in_place or {},
        **more,
    )


def swapped(x, far):
    size = lax.axis_size(AXES)
    return lax.ppermute(x, AXES, [(i, (i + (1 if (i % 2 == 0) != far else -1)) % size) for i in range(size)])


def everyone(payload, shape):
    devices = lax.axis_size(AXES)
    return lax.all_to_all(payload.reshape((devices,) + shape), AXES, 0, 0, tiled=True).reshape(-1, 128)


def per_device(forcing, kappa, elem_order):
    devices = lax.axis_size(AXES)
    nodes, face, face_row = (2, 512, 128), (2, 56, 128), (2, 64, 128)
    plane, grid, flat = (8, PLANE), (devices, PLANE), (512, PLANE)
    edge, stored, choice = (2, 128, 128), (PLANE, 512), ((PLANE, PLANE), jnp.bfloat16)
    table = jnp.asarray(np.concatenate([STIFF_PARTS[k] for k in (0, 0, 1, 1, 0, 2)], 1), jnp.bfloat16)
    long = pl.CostEstimate(flops=10**11, bytes_accessed=2**28, transcendentals=0)
    payload_rows = (devices * 6, 128)
    load, far, near, own, payload = call(
        opening,
        [nodes, face_row, face_row, plane, payload_rows],
        [(2, PLANE, 256), (1, PLANE), ((1, PLANE), jnp.int32), payload_rows],
        5,
        hbm_in=(0, 1, 2),
        hbm_out=(4,),
        inputs=3,
    )(*(pltpu.with_memory_space_constraint(x, pltpu.HBM) for x in (forcing, kappa.reshape(1, PLANE), elem_order)))
    far, near = swapped(far, True), swapped(near, False)
    (payload,) = call(
        late_payload, [payload_rows], [payload_rows], 1, in_place={2: 0}, hbm_in=(2,), hbm_out=(0,), inputs=3
    )(load, own, payload)
    gather = everyone(payload, (3, 2, 128))
    resid, scaled, image, layers, lower, far, near = call(
        first_faces, [nodes, nodes, nodes, plane, plane, face_row, face_row], [flat], cost=long, in_place={0: 0}
    )(load, far, near, own, table)
    far, near = swapped(far, True), swapped(near, False)
    vert, target, scale, coeff, smooth = call(first_coarse, [grid] * 4 + [nodes], [edge])(gather, layers)
    scaled_change, change, sums, planes, column_planes, outer = call(
        second_rough, [nodes] * 2 + [(48, PLANE), plane, (128, PLANE), (128, PLANE)], [flat, nodes], in_place={1: 0}
    )(image, smooth, layers, table, resid, scaled)
    added, next_far, next_near, payload = call(
        second_faces, [(128, PLANE), face, face, (devices * 7, 128)], [edge, (64, 2 * PLANE)]
    )(image, scaled_change, change, outer, far, near, layers, table, scaled, lower, sums, planes, column_planes)
    step = everyone(payload, (7, 1, 128))
    next_far, next_near = swapped(next_far, True), swapped(next_near, False)
    image, scaled_change, change, choose, applied, first_modes = call(
        complete, [nodes] * 3 + [choice, grid, (24, PLANE)], [(2, 256, 128)], in_place={0: 0, 1: 1, 2: 2}
    )(image, scaled_change, change, far, near, added, layers, coeff, vert)
    modes, scalars = call(second_coarse, [(24, PLANE), (8, 128)], [grid])(
        coeff, step, vert, applied, target, scale, first_modes
    )
    found, left = call(closing, [stored, stored], [flat, nodes, edge, (2,) + stored], 2, hbm_out=(0, 1))(
        resid, scaled, image, scaled_change, change, next_far, next_near, modes, layers, scalars, choose
    )
    return found, left


def solution(mesh):
    in_specs = (P(AXES, None), P(AXES), P(AXES, None))
    out_specs = (P(AXES, None), P(AXES, None))
    return jax.shard_map(
        per_device, mesh=mesh, in_specs=in_specs, out_specs=out_specs, check_vma=False
    )
```

```python
import functools
import math

import jax
import jax.numpy as jnp
import ml_dtypes
import numpy as np
from jax import lax
from jax.experimental import pallas as pl
from jax.experimental.pallas import tpu as pltpu
from jax.sharding import PartitionSpec as P

EX = 8
EY = 32
PLANE = EX * EY
SWEEPS = 4
REACT = 0.02
OMEGA = 0.6
AXES = ("elem", "face")
F32 = jnp.float32


def legendre_seven(points):
    before = np.ones(8)
    current = np.array(points)
    for degree in range(1, 7):
        following = ((2 * degree + 1) * points * current - degree * before) / (degree + 1)
        before = current
        current = following
    return current


def line_tables():
    points = np.array(
        [
            -1.0,
            -0.8717401485096066,
            -0.5917001814331423,
            -0.2092992179024789,
            0.2092992179024789,
            0.5917001814331423,
            0.8717401485096066,
            1.0,
        ]
    )
    weights = np.array(
        [
            1.0 / 28.0,
            0.2107042271435061,
            0.3411226924835044,
            0.4124587946587038,
            0.4124587946587038,
            0.3411226924835044,
            0.2107042271435061,
            1.0 / 28.0,
        ]
    )
    legendre = legendre_seven(points)
    derivative = np.zeros((8, 8))
    for left_node in range(8):
        for right_node in range(8):
            if left_node != right_node:
                derivative[left_node, right_node] = legendre[left_node] / (
                    legendre[right_node] * (points[left_node] - points[right_node])
                )
    derivative[0, 0] = -14.0
    derivative[7, 7] = 14.0
    stiffness = derivative.T @ (weights[:, None] * derivative)
    return points, weights, stiffness


POINTS, WEIGHTS, STIFF = line_tables()
DIAG = np.diag(STIFF)
ENDS = np.array([2.0] + [1.0] * 6 + [2.0])
MASS = np.diag(WEIGHTS)
STIFF_XY = np.kron(MASS, STIFF) + np.kron(STIFF, MASS)
STIFF_PARTS = []
for part in range(3):
    STIFF_PARTS.append((STIFF_XY - sum(STIFF_PARTS)).astype(ml_dtypes.bfloat16).astype(np.float64))
INTERP = np.stack([(1.0 - POINTS) / 2.0, (1.0 + POINTS) / 2.0], 1)
LINE_MASS = INTERP.T @ (WEIGHTS[:, None] * INTERP)
LINE_STIFF = INTERP.T @ STIFF @ INTERP
MASS_SUM = (LINE_MASS[0, 0] + LINE_MASS[0, 1]) / 2.0
MASS_DIF = (LINE_MASS[0, 0] - LINE_MASS[0, 1]) / 2.0
STIFF_DIF = LINE_STIFF[0, 0]
MODE_STIFF = [
    0.0,
    STIFF_DIF * MASS_SUM**2,
    2.0 * STIFF_DIF * MASS_DIF * MASS_SUM,
    3.0 * STIFF_DIF * MASS_DIF**2,
]
MODE_MASS = [MASS_SUM ** (3 - j) * MASS_DIF**j for j in range(4)]
CORNER_STIFF = 3.0 * LINE_STIFF[0, 0] * LINE_MASS[0, 0] ** 2
CORNER_MASS = LINE_MASS[0, 0] ** 3


def lane(shape):
    return lax.broadcasted_iota(jnp.int32, shape, len(shape) - 1)


def next_x(v):
    return jnp.where(lane(v.shape) % EX == EX - 1, pltpu.roll(v, EX - 1, 1), pltpu.roll(v, PLANE - 1, 1))


def prev_x(v):
    return jnp.where(lane(v.shape) % EX == 0, pltpu.roll(v, PLANE - EX + 1, 1), pltpu.roll(v, 1, 1))


def next_y(v):
    return pltpu.roll(v, PLANE - EX, 1)


def prev_y(v):
    return pltpu.roll(v, EX, 1)


def next_xy(v):
    return jnp.where(lane(v.shape) % EX == EX - 1, pltpu.roll(v, PLANE - 1, 1), pltpu.roll(v, PLANE - EX - 1, 1))


def prev_xy(v):
    return jnp.where(lane(v.shape) % EX == 0, pltpu.roll(v, 1, 1), pltpu.roll(v, EX + 1, 1))


def next_z(v):
    half = v.shape[0] // 2
    return jnp.concatenate([v[half:], pltpu.roll(v[:half], half - 1, 0)], axis=0)


def prev_z(v):
    half = v.shape[0] // 2
    return jnp.concatenate([pltpu.roll(v[half:], 1, 0), v[:half]], axis=0)


def plane_row(layer, planes):
    layer = lax.rem(layer + planes, planes)
    return pl.ds(lax.div(layer, 2) + lax.rem(layer, 2) * (planes // 2), 1)


def column(values):
    row = lax.broadcasted_iota(jnp.int32, (8, PLANE), 0)
    out = jnp.full((8, PLANE), float(values[0]), F32)
    for k in range(1, 8):
        out = jnp.where(row == k, float(values[k]), out)
    return out


def rows_of(nz, ny):
    start = (nz * 8 + ny) * 8
    return slice(start, start + 8)


def get(ref, rows):
    return jnp.concatenate([ref[0, rows, :], ref[1, rows, :]], axis=1)


def put(ref, rows, value):
    ref[0, rows, :] = value[:, :128]
    ref[1, rows, :] = value[:, 128:]


def sum_xy(ref):
    planes = ref.shape[1] // 64
    first, last = pl.ds(0, planes * 8, stride=8), pl.ds(7, planes * 8, stride=8)
    shared = get(ref, last) + next_x(get(ref, first))
    put(ref, last, shared)
    put(ref, first, prev_x(shared))
    for nz in range(planes):
        shared = get(ref, rows_of(nz, 7)) + next_y(get(ref, rows_of(nz, 0)))
        put(ref, rows_of(nz, 7), shared)
        put(ref, rows_of(nz, 0), prev_y(shared))


def restrict(ref, points):
    sums_z, difs_z = [], []
    for ny in range(8):
        tiles = [get(ref, rows_of(nz, ny)) for nz in range(8)]
        sums_z.append(functools.reduce(lambda a, b: a + b, tiles))
        difs_z.append(sum(float(POINTS[7 - k]) * (tiles[7 - k] - tiles[k]) for k in range(4)))
    return restrict_xy(sums_z, difs_z, points)


def restrict_summed(ref, points):
    inv_ends = column(1.0 / ENDS)
    sums_z, difs_z = [], []
    for ny in range(8):
        tiles = [get(ref, rows_of(nz, ny)) for nz in range(8)]
        share = inv_ends * float(1.0 / ENDS[ny])
        sums_z.append(functools.reduce(lambda a, b: a + b, tiles) * share)
        difs_z.append(sum(float(POINTS[7 - k]) * (tiles[7 - k] - tiles[k]) for k in range(4)) * share)
    return restrict_xy(sums_z, difs_z, points)


def restrict_xy(sums_z, difs_z, points):
    planes = []
    for parts in (sums_z, difs_z):
        total = functools.reduce(lambda a, b: a + b, parts)
        slope = sum(float(POINTS[7 - k]) * (parts[7 - k] - parts[k]) for k in range(4))
        in_y = []
        for part in (total, slope):
            flat = jnp.sum(part, axis=0, keepdims=True)
            steep = jnp.sum(part * points, axis=0, keepdims=True)
            in_y.append((flat - steep) + prev_x(flat + steep))
        planes.append((in_y[0] - in_y[1]) + prev_y(in_y[0] + in_y[1]))
    return (planes[0] - planes[1]) * 0.125, (planes[0] + planes[1]) * 0.125


def both(v, following):
    after = following(v)
    return after + v, after - v


def both_back(total, dif, preceding):
    return (total - dif) + preceding(total + dif)


def coarse_modes(coeff):
    return [float(REACT * MODE_MASS[0])] + [
        float(MODE_STIFF[j]) * coeff + float(REACT * MODE_MASS[j]) for j in range(1, 4)
    ]


def coarse_tables(coeff):
    near = coeff + prev_x(coeff)
    near = near + prev_y(near)
    near = near + prev_z(near)
    scale = float(OMEGA) / (float(CORNER_STIFF) * near + float(8.0 * REACT * CORNER_MASS))
    return coarse_modes(coeff), scale


def coarse_apply(vert, modes):
    after_x, after_y, after_xy = next_x(vert), next_y(vert), next_xy(vert)
    in_x = [(after_x + vert, after_xy + after_y), (after_x - vert, after_xy - after_y)]
    back = []
    for jx in range(2):
        first, second = in_x[jx]
        for jy, in_y in enumerate((second + first, second - first)):
            in_z = both(in_y, next_z)
            scaled = [modes[jx + jy + jz] * in_z[jz] for jz in range(2)]
            back.append(both_back(scaled[0], scaled[1], prev_z))
    ss, sd, ds, dd = back
    low, high = (ss - sd, ss + sd), (ds - dd, ds + dd)
    return ((low[0] - high[0]) + prev_x(low[0] + high[0])) + (prev_y(low[1] - high[1]) + prev_xy(low[1] + high[1]))


def coarse_solve(target, modes, scale):
    vert = scale * target
    for _ in range(SWEEPS - 1):
        vert = vert + scale * (target - coarse_apply(vert, modes))
    return vert


def gathered_rows(ref, row, size):
    chips = ref.shape[0] // (2 * size)
    return jnp.concatenate([ref[pl.ds(core * size + row, chips, stride=2 * size), :] for core in range(2)], axis=0)


def gathered(ref, k, size):
    return jnp.concatenate([gathered_rows(ref, 2 * k + h, size) for h in range(2)], axis=1)


def halves(row):
    return [row[:, :128], row[:, 128:]]


def send(ref, rows):
    count = len(rows)
    times = 8 // math.gcd(count, 8)
    block = jnp.concatenate(rows * times, axis=0)
    for k in range(0, ref.shape[0], count * times):
        ref[k : k + count * times, :] = block


def layer_modes(vert_ref, shift):
    me, devices = my_layer(), vert_ref.shape[0]
    lower, upper = (vert_ref[plane_row(me + shift + k, devices), :] for k in range(2))
    modes = []
    for along_z in (upper + lower, upper - lower):
        for along_y in both(along_z, next_y):
            modes += both(along_y, next_x)
    return 0.125 * jnp.concatenate(modes, axis=0)


class Smooth:
    def __init__(self, modes, coeff, points, weight_x):
        row = lax.broadcasted_iota(jnp.int32, (8, PLANE), 0)
        ends = jnp.where(row == 0, -1.0, jnp.where(row == 7, 1.0, 0.0))
        m = [[[modes[4 * z + 2 * y + x : 4 * z + 2 * y + x + 1] for x in range(2)] for y in range(2)] for z in range(2)]
        self.xy = [[m[z][y][0] + m[z][y][1] * points for y in range(2)] for z in range(2)]
        self.dx = [[m[z][y][1] for y in range(2)] for z in range(2)]
        self.ends_coeff = ends * coeff
        self.weight_coeff = weight_x * coeff
        self.mass = float(REACT) * weight_x

    def value(self, nz, ny):
        by_y = [self.xy[z][0] + float(POINTS[ny]) * self.xy[z][1] for z in range(2)]
        return by_y[0] + float(POINTS[nz]) * by_y[1]

    def operated(self, nz, ny, value):
        wy, wz, py, pz = (float(t) for t in (WEIGHTS[ny], WEIGHTS[nz], POINTS[ny], POINTS[nz]))
        slope = (self.dx[0][0] + py * self.dx[0][1]) + pz * (self.dx[1][0] + py * self.dx[1][1])
        out = self.ends_coeff * (slope * (wy * wz)) + (self.mass * (wy * wz)) * value
        flux = None
        if ny in (0, 7):
            flux = (self.xy[0][1] + pz * self.xy[1][1]) * (wz * py)
        if nz in (0, 7):
            along = (self.xy[1][0] + py * self.xy[1][1]) * (wy * pz)
            flux = along if flux is None else flux + along
        return out if flux is None else out + self.weight_coeff * flux


def kappa_sums(own, below, above):
    row = lax.broadcasted_iota(jnp.int32, (8, PLANE), 0)
    table = []
    for along_z in (own + below, own, own + above):
        in_z = []
        for along_y in (along_z + prev_y(along_z), along_z, along_z + next_y(along_z)):
            first = along_y + prev_x(along_y)
            last = along_y + next_x(along_y)
            in_z.append(jnp.where(row == 0, first, jnp.where(row == 7, last, along_y)))
        table.append(in_z)
    return table


def kind(node):
    return 0 if node == 0 else (2 if node == 7 else 1)


def product(table, values):
    low, middle, high = pieces(values)
    stacked = jnp.concatenate([high, middle, high, middle, low, high], axis=0)
    return jnp.dot(table, stacked, preferred_element_type=F32)


def operate(z_ref, xy_ref, out_ref, table_ref, coeff, weight_x):
    for nz in range(8):
        rows = slice(64 * nz, 64 * nz + 64)
        xy_ref[rows, :] = product(table_ref[...], get(z_ref, rows))
    for ny in range(8):
        tiles = [get(z_ref, rows_of(nz, ny)) for nz in range(8)]
        even = [tiles[k] + tiles[7 - k] for k in range(4)]
        odd = [tiles[k] - tiles[7 - k] for k in range(4)]
        for nz in range(4):
            even_part = sum(float((STIFF[nz, k] + STIFF[nz, 7 - k]) / 2) * even[k] for k in range(4))
            odd_part = sum(float((STIFF[nz, k] - STIFF[nz, 7 - k]) / 2) * odd[k] for k in range(4))
            for node, term in ((nz, even_part + odd_part), (7 - nz, even_part - odd_part)):
                area = weight_x * float(WEIGHTS[ny])
                local = coeff * (
                    float(WEIGHTS[node]) * xy_ref[rows_of(node, ny), :] + area * term
                ) + (float(REACT * WEIGHTS[node]) * area) * tiles[node]
                put(out_ref, rows_of(node, ny), local)


def fine_diag(sums, nz, ny, weight_x, diag_x, ends_x):
    wy, wz, ky, kz = (float(t) for t in (WEIGHTS[ny], WEIGHTS[nz], DIAG[ny], DIAG[nz]))
    stiff = diag_x * (wy * wz) + weight_x * (ky * wz + wy * kz)
    mass = (weight_x * ends_x) * float(REACT * wy * wz * ENDS[ny] * ENDS[nz])
    return sums[kind(nz)][kind(ny)] * stiff + mass


def my_layer():
    return lax.axis_index("elem") * lax.axis_size("face") + lax.axis_index("face")


def face_rows(ref):
    even = lax.rem(my_layer(), 2) == 0
    last = ref.shape[1] - 64
    near = pl.multiple_of(jnp.where(even, last, 0), 64)
    far = pl.multiple_of(jnp.where(even, 0, last), 64)
    return pl.ds(near, 64), pl.ds(far, 64)


def faces_out(ref, near_ref, far_ref):
    for rows, out_ref in zip(face_rows(ref), (near_ref, far_ref)):
        out_ref[:, 0:56, :] = ref[:, pl.ds(rows.start, 56), :]


def face_in(ref):
    return jnp.concatenate([get(ref, slice(0, 56)), next_y(get(ref, slice(0, 8)))], axis=0)


def faces_in(ref, near_ref, far_ref):
    for rows, in_ref in zip(face_rows(ref), (near_ref, far_ref)):
        put(ref, rows, get(ref, rows) + face_in(in_ref))


def columns_of_nodes():
    return column(POINTS), column(WEIGHTS), column(DIAG), column(ENDS)


def pieces(v):
    high = v.astype(jnp.bfloat16)
    rest = v - high.astype(F32)
    middle = rest.astype(jnp.bfloat16)
    low = (rest - middle.astype(F32)).astype(jnp.bfloat16)
    return low, middle, high


def selection(order):
    place = lax.broadcasted_iota(jnp.int32, (PLANE, PLANE), 0).astype(order.dtype)
    return jnp.where(place == order, 1.0, 0.0).astype(jnp.bfloat16)


def opening(
    forcing_ref, kappa_ref, order_ref, load_ref, far_ref, near_ref, own_ref, payload_ref,
    held, held_kappa, held_order, held_payload, sems,
):
    small = [
        pltpu.make_async_copy(order_ref, held_order, sems.at[0]),
        pltpu.make_async_copy(kappa_ref, held_kappa, sems.at[1]),
    ]
    parts = [
        pltpu.make_async_copy(forcing_ref.at[pl.ds(64 * k, 64)], held.at[pl.ds(64 * k, 64)], sems.at[2 + k])
        for k in range(4)
    ]
    for copy in small + parts:
        copy.start()
    for copy in small + parts:
        copy.wait()
    order = held_order[...]
    choose = selection(order)
    choose = jnp.concatenate([choose] * 3, axis=1)
    coeff = lax.dot_general(
        jnp.concatenate(pieces(jnp.broadcast_to(held_kappa[...], (8, PLANE))), axis=1),
        choose,
        (((1,), (1,)), ((), ())),
        preferred_element_type=F32,
    )
    own = jnp.concatenate([coeff[0:3], order.astype(F32), coeff[4:8]], axis=0)
    own_ref[...] = own
    for k in range(2):
        load = jnp.dot(choose, jnp.concatenate(pieces(held[:, 256 * k : 256 * k + 256]), axis=0), preferred_element_type=F32)
        put(load_ref, slice(256 * k, 256 * k + 256), load.T)
    sum_xy(load_ref)
    faces_out(load_ref, near_ref, far_ref)
    put(near_ref, slice(56, 64), own)
    put(far_ref, slice(56, 64), own)


    @pl.when(starts_early())
    def _():
        write_payload(load_ref, own_ref, payload_ref, held_payload, sems.at[6])


def starts_early():
    return my_layer() < lax.axis_size("elem") * lax.axis_size("face") // 2


def write_payload(load_ref, own_ref, payload_ref, held, sem):
    lower, upper = restrict_summed(load_ref, column(POINTS))
    send(held, halves(lower) + halves(upper) + halves(own_ref[0:1, :]))
    copy = pltpu.make_async_copy(held, payload_ref, sem)
    copy.start()
    copy.wait()


def late_payload(load_ref, own_ref, _, payload_ref, held, sems):
    @pl.when(jnp.logical_not(starts_early()))
    def _():
        write_payload(load_ref, own_ref, payload_ref, held, sems.at[0])


def below_above(near, far):
    even = lax.rem(my_layer(), 2) == 0
    return jnp.where(even, far, near), jnp.where(even, near, far)


def row_after_face(ref):
    return get(ref, slice(56, 64))[0:1]


def first_faces(
    load_ref, far_in_ref, near_in_ref, own_ref, table_ref,
    resid_ref, scaled_ref, image_ref, layers_ref, lower_ref, far_ref, near_ref, xy_ref,
):
    points, weight_x, _, _ = columns_of_nodes()
    own = own_ref[0:1, :]
    below, above = below_above(row_after_face(near_in_ref), row_after_face(far_in_ref))
    layers_ref[...] = jnp.concatenate([own, below, above, own_ref[3:8, :]], axis=0)
    resid_ref[...] = load_ref[...]
    faces_in(resid_ref, near_in_ref, far_in_ref)
    over_diag(functools.partial(get, resid_ref), scaled_ref, layers_ref)
    operate(scaled_ref, xy_ref, image_ref, table_ref, own, weight_x)
    lower, upper = restrict(image_ref, points)
    sum_xy(image_ref)
    faces_out(image_ref, near_ref, far_ref)
    lower_ref[...] = jnp.broadcast_to(lower, lower_ref.shape)
    put(near_ref, slice(56, 64), jnp.broadcast_to(upper, (8, PLANE)))
    put(far_ref, slice(56, 64), jnp.broadcast_to(upper, (8, PLANE)))


def over_diag(resid, scaled_ref, layers_ref):
    _, weight_x, diag_x, ends_x = columns_of_nodes()
    sums = kappa_sums(*(layers_ref[k : k + 1, :] for k in range(3)))
    for nz in range(8):
        for ny in range(8):
            rows = rows_of(nz, ny)
            put(scaled_ref, rows, resid(rows) / fine_diag(sums, nz, ny, weight_x, diag_x, ends_x))


def three_modes(vert_ref):
    return jnp.concatenate([layer_modes(vert_ref, shift) for shift in (0, -1, 1)], axis=0)


def smooths_of(modes, layers_ref):
    points, weight_x, _, _ = columns_of_nodes()
    return [Smooth(modes[8 * k : 8 * k + 8], layers_ref[k : k + 1, :], points, weight_x) for k in range(3)]


def smooth_image(smooths, out_ref, edge_ref):
    own, below, above = smooths
    for nz in range(8):
        for ny in range(8):
            put(out_ref, rows_of(nz, ny), own.operated(nz, ny, own.value(nz, ny)))
    sum_xy(out_ref)
    for plane, (smooth, nz) in enumerate(((below, 7), (above, 0))):
        for ny in range(8):
            put(edge_ref, rows_of(plane, ny), smooth.operated(nz, ny, smooth.value(nz, ny)))
    sum_xy(edge_ref)
    out_ref[:, 0:64, :] += edge_ref[:, 0:64, :]
    out_ref[:, 448:512, :] += edge_ref[:, 64:128, :]


def first_coarse(coarse_ref, layers_ref, vert_ref, target_ref, scale_ref, coeff_ref, smooth_ref, edge_ref):
    coeff = gathered(coarse_ref, 2, 6)
    coeff_ref[...] = coeff
    modes, scale = coarse_tables(coeff)
    target = gathered(coarse_ref, 0, 6) + prev_z(gathered(coarse_ref, 1, 6))
    vert = coarse_solve(target, modes, scale)
    vert_ref[...] = vert
    target_ref[...] = target
    scale_ref[...] = scale
    smooth_image(smooths_of(three_modes(vert_ref), layers_ref), smooth_ref, edge_ref)


def pack(sums):
    place = lane((8, 128)) // 16
    packed = jnp.zeros((8, 128), F32)
    for k, total in enumerate(sums):
        total = total[:, :128] + total[:, 128:]
        for by in (64, 32, 16):
            total = total + pltpu.roll(total, by, 1)
        packed = jnp.where(place == k, total, packed)
    return jnp.sum(packed, axis=0, keepdims=True)


def second_rough(
    image_ref, smooth_ref, layers_ref, table_ref, resid_ref, scaled_ref,
    scaled_change_ref, change_ref, sums_ref, planes_ref, column_ref, outer_ref, xy_ref, whole_ref,
):
    points, weight_x, _, _ = columns_of_nodes()
    inv_ends = column(1.0 / ENDS)
    whole_ref[...] = image_ref[...] + smooth_ref[...]
    over_diag(functools.partial(get, whole_ref), scaled_change_ref, layers_ref)
    operate(scaled_change_ref, xy_ref, change_ref, table_ref, layers_ref[0:1, :], weight_x)
    planes_ref[...] = jnp.concatenate(list(restrict(change_ref, points)) * 4, axis=0)
    sum_xy(change_ref)
    sums = [jnp.zeros((8, PLANE), F32)] * 6
    for ny in range(8):
        along = [jnp.zeros((8, PLANE), F32)] * 2
        for nz in range(8):
            rows = rows_of(nz, ny)
            share = float(1.0 / (ENDS[nz] * ENDS[ny]))
            scaled, change = get(scaled_ref, rows) * share, get(scaled_change_ref, rows)
            along = [total + float(STIFF[nz, node]) * change for total, node in zip(along, (0, 7))]
            change = change * share
            whole, image = get(whole_ref, rows), get(image_ref, rows)
            terms = [
                scaled * get(resid_ref, rows), scaled * whole, change * whole, scaled * image, change * image,
                change * (get(change_ref, rows) * float(ENDS[nz])),
            ]
            sums = [total + term for total, term in zip(sums, terms)]
        for k in range(2):
            column_ref[64 * k + 8 * ny : 64 * k + 8 * ny + 8, :] = along[k]
    sums_ref[...] = jnp.concatenate([total * inv_ends for total in sums], axis=0)
    for k, rows in enumerate((slice(0, 64), slice(448, 512))):
        outer_ref[64 * k : 64 * k + 64, :] = get(whole_ref, rows)


def first_rest(
    coarse_ref, image_ref, layers_ref, table_ref, resid_ref, scaled_ref,
    vert_ref, target_ref, scale_ref, coeff_ref, scaled_change_ref, change_ref, sums_ref, planes_ref, column_ref, outer_ref,
    smooth_ref, edge_ref, xy_ref, whole_ref,
):
    first_coarse(coarse_ref, layers_ref, vert_ref, target_ref, scale_ref, coeff_ref, smooth_ref, edge_ref)
    second_rough(
        image_ref, smooth_ref, layers_ref, table_ref, resid_ref, scaled_ref,
        scaled_change_ref, change_ref, sums_ref, planes_ref, column_ref, outer_ref, xy_ref, whole_ref,
    )


def second_faces(
    image_ref, scaled_change_ref, change_ref, outer_ref, far_in_ref, near_in_ref, layers_ref, table_ref,
    scaled_ref, lower_ref, sums_ref, planes_ref, column_ref,
    added_ref, far_ref, near_ref, payload_ref, edge_ref, xy_ref,
):
    points, weight_x, _, _ = columns_of_nodes()
    inv_ends = column(1.0 / ENDS)
    even = lax.rem(my_layer(), 2) == 0
    own = layers_ref[0:1, :]
    kappas = kappa_sums(*(layers_ref[k : k + 1, :] for k in range(3)))
    faces = below_above(face_in(near_in_ref), face_in(far_in_ref))
    tiles = [slice(8 * ny, 8 * ny + 8) for ny in range(8)]
    added = added_by(faces, kappas, columns_of_nodes())
    xy_ref[...] = product(table_ref[...], jnp.concatenate(added, axis=1))
    along, at_face = [], []
    for k in range(2):
        along.append(local_along(own, weight_x, added[k]))
        flux = own * xy_ref[:, PLANE * k : PLANE * k + PLANE]
        at_face.append(float(WEIGHTS[0]) * jnp.concatenate(
            [flux[t] + (float(REACT * WEIGHTS[ny]) * weight_x) * added[k][t] for ny, t in enumerate(tiles)], axis=0
        ))
    local = [
        (float(STIFF[nz, 0]) * along[0] + float(STIFF[nz, 7]) * along[1]) + at_face[k] for k, nz in enumerate((0, 7))
    ]
    flat = at_face[0] + at_face[1]
    slope = (along[1] + at_face[1]) - (along[0] + at_face[0])
    lower, upper = restrict_xy([flat[t] for t in tiles], [slope[t] for t in tiles], points)
    lower, upper = lower + planes_ref[0:1, :], upper + planes_ref[1:2, :]
    sums = [jnp.zeros((8, PLANE), F32)] * 5
    energy = jnp.zeros((8, PLANE), F32)
    planes = [slice(0, 64), slice(448, 512)]
    for k in range(2):
        s_plane, q_plane, i_plane, c_plane = (
            get(ref, planes[k]) for ref in (scaled_ref, scaled_change_ref, image_ref, change_ref)
        )
        w_plane = outer_ref[64 * k : 64 * k + 64, :]
        for ny in range(8):
            tile = tiles[ny]
            share = float(1.0 / ENDS[ny])
            half = share * float(1.0 / ENDS[0])
            face = faces[k][tile]
            s, q, dq = s_plane[tile] * half, q_plane[tile] * half, added[k][tile] * half
            sums[0] = sums[0] + s * face
            sums[1] = sums[1] + (q * face + dq * (w_plane[tile] + face))
            sums[2] = sums[2] + s * face
            sums[3] = sums[3] + (q * face + dq * (i_plane[tile] + face))
            sums[4] = sums[4] + (added[k][tile] * c_plane[tile]) * share
            energy = energy + (
                column_ref[64 * k + 8 * ny : 64 * k + 8 * ny + 8, :] * along[k][tile]
                + q_plane[tile] * at_face[k][tile]
                + added[k][tile] * local[k][tile]
            )
    sums = [sums_ref[8 * k + 8 : 8 * k + 16, :] + sums[k] * inv_ends for k in range(5)]
    sums = pack([sums_ref[0:8, :]] + sums[:4] + [sums[4] + energy])
    below, _ = below_above(row_after_face(near_in_ref), row_after_face(far_in_ref))
    send(payload_ref, halves(lower_ref[0:1, :] + below) + halves(lower) + halves(upper) + [sums])
    for k in range(2):
        put(edge_ref, slice(64 * k, 64 * k + 64), local[k])
        added_ref[64 * k : 64 * k + 64, :] = at_face[k]
    sum_xy(edge_ref)
    change = [(get(change_ref, planes[k]) + get(edge_ref, slice(64 * k, 64 * k + 64)))[0:56] for k in range(2)]
    put(far_ref, slice(0, 56), jnp.where(even, change[0], change[1]))
    put(near_ref, slice(0, 56), jnp.where(even, change[1], change[0]))


def local_along(own, weight_x, added):
    return own * jnp.concatenate(
        [(weight_x * float(WEIGHTS[ny])) * added[8 * ny : 8 * ny + 8] for ny in range(8)], axis=0
    )


def added_by(faces, kappas, columns):
    _, weight_x, diag_x, ends_x = columns
    return [
        jnp.concatenate(
            [
                face[8 * ny : 8 * ny + 8] / fine_diag(kappas, nz, ny, weight_x, diag_x, ends_x)
                for ny in range(8)
            ],
            axis=0,
        )
        for nz, face in zip((0, 7), faces)
    ]


def complete(
    first_ref, first_scaled_ref, first_change_ref, far_in_ref, near_in_ref, at_face_ref, layers_ref, coeff_ref, vert_ref,
    image_ref, scaled_change_ref, change_ref, choose_ref, applied_ref, modes_ref, edge_ref,
):
    columns = columns_of_nodes()
    applied_ref[...] = coarse_apply(vert_ref[...], coarse_modes(coeff_ref[...]))
    modes_ref[...] = three_modes(vert_ref)
    choose_ref[...] = selection(layers_ref[3:4, :]).astype(F32).T.astype(jnp.bfloat16)
    image_ref[...] = first_ref[...]
    scaled_change_ref[...] = first_scaled_ref[...]
    faces_in(image_ref, near_in_ref, far_in_ref)
    kappas = kappa_sums(*(layers_ref[k : k + 1, :] for k in range(3)))
    added = added_by(below_above(face_in(near_in_ref), face_in(far_in_ref)), kappas, columns)
    for k, rows in enumerate((slice(0, 64), slice(448, 512))):
        put(scaled_change_ref, rows, get(scaled_change_ref, rows) + added[k])
        put(edge_ref, slice(64 * k, 64 * k + 64), local_along(layers_ref[0:1, :], columns[1], added[k]))
        put(edge_ref, slice(128 + 64 * k, 192 + 64 * k), at_face_ref[64 * k : 64 * k + 64, :])
    sum_xy(edge_ref)
    along = [get(edge_ref, slice(64 * k, 64 * k + 64)) for k in range(2)]
    for nz in range(8):
        rows = slice(64 * nz, 64 * nz + 64)
        new = get(first_change_ref, rows) + (float(STIFF[nz, 0]) * along[0] + float(STIFF[nz, 7]) * along[1])
        if nz in (0, 7):
            new = new + get(edge_ref, slice(128 + 64 * (nz // 7), 192 + 64 * (nz // 7)))
        put(change_ref, rows, new)


def folded(value):
    return functools.reduce(lambda a, b: a + b, [value[k : k + 8] for k in range(0, value.shape[0], 8)])


def second_coarse(
    coeff_ref, step_ref, first_ref, applied_ref, target_ref, scale_ref, first_modes_ref, modes_ref, scalars_ref, vert_ref
):
    modes = coarse_modes(coeff_ref[...])
    target, first, applied = target_ref[...], first_ref[...], applied_ref[...]
    rough, rough_change = gathered(step_ref, 0, 7), gathered(step_ref, 1, 7) + prev_z(gathered(step_ref, 2, 7))
    parts = folded(gathered_rows(step_ref, 6, 7))
    sums = [parts] + [pltpu.roll(parts, 128 - 16 * k, 1) for k in range(1, 6)]
    used = lane(parts.shape) < 16

    def total(fine, coarse):
        coarse = folded(coarse)
        return jnp.sum(jnp.where(used, fine, 0.0) + (coarse[:, :128] + coarse[:, 128:]), keepdims=True)

    image = rough + applied
    change = coarse_solve(image, modes, scale_ref[...])
    vert_ref[...] = change
    change_modes = three_modes(vert_ref)
    change_applied = coarse_apply(change, modes)
    gamma = total(sums[0], target * first)
    energy = total(sums[3], first * (2.0 * rough + applied))
    alpha = gamma / energy
    vert = first - alpha * change
    progress = total(sums[0] - alpha * (2.0 * sums[1] - alpha * sums[2]), (target - alpha * image) * vert)
    second = total(
        sums[3] - alpha * (2.0 * sums[4] - alpha * sums[5]),
        vert * (2.0 * (rough - alpha * rough_change) + (applied - alpha * change_applied)),
    )
    cross = total(sums[1] - alpha * sums[2], vert * image)
    beta = progress / gamma
    alpha_next = progress / (second + beta * (2.0 * cross + beta * energy))
    scalars = [alpha + alpha_next * beta + alpha_next, alpha_next * alpha]
    modes_ref[...] = scalars[0] * first_modes_ref[...] - scalars[1] * change_modes
    scalars_ref[...] = jnp.concatenate([jnp.broadcast_to(t, (1, 128)) for t in scalars * 4], axis=0)


def to_stored(choose, value):
    return lax.dot_general(
        jnp.concatenate([choose] * 2, axis=1),
        jnp.concatenate(pieces(value)[1:], axis=1),
        (((1,), (1,)), ((), ())),
        preferred_element_type=F32,
    )


def closing(
    resid_ref, scaled_ref, image_ref, scaled_change_ref, change_ref, far_ref, near_ref, modes_ref, layers_ref, scalars_ref,
    choose_ref, solution_ref, residual_ref, grid_ref, sum_ref, edge_ref, held, sems,
):
    smooths = smooths_of(modes_ref[...], layers_ref)
    first, second = scalars_ref[0:1, 0:1], scalars_ref[1:2, 0:1]
    choose = choose_ref[...]
    for nz in range(8):
        for ny in range(8):
            rows = rows_of(nz, ny)
            rough = first * get(scaled_ref, rows) - second * get(scaled_change_ref, rows)
            grid_ref[rows, :] = rough + smooths[0].value(nz, ny)
    held[0] = to_stored(choose, grid_ref[...])
    smooth_image(smooths, sum_ref, edge_ref)
    first, second = first[None], second[None]
    sum_ref[...] = resid_ref[...] - first * image_ref[...] + second * change_ref[...] - sum_ref[...]
    for rows, ref in zip(face_rows(sum_ref), (near_ref, far_ref)):
        put(sum_ref, rows, get(sum_ref, rows) + second[0] * face_in(ref))
    copies = [pltpu.make_async_copy(held.at[0], solution_ref, sems.at[0])]
    copies[0].start()
    held[1] = to_stored(choose, get(sum_ref, slice(0, 512)))
    copies.append(pltpu.make_async_copy(held.at[1], residual_ref, sems.at[1]))
    copies[1].start()
    for copy in copies:
        copy.wait()


def call(kernel, outs, scratch=(), sems=0, cost=None, in_place=None, hbm_in=(), hbm_out=(), inputs=0):
    def specs(count, far):
        return [pl.BlockSpec(memory_space=pltpu.HBM if k in far else pltpu.VMEM) for k in range(count)]

    more = {"in_specs": specs(inputs, hbm_in)} if hbm_in else {}
    return pl.pallas_call(
        kernel,
        out_shape=[jax.ShapeDtypeStruct(*(s if isinstance(s[0], tuple) else (s, F32))) for s in outs],
        out_specs=specs(len(outs), hbm_out),
        scratch_shapes=[pltpu.VMEM(*(s if isinstance(s[0], tuple) else (s, F32))) for s in scratch]
        + ([pltpu.SemaphoreType.DMA((sems,))] if sems else []),
        compiler_params=pltpu.CompilerParams(vmem_limit_bytes=12 * 1024 * 1024),
        cost_estimate=cost,
        input_output_aliases=in_place or {},
        **more,
    )


def swapped(x, far):
    size = lax.axis_size(AXES)
    return lax.ppermute(x, AXES, [(i, (i + (1 if (i % 2 == 0) != far else -1)) % size) for i in range(size)])


def everyone(payload, shape):
    devices = lax.axis_size(AXES)
    return lax.all_to_all(payload.reshape((devices,) + shape), AXES, 0, 0, tiled=True).reshape(-1, 128)


def per_device(forcing, kappa, elem_order):
    devices = lax.axis_size(AXES)
    nodes, face, face_row = (2, 512, 128), (2, 56, 128), (2, 64, 128)
    plane, grid, flat = (8, PLANE), (devices, PLANE), (512, PLANE)
    edge, stored, choice = (2, 128, 128), (PLANE, 512), ((PLANE, PLANE), jnp.bfloat16)
    table = jnp.asarray(np.concatenate([STIFF_PARTS[k] for k in (0, 0, 1, 1, 0, 2)], 1), jnp.bfloat16)
    long = pl.CostEstimate(flops=10**11, bytes_accessed=2**28, transcendentals=0)
    payload_rows = (devices * 6, 128)
    load, far, near, own, payload = call(
        opening,
        [nodes, face_row, face_row, plane, payload_rows],
        [stored, (1, PLANE), ((1, PLANE), jnp.int32), payload_rows],
        7,
        hbm_in=(0, 1, 2),
        hbm_out=(4,),
        inputs=3,
    )(*(pltpu.with_memory_space_constraint(x, pltpu.HBM) for x in (forcing, kappa.reshape(1, PLANE), elem_order)))
    far, near = swapped(far, True), swapped(near, False)
    (payload,) = call(
        late_payload, [payload_rows], [payload_rows], 1, in_place={2: 0}, hbm_in=(2,), hbm_out=(0,), inputs=3
    )(load, own, payload)
    gather = everyone(payload, (3, 2, 128))
    resid, scaled, image, layers, lower, far, near = call(
        first_faces, [nodes, nodes, nodes, plane, plane, face_row, face_row], [flat], cost=long, in_place={0: 0}
    )(load, far, near, own, table)
    far, near = swapped(far, True), swapped(near, False)
    vert, target, scale, coeff, scaled_change, change, sums, planes, column_planes, outer = call(
        first_rest,
        [grid] * 4 + [nodes] * 2 + [(48, PLANE), plane, (128, PLANE), (128, PLANE)],
        [nodes, edge, flat, nodes],
    )(gather, image, layers, table, resid, scaled)
    added, next_far, next_near, payload = call(
        second_faces, [(128, PLANE), face, face, (devices * 7, 128)], [edge, (64, 2 * PLANE)]
    )(image, scaled_change, change, outer, far, near, layers, table, scaled, lower, sums, planes, column_planes)
    step = everyone(payload, (7, 1, 128))
    next_far, next_near = swapped(next_far, True), swapped(next_near, False)
    image, scaled_change, change, choose, applied, first_modes = call(
        complete, [nodes] * 3 + [choice, grid, (24, PLANE)], [(2, 256, 128)], in_place={0: 0, 1: 1, 2: 2}
    )(image, scaled_change, change, far, near, added, layers, coeff, vert)
    modes, scalars = call(second_coarse, [(24, PLANE), (8, 128)], [grid])(
        coeff, step, vert, applied, target, scale, first_modes
    )
    found, left = call(closing, [stored, stored], [flat, nodes, edge, (2,) + stored], 2, hbm_out=(0, 1))(
        resid, scaled, image, scaled_change, change, next_far, next_near, modes, layers, scalars, choose
    )
    return found, left


def solution(mesh):
    in_specs = (P(AXES, None), P(AXES), P(AXES, None))
    out_specs = (P(AXES, None), P(AXES, None))
    return jax.shard_map(
        per_device, mesh=mesh, in_specs=in_specs, out_specs=out_specs, check_vma=False
    )
```
